128 devices in a mesh: dp: 8 (over x, core), expert: 16 (over y, z).
Axes of the slice: x: 4, y: 4, z: 4, core: 2. Of those that a mesh axis runs over, the one named last changes fastest.
Arguments:
- tokens_in: bfloat16 [16, 2048, 1024], P('expert', 'dp'), may hold values from -6 to 6
- lengths: int32 [16], P('expert'), may hold values from 1793 to 2048, as said below
- routes: int32 [16, 2048, 8], P('expert', 'dp'), may hold values from 0 to 31, all different within a row
- w_query: float32 [1024, 1024], P(('dp', 'expert')), may hold values from -0.1875 to 0.1875
- w_key: float32 [1024, 512], P(('dp', 'expert')), may hold values from -0.1875 to 0.1875
- w_value: float32 [1024, 512], P(('dp', 'expert')), may hold values from -0.1875 to 0.1875
- w_output: float32 [1024, 1024], P(('dp', 'expert')), may hold values from -4 to 4
- w_router: float32 [1024, 32], P(('dp', 'expert')), may hold values from -0.09375 to 0.09375
- attn_gain: float32 [1024], P(('dp', 'expert')), may hold values from 0.25 to 1.75
- ffn_gain: float32 [1024], P(('dp', 'expert')), may hold values from 0.25 to 1.75
- query_gain: float32 [1024], P(('dp', 'expert')), may hold values from 0.25 to 1.75
- key_gain: float32 [512], P(('dp', 'expert')), may hold values from 0.25 to 1.75
- expert_in: bfloat16 [32, 1024, 1024], P('expert'), may hold values from -0.1875 to 0.1875
- expert_down: bfloat16 [32, 1024, 512], P('expert'), may hold values from -4 to 4
- out_grad: bfloat16 [16, 2048, 1024], P('expert', 'dp'), may hold values from -6 to 6
Outputs:
- output: bfloat16 [16, 2048, 1024], P('expert', 'dp')
- grad_tokens: bfloat16 [16, 2048, 1024], P('expert', 'dp')
- grad_w_query: float32 [1024, 1024], P(('dp', 'expert'))
- grad_w_key: float32 [1024, 512], P(('dp', 'expert'))
- grad_w_value: float32 [1024, 512], P(('dp', 'expert'))
- grad_w_output: float32 [1024, 1024], P(('dp', 'expert'))
- grad_w_router: float32 [1024, 32], P(('dp', 'expert'))
- grad_attn_gain: float32 [1024], P(('dp', 'expert'))
- grad_ffn_gain: float32 [1024], P(('dp', 'expert'))
- grad_query_gain: float32 [1024], P(('dp', 'expert'))
- grad_key_gain: float32 [512], P(('dp', 'expert'))
- grad_expert_in: float32 [32, 1024, 1024], P('expert', 'dp')
- grad_expert_down: float32 [32, 1024, 512], P('expert', 'dp')
The draws below stay inside these ranges and needn't reach their ends.
Inputs may be any that keep to these rules, and one draw needn't show every extreme that they name: `lengths`: each sequence's real tokens come first; at least one sequence has all 2048. `routes`: each token names 8 different experts.
All inputs are finite; a program needn't handle non-finite values.
Results may differ from the reference program's by a relative error of at most 0.028.
Values may be sent and summed in bfloat16 or wider, within the bound.
A program may use at most 320 MiB of HBM per device.

```python
import jax
import jax.numpy as jnp
from jax import lax

D = 1024
HEADS = 16
HEAD_DIM = 64
KV_HEADS = 8
FF = 512
TOP = 8
TOK_DEV = 256
EXPERTS = 32
SEQ_LEN = 2048
SEQS = 16
KV = 512
CAP = 80
N_DP = 8


def draw_lengths(key, part):
    key = jax.random.fold_in(key, 11)
    first_key, second_key = jax.random.split(key)
    lowest = SEQ_LEN - TOK_DEV + 1
    drawn = jax.random.randint(first_key, (SEQS,), lowest, SEQ_LEN + 1)
    picked = jax.random.randint(second_key, (), 0, SEQS)
    return jnp.where(jnp.arange(SEQS) == picked, SEQ_LEN, drawn).astype(jnp.int32)


def level_of(rng, shape, cuts, least, high):
    def one(dim, shards_of):
        draws = jax.random.uniform(jax.random.fold_in(jax.random.fold_in(rng, 6), dim), (shards_of,), jnp.float32, least / len(cuts), high / len(cuts))
        return jnp.repeat(jnp.exp(draws), shape[dim] // shards_of).reshape((-1,) + (1,) * (len(shape) - dim - 1))

    loudness = one(*cuts[0])
    for cut in cuts[1:]:
        loudness = loudness * one(*cut)
    return loudness


def choose_distinct(rng, rows, count, top, lift):
    order = jax.random.permutation(jax.random.fold_in(rng, 1), count)
    favour = order
    for power in range(3):
        favour = favour * favour // count
    favour = favour * lift // count
    tickets = jax.random.randint(jax.random.fold_in(rng, 2), (rows, count), 0, 4096) + favour
    sure = jax.random.permutation(jax.random.fold_in(rng, 3), rows)[jnp.arange(count) % rows]
    tickets = jnp.where(jnp.arange(rows)[:, None] == sure[None, :], 1 << 14, tickets)
    merit = tickets * count + jnp.arange(count)
    return lax.top_k(merit.astype(jnp.int32), top)[1].astype(jnp.int32)


def gaussian(key, dims, scale, most, shards=(), held_as=jnp.bfloat16):
    gain = level_of(key, dims, shards, -0.22, 0.18) if shards else 1.0
    entries = jax.random.normal(key, dims, jnp.float32) * scale * gain
    return jnp.minimum(jnp.maximum(entries, -most), most).astype(held_as)


def setup_inputs(seed: int = 0) -> dict:
    streams_of = jax.random.split(jax.random.key(seed), 16)
    return {
        "tokens_in": gaussian(streams_of[0], (SEQS, SEQ_LEN, D), 1.0, 6.0, ((0, 16), (1, 8))),
        "lengths": draw_lengths(jax.random.fold_in(streams_of[15], 71), 0),
        "routes": choose_distinct(streams_of[2], SEQS * SEQ_LEN, EXPERTS, TOP, 2048).reshape((SEQS, SEQ_LEN, TOP)),
        "w_query": gaussian(streams_of[3], (D, D), D ** -0.5, 0.1875, ((0, 128),), jnp.float32),
        "w_key": gaussian(streams_of[4], (D, KV), D ** -0.5, 0.1875, ((0, 128),), jnp.float32),
        "w_value": gaussian(streams_of[5], (D, KV), D ** -0.5, 0.1875, ((0, 128),), jnp.float32),
        "w_output": gaussian(streams_of[6], (D, D), (max(1, 4 * D // SEQ_LEN)) ** -0.5, 4.0, ((0, 128),), jnp.float32),
        "w_router": gaussian(streams_of[7], (D, EXPERTS), (4 * D) ** -0.5, 0.09375, ((0, 128),), jnp.float32),
        "attn_gain": jnp.clip(1.0 + 0.15 * jax.random.normal(streams_of[8], (D,), jnp.float32), 0.25, 1.75),
        "ffn_gain": jnp.clip(1.0 + 0.15 * jax.random.normal(streams_of[9], (D,), jnp.float32), 0.25, 1.75),
        "query_gain": jnp.clip(1.0 + 0.15 * jax.random.normal(streams_of[10], (D,), jnp.float32), 0.25, 1.75),
        "key_gain": jnp.clip(1.0 + 0.15 * jax.random.normal(streams_of[11], (KV,), jnp.float32), 0.25, 1.75),
        "expert_in": gaussian(streams_of[12], (EXPERTS, D, 2 * FF), D ** -0.5, 0.1875, ((0, 16),)),
        "expert_down": gaussian(streams_of[13], (EXPERTS, D, FF), (max(1, FF // 256)) ** -0.5, 4.0, ((0, 16),)),
        "out_grad": gaussian(streams_of[14], (SEQS, SEQ_LEN, D), 1.0, 6.0, ((0, 16), (1, 8))),
    }


@jax.custom_vjp
def low(v):
    return lax.optimization_barrier(v.astype(jnp.bfloat16)).astype(jnp.float32)

@jax.custom_vjp
def low_back(v):
    return v

def low_keep(v):
    return (low(v), None)

def low_pass(kept, grad):
    return (grad,)

def back_keep(v):
    return (v, None)

def back_low(kept, grad):
    return (low(grad),)
low.defvjp(low_keep, low_pass)
low_back.defvjp(back_keep, back_low)
norm_eps = 1e-06
rope_base = 10000.0
masked_score = -1e+30
highest = lax.Precision.HIGHEST

def rms_scale(values, weight):
    inverse = lax.rsqrt(lax.optimization_barrier(jnp.mean(values * values, axis=-1, keepdims=True)) + norm_eps)
    return values * inverse * weight

def rotary(values, places):
    row_count = values.shape[0]
    full_width = values.shape[1]
    head_half = HEAD_DIM // 2
    shaped = values.reshape(row_count, full_width // HEAD_DIM, HEAD_DIM)
    frequency = rope_base ** (-2.0 * jnp.arange(head_half).astype(jnp.float32) / HEAD_DIM)
    angles = places.astype(jnp.float32)[:, None] * frequency[None, :]
    cosine = jnp.cos(angles)[:, None, :]
    sine_part = jnp.sin(angles)[:, None, :]
    first_half = shaped[:, :, :head_half]
    second = shaped[:, :, head_half:]
    turned = jnp.concatenate([first_half * cosine - second * sine_part, second * cosine + first_half * sine_part], axis=-1)
    return turned.reshape(row_count, full_width)

def silu_of(values):
    return values / (1.0 + jnp.exp(-values))

def gated_hidden(projected):
    half_width = projected.shape[-1] // 2
    return silu_of(projected[..., :half_width]) * projected[..., half_width:]

def softmax_rows(logits):
    shifted = jnp.exp(logits - lax.optimization_barrier(jnp.max(logits, axis=-1, keepdims=True)))
    return shifted / lax.optimization_barrier(jnp.sum(shifted, axis=-1, keepdims=True))

def reference(tokens_in, lengths, routes, w_query, w_key, w_value, w_output, w_router, attn_gain, ffn_gain, query_gain, key_gain, expert_in, expert_down, out_grad):
    score_scale = HEAD_DIM ** (-0.5)
    group_size = HEADS // KV_HEADS
    block_rows = min(512, SEQ_LEN)
    block_count = SEQ_LEN // block_rows
    expert_ids = jnp.arange(EXPERTS).astype(jnp.int32)
    slot_ids = jnp.arange(CAP).astype(jnp.int32)
    places = jnp.arange(SEQ_LEN).astype(jnp.int32)

    def attend(query_rot, key_rot, value_rot, length):
        key_heads = key_rot.reshape(SEQ_LEN, KV_HEADS, HEAD_DIM)
        value_heads = value_rot.reshape(SEQ_LEN, KV_HEADS, HEAD_DIM)

        def attend_block(block_start):
            query_block = lax.dynamic_slice_in_dim(query_rot, block_start, block_rows, 0)
            query_block = query_block.reshape(block_rows, KV_HEADS, group_size, HEAD_DIM)
            scores = low_back(score_scale * jnp.einsum('qgrd,kgd->grqk', query_block, key_heads, precision=highest))
            query_place = block_start + jnp.arange(block_rows).astype(jnp.int32)
            allowed = (places[None, :] <= query_place[:, None]) & (places[None, :] < length)
            scores = jnp.where(allowed, scores, masked_score)
            soft_weights = low(softmax_rows(scores))
            attended = jnp.einsum('grqk,kgd->qgrd', soft_weights, value_heads, precision=highest)
            return attended.reshape(block_rows, HEADS * HEAD_DIM)
        starts = (jnp.arange(block_count) * block_rows).astype(jnp.int32)
        return lax.map(jax.checkpoint(attend_block), starts).reshape(SEQ_LEN, HEADS * HEAD_DIM)

    def whole_layer(token_vals, query_proj, key_proj, value_proj, output_proj, router_proj, gain_attn, gain_ffn, gain_query, gain_key, gate_up, down_proj):
        query_proj = low(query_proj)
        key_proj = low(key_proj)
        value_proj = low(value_proj)
        output_proj = low(output_proj)
        router_proj = low(router_proj)
        gain_attn = low(gain_attn)
        gain_ffn = low(gain_ffn)
        gain_query = low(gain_query)
        gain_key = low(gain_key)

        def moe_block(pieces):
            block_in, block_routes, block_valid = pieces
            logits = low_back(jnp.dot(block_in, router_proj, precision=highest))
            routing = softmax_rows(logits)
            chosen = lax.optimization_barrier(jnp.sum((block_routes[:, :, None] == expert_ids[None, None, :]).astype(jnp.int32), axis=1)) * block_valid[:, None]
            earlier = jnp.cumsum(chosen, axis=0) - chosen
            placed = ((chosen[:, :, None] == 1) & (earlier[:, :, None] == slot_ids[None, None, :])).astype(jnp.float32)
            dispatched = low_back(jnp.einsum('tec,td->ecd', placed, block_in, precision=highest))
            projected = low_back(jnp.einsum('ecd,edf->ecf', dispatched, gate_up, precision=highest))
            hidden = low(gated_hidden(projected))
            expert_out = low(low_back(jnp.einsum('ecf,edf->ecd', hidden, down_proj, precision=highest)))
            gate_vals = low(routing)
            return low_back(jnp.einsum('tec,ecd->td', placed * gate_vals[:, :, None], expert_out, precision=highest))

        def one_sequence(carried, pieces):
            seq_in, length, seq_routes = pieces
            normed = low(rms_scale(seq_in, gain_attn))
            query_raw = low_back(jnp.dot(normed, query_proj, precision=highest))
            key_raw = low_back(jnp.dot(normed, key_proj, precision=highest))
            value_rot = low(low_back(jnp.dot(normed, value_proj, precision=highest)))
            query_rot = low(rotary(rms_scale(query_raw, gain_query), places))
            key_rot = low(rotary(rms_scale(key_raw, gain_key), places))
            attended = low(low_back(attend(query_rot, key_rot, value_rot, length)))
            residual_mid = seq_in + low_back(jnp.dot(attended, output_proj, precision=highest))
            moe_in = low(rms_scale(residual_mid, gain_ffn))
            valid_rows = (places < length).astype(jnp.int32)
            mixture = lax.map(jax.checkpoint(moe_block), (moe_in.reshape(N_DP, TOK_DEV, D), seq_routes.reshape(N_DP, TOK_DEV, TOP), valid_rows.reshape(N_DP, TOK_DEV)))
            return (carried, residual_mid + mixture.reshape(SEQ_LEN, D))
        unused, result = lax.scan(jax.checkpoint(one_sequence), jnp.zeros((), jnp.float32), (token_vals, lengths, routes))
        return result
    result, pullback = jax.vjp(whole_layer, tokens_in.astype(jnp.float32), w_query, w_key, w_value, w_output, w_router, attn_gain, ffn_gain, query_gain, key_gain, expert_in.astype(jnp.float32), expert_down.astype(jnp.float32))
    gradients = pullback(out_grad.astype(jnp.float32))
    return (result.astype(jnp.bfloat16), gradients[0].astype(jnp.bfloat16), gradients[1], gradients[2], gradients[3], gradients[4], gradients[5], gradients[6], gradients[7], gradients[8], gradients[9], gradients[10], gradients[11])
```

```python
import functools

import jax
import jax.numpy as jnp
from jax import lax
from jax.experimental import pallas as pl
from jax.experimental.pallas import tpu as pltpu
from jax.sharding import PartitionSpec as P

HEADS = 16
HEAD_DIM = 64
KV_HEADS = 8
GROUP = HEADS // KV_HEADS
PAIR = GROUP * HEAD_DIM
PACK = PAIR + 2 * HEAD_DIM
EXTRA = 128

norm_eps = 1e-06
rope_base = 10000.0
masked_score = -1e30
score_scale = HEAD_DIM ** (-0.5)
low_type = jnp.bfloat16
full = jnp.float32

VMEM = pl.BlockSpec(memory_space=pltpu.VMEM)
SMEM = pl.BlockSpec(memory_space=pltpu.SMEM)
LIMIT = 56 * 1024 * 1024


def dot(left, right):
    return jnp.dot(left, right, preferred_element_type=full)


def dot_nt(left, right):
    return lax.dot_general(left, right, (((1,), (1,)), ((), ())), preferred_element_type=full)


def dot_tn(left, right):
    return lax.dot_general(left, right, (((0,), (0,)), ((), ())), preferred_element_type=full)


def partner(values):
    lane = lax.broadcasted_iota(jnp.int32, values.shape, 1)
    half = HEAD_DIM // 2
    return jnp.where(
        lane % HEAD_DIM < half, pltpu.roll(values, 128 - half, 1), pltpu.roll(values, half, 1)
    )


def flip(values):
    return values.astype(full).T


def cost(microseconds):
    return pl.CostEstimate(
        flops=int(microseconds * 1.15e9), bytes_accessed=1 << 20, transcendentals=0
    )


def params(microseconds):
    return dict(
        compiler_params=pltpu.CompilerParams(vmem_limit_bytes=LIMIT),
        cost_estimate=cost(microseconds),
    )


MESH = pl.DeviceIdType.MESH
ANY = pl.BlockSpec(memory_space=pl.ANY)


def comm_params(number):
    return pltpu.CompilerParams(
        collective_id=number, has_side_effects=True, vmem_limit_bytes=LIMIT
    )


def place_of():
    dp, expert = lax.axis_index("dp"), lax.axis_index("expert")
    return dp, expert, dict(x=dp // 2, core=dp % 2, y=expert // 4, z=expert % 4)


def peer_on(axis, step):
    dp, expert, _ = place_of()
    if axis == "core":
        return lax.bitwise_xor(dp, 1), expert
    if axis == "x":
        return lax.bitwise_xor(dp, 2 * step), expert
    if axis == "y":
        return dp, lax.bitwise_xor(expert, 4 * step)
    return dp, lax.bitwise_xor(expert, step)


def greet(peers):
    barrier = pltpu.get_barrier_semaphore()
    for device in peers:
        pl.semaphore_signal(barrier, inc=1, device_id=device, device_id_type=MESH)


def meet(peers):
    pl.semaphore_wait(pltpu.get_barrier_semaphore(), len(peers))


def dp_peers():
    dp, expert, _ = place_of()
    return [(lax.bitwise_xor(dp, k), expert) for k in range(1, 8)]


class Mover:
    def __init__(self, sems):
        self.sems, self.count = sems, 0

    def __call__(self, source, target):
        copy = pltpu.make_async_copy(source, target, self.sems.at[self.count])
        self.count += 1
        copy.start()
        return copy


class Sender:
    def __init__(self, send_sem, recv_sem):
        self.send_sem, self.recv_sem, self.count = send_sem, recv_sem, 0

    def __call__(self, source, target, device):
        copy = pltpu.make_async_remote_copy(
            src_ref=source,
            dst_ref=target,
            send_sem=self.send_sem.at[self.count],
            recv_sem=self.recv_sem.at[self.count],
            device_id=device,
            device_id_type=MESH,
        )
        self.count += 1
        copy.start()
        return copy


AXES = ("x", "y", "z")
CUBE = [("core", 1)] + [(axis, k) for axis in AXES for k in (1, 2, 3)]


def placed_rows(slot_row, slots):
    rows = slot_row.shape[1]
    slot = lax.broadcasted_iota(jnp.int32, (slots, rows), 0).astype(full)
    return jnp.where(slot == slot_row, 1.0, 0.0).astype(low_type)


def placed_of(table, slots):
    return jnp.concatenate(
        [placed_rows(table[e : e + 1], slots) for e in range(table.shape[0])], axis=0
    )


def gather_kernel(
    cut, query_ref, key_ref, value_ref, router_ref, gains_ref, slot_ref, grad_ref, output_ref, out_ref, third_ref, rows_ref, shard_ref, shards_ref, mine_ref, others_ref, ours_ref, rows_buf, send_sem, recv_sem, local_sem
):
    _, _, at = place_of()
    x, y, z, c = at["x"], at["y"], at["z"], at["core"]
    columns = shard_ref.shape[1]
    sides = (pl.ds(0, cut), pl.ds(cut, columns - cut))
    peers = [peer_on(axis, k) for axis, k in CUBE]
    greet(peers)
    rows = shard_ref.shape[0]
    for g in range(KV_HEADS):
        here = g * PACK
        shard_ref[:, here : here + PAIR] = query_ref[:, g * PAIR : (g + 1) * PAIR]
        head = slice(g * HEAD_DIM, (g + 1) * HEAD_DIM)
        shard_ref[:, here + PAIR : here + PACK] = jnp.concatenate(
            [key_ref[:, head], value_ref[:, head]], axis=1
        )
    experts = router_ref.shape[1]
    lane = lax.broadcasted_iota(jnp.int32, (rows, EXTRA), 1)
    row = lax.broadcasted_iota(jnp.int32, (rows, EXTRA), 0)
    gains = jnp.broadcast_to(gains_ref[...], (rows, EXTRA))
    extra = jnp.concatenate(
        [router_ref[...], jnp.zeros((rows, EXTRA - experts), full)], axis=1
    )
    for n in range(4):
        column = jnp.sum(jnp.where(lane == row + n * rows, gains, 0.0), axis=1, keepdims=True)
        extra += jnp.where(lane == experts + n, column, 0.0)
    shard_ref[:, KV_HEADS * PACK :] = extra
    meet(peers)
    send = Sender(send_sem, recv_sem)
    first = [send(shard_ref, shards_ref.at[z], peer_on("z", k)) for k in (1, 2, 3)]
    first += [send(output_ref, others_ref.at[x], peer_on("x", k)) for k in (1, 2, 3)]
    shards_ref[z] = shard_ref[...]
    others_ref[x] = output_ref[...]
    move = Mover(local_sem)
    owners, parts, slots, _ = rows_buf.shape
    stores = []

    def slot_job(n):
        for o in range(n * 4, n * 4 + 4):
            for j in range(parts):
                e = o * parts + j
                placed = placed_rows(slot_ref[e : e + 1, :], slots)
                rows_buf[o, j] = dot(placed, grad_ref[...]).astype(low_type)
        piece = pl.ds(n * 4, 4)
        stores.append(move(rows_buf.at[piece], rows_ref.at[piece]))

    slot_job(0)
    for copy in first:
        copy.wait()
    mine_ref[...] = shards_ref[...].reshape(mine_ref.shape).astype(low_type)
    ours_ref[...] = others_ref[...].reshape(ours_ref.shape).astype(low_type)
    local = move(mine_ref, out_ref.at[x, c, y])
    local_third = move(ours_ref, third_ref.at[z, c, y])
    second = []
    for k in (1, 2, 3):
        for side, axis in ((0, "y"), (1, "x")):
            second.append(
                send(
                    mine_ref.at[:, sides[side]],
                    out_ref.at[x, c, y, :, sides[side]],
                    peer_on(axis, k),
                )
            )
        second.append(send(ours_ref, third_ref.at[z, c, y], peer_on("y", k)))
    local.wait()
    local_third.wait()
    slot_job(1)
    for copy in second:
        copy.wait()
    third = []
    for k in (1, 2, 3):
        piece = out_ref.at[x, c, :, :, sides[0]]
        third.append(send(piece, piece, peer_on("x", k)))
        piece = out_ref.at[:, c, y, :, sides[1]]
        third.append(send(piece, piece, peer_on("y", k)))
        piece = third_ref.at[z, c]
        third.append(send(piece, piece, peer_on("z", k)))
    other = peer_on("core", 1)
    last = []
    for piece in (
        out_ref.at[x, c, :, :, sides[0]], out_ref.at[:, c, y, :, sides[1]], third_ref.at[z, c]
    ):
        last.append(send(piece, piece, other))
    slot_job(2)
    slot_job(3)
    for n, k in enumerate((1, 2, 3)):
        third[3 * n].wait_recv()
        piece = out_ref.at[lax.bitwise_xor(x, k), c, :, :, sides[0]]
        last.append(send(piece, piece, other))
        third[3 * n + 1].wait_recv()
        piece = out_ref.at[:, c, lax.bitwise_xor(y, k), :, sides[1]]
        last.append(send(piece, piece, other))
        third[3 * n + 2].wait_recv()
        piece = third_ref.at[lax.bitwise_xor(z, k), c]
        last.append(send(piece, piece, other))
    for copy in third:
        copy.wait_send()
    for copy in last:
        copy.wait()
    for copy in stores:
        copy.wait()


def gather_dense(query, key, value, router, gains, slot_of, grad, output, parts, slots, number):
    rows = query.shape[0]
    columns = KV_HEADS * PACK + EXTRA
    cut = columns // 256 * 128
    held = (slot_of.shape[0] // parts, parts, slots, grad.shape[1])
    out, third, grad_rows = pl.pallas_call(
        functools.partial(gather_kernel, cut),
        out_shape=(
            jax.ShapeDtypeStruct((4, 2, 4, 4 * rows, columns), low_type),
            jax.ShapeDtypeStruct((4, 2, 4, 4 * rows, output.shape[1]), low_type),
            jax.ShapeDtypeStruct(held, low_type),
        ),
        in_specs=[VMEM] * 8,
        out_specs=(ANY, ANY, ANY),
        scratch_shapes=[
            pltpu.VMEM((rows, columns), full),
            pltpu.VMEM((4, rows, columns), full),
            pltpu.VMEM((4 * rows, columns), low_type),
            pltpu.VMEM((4,) + output.shape, full),
            pltpu.VMEM((4 * rows, output.shape[1]), low_type),
            pltpu.VMEM(held, low_type),
            pltpu.SemaphoreType.DMA((36,)),
            pltpu.SemaphoreType.DMA((36,)),
            pltpu.SemaphoreType.DMA((6,)),
        ],
        compiler_params=comm_params(number),
        cost_estimate=cost(34),
        name="gather_dense",
    )(query, key, value, router, gains, slot_of, grad, output)
    return out.reshape(128 * rows, columns), third, grad_rows


def reduce_kernel(
    in0, in1, in2, out0, out1, out2, core0, core1, core2, half0, half1, half2, row0, row1, row2, *rest
):
    (send0, send1, send2, sum0, sum1, sum2, tail0, tail1, tail2, send_sem, recv_sem) = rest
    parts = (
        (in0, out0, core0, half0, row0, send0, sum0, tail0, ("x", "y", "z")),
        (in1, out1, core1, half1, row1, send1, sum1, tail1, ("y", "z", "x")),
        (in2, out2, core2, half2, row2, send2, sum2, tail2, ("z", "x", "y")),
    )
    _, _, at = place_of()
    c = at["core"]
    other = 1 - c
    peers = [peer_on(axis, k) for axis, k in CUBE]
    greet(peers)
    meet(peers)
    send = Sender(send_sem, recv_sem)

    def seat(axis, k):
        return lax.bitwise_xor(at[axis], k)

    first, second, third, fourth = {}, {}, {}, {}
    for k in (1, 2, 3, 0):
        for n, (given, _, core, _, _, _, _, _, axes) in enumerate(parts):
            a = seat(axes[0], k)
            first[n, k] = send(given.at[a, other], core.at[a], peer_on("core", 1))
    for k in (1, 2, 3):
        for n, (given, _, core, half, _, out_buf, _, _, axes) in enumerate(parts):
            a = seat(axes[0], k)
            first[n, k].wait_recv()
            out_buf[k - 1] = (given[a, c].astype(full) + core[a].astype(full)).astype(low_type)
            second[n, k] = send(out_buf.at[k - 1], half.at[k - 1], peer_on(axes[0], k))
    for n, (given, _, core, half, row, out_buf, total, _, axes) in enumerate(parts):
        a = seat(axes[0], 0)
        first[n, 0].wait_recv()
        for k in (1, 2, 3):
            second[n, k].wait()
        for k in (1, 2, 3, 0):
            b = seat(axes[1], k)
            value = given[a, c, b].astype(full) + core[a, b].astype(full)
            for m in range(3):
                value += half[m, b].astype(full)
            if k:
                out_buf[k - 1, 0] = value.astype(low_type)
                third[n, k] = send(out_buf.at[k - 1, 0], row.at[k - 1], peer_on(axes[1], k))
            else:
                total[...] = value.reshape(total.shape)
    for n, (_, _, _, _, row, _, total, tail, axes) in enumerate(parts):
        for k in (1, 2, 3):
            third[n, k].wait()
        value = total[...].reshape(row.shape[1:])
        for m in range(3):
            value += row[m].astype(full)
        total[...] = value.reshape(total.shape)
        for k in (1, 2, 3):
            d = seat(axes[2], k)
            fourth[n, k] = send(total.at[d], tail.at[k - 1], peer_on(axes[2], k))
    for n, (_, out, _, _, _, _, total, tail, axes) in enumerate(parts):
        for k in (1, 2, 3):
            fourth[n, k].wait()
        out[...] = total[at[axes[2]]] + tail[0] + tail[1] + tail[2]
    for copy in first.values():
        copy.wait_send()


def reduce_dense(pieces, number):
    widths = [p.shape[1] for p in pieces]
    pieces = [p.reshape(4, 2, 4, 32, p.shape[1]) for p in pieces]

    def each(*shape, kind=low_type):
        return [pltpu.VMEM(shape + (w,), kind) for w in widths]

    return pl.pallas_call(
        reduce_kernel,
        out_shape=[jax.ShapeDtypeStruct((8, w), full) for w in widths],
        in_specs=[VMEM] * 3,
        out_specs=[VMEM] * 3,
        scratch_shapes=[
            *each(4, 4, 32),
            *each(3, 4, 32),
            *each(3, 32),
            *each(3, 4, 32),
            *each(4, 8, kind=full),
            *each(3, 8, kind=full),
            pltpu.SemaphoreType.DMA((39,)),
            pltpu.SemaphoreType.DMA((39,)),
        ],
        compiler_params=comm_params(number),
        cost_estimate=cost(38),
        name="reduce_dense",
    )(*pieces)


PLANE = [(axis, k) for axis in ("y", "z") for k in (1, 2, 3)]


def dispatch_kernel(
    att_ref, output_ref, tokens_ref, gains_ref, left_ref, right_ref, mid_ref, moe_ref, out_ref, held_a, held_b, rows_a, rows_b, send_sem, recv_sem, local_sem
):
    _, _, at = place_of()
    y, z = at["y"], at["z"]
    peers = [peer_on(axis, k) for axis, k in PLANE]
    greet(peers)
    attended = jnp.concatenate([att_ref[g] for g in range(KV_HEADS)], axis=1)
    mid = tokens_ref[...].astype(full) + dot(attended, output_ref[...])
    mid_ref[...] = mid
    inverse = lax.rsqrt(jnp.mean(mid * mid, axis=-1, keepdims=True) + norm_eps)
    moe_ref[...] = (mid * inverse * gains_ref[1:2, :]).astype(low_type)
    half = moe_ref.shape[1] // 2
    slots = rows_a.shape[3]
    sides = (pl.ds(0, half), pl.ds(half, half))
    meet(peers)
    send = Sender(send_sem, recv_sem)
    first = {}
    for k in (1, 2, 3):
        first[0, k] = send(moe_ref.at[:, sides[0]], held_a.at[k], peer_on("y", k))
        first[1, k] = send(moe_ref.at[:, sides[1]], held_b.at[k], peer_on("z", k))
    move = Mover(local_sem)
    copies = []
    for k in range(4):
        for side, (held, rows, table, seat) in enumerate(
            ((held_a, rows_a, left_ref, y), (held_b, rows_b, right_ref, z))
        ):
            source = lax.bitwise_xor(seat, k)
            placed = placed_of(table[source], slots)
            if k:
                first[side, k].wait_recv()
                tokens = held[k]
            else:
                tokens = moe_ref[:, side * half : (side + 1) * half]
            rows[k] = dot(placed, tokens).astype(low_type).reshape(rows.shape[1:])
            target = (
                out_ref.at[source, z, :, :, sides[0]]
                if side == 0
                else out_ref.at[y, source, :, :, sides[1]]
            )
            across, mine = ("z", z) if side == 0 else ("y", y)
            for n in (1, 2, 3):
                piece = rows.at[k, lax.bitwise_xor(mine, n)]
                copies.append(send(piece, target, peer_on(across, n)))
            copies.append(move(rows.at[k, mine], target))
    for copy in first.values():
        copy.wait_send()
    for copy in copies:
        copy.wait()


def dispatch(att, output_proj, tokens, gains, left, right, parts, slots, number):
    rows, wide = tokens.shape
    half = wide // 2
    return pl.pallas_call(
        dispatch_kernel,
        out_shape=(
            jax.ShapeDtypeStruct((rows, wide), full),
            jax.ShapeDtypeStruct((rows, wide), low_type),
            jax.ShapeDtypeStruct((4, 4, parts, slots, wide), low_type),
        ),
        in_specs=[VMEM] * 6,
        out_specs=(VMEM, VMEM, ANY),
        scratch_shapes=[
            pltpu.VMEM((4, rows, half), low_type),
            pltpu.VMEM((4, rows, half), low_type),
            pltpu.VMEM((4, 4, parts, slots, half), low_type),
            pltpu.VMEM((4, 4, parts, slots, half), low_type),
            pltpu.SemaphoreType.DMA((30,)),
            pltpu.SemaphoreType.DMA((30,)),
            pltpu.SemaphoreType.DMA((8,)),
        ],
        compiler_params=comm_params(number),
        cost_estimate=cost(50),
        name="dispatch",
    )(att, output_proj, tokens, gains, left, right)


def collect_kernel(sizes, *refs):
    experts, slots = sizes
    (back_ref, left_ref, right_ref, slot_ref, gains_ref, *given) = refs[:17]
    (in_out, down_out, router_out, normed_out, att_out, combine_out, mid_grad_ref, low_ref, ffn_ref, home_ref) = refs[17:27]
    held_a, held_b, going_a, going_b, came_a, came_b = refs[27:33]
    here = refs[33:45]
    in_buf, down_buf, normed_buf, att_buf, combine_buf, grad_buf = refs[45:51]
    in_core, down_core, in_going, down_going, in_came, down_came = refs[51:57]
    send_sem, recv_sem, local_sem = refs[57:]
    dp, _, at = place_of()
    x, y, z, c = at["x"], at["y"], at["z"], at["core"]
    rows, wide = mid_grad_ref.shape
    half = wide // 2
    sides = (pl.ds(0, half), pl.ds(half, half))
    peers = [peer_on(axis, k) for axis, k in PLANE] + dp_peers()
    greet(peers)
    meet(peers)
    send, move = Sender(send_sem, recv_sem), Mover(local_sem)
    order = (1, 2, 3, 0)
    first, locals_ = {}, {}
    for k in order:
        to_y, to_z = lax.bitwise_xor(y, k), lax.bitwise_xor(z, k)
        for n in (1, 2, 3):
            piece = back_ref.at[to_y, lax.bitwise_xor(z, n), :, :, sides[0]]
            first[0, k, n] = send(piece, held_a.at[k, n], peer_on("z", n))
            piece = back_ref.at[lax.bitwise_xor(y, n), to_z, :, :, sides[1]]
            first[1, k, n] = send(piece, held_b.at[k, n], peer_on("y", n))
        locals_[0, k] = move(back_ref.at[to_y, z, :, :, sides[0]], held_a.at[k, 0])
        locals_[1, k] = move(back_ref.at[y, to_z, :, :, sides[1]], held_b.at[k, 0])
    x_buf, p_buf, s_buf, h_buf, l_buf, moe_buf, normed_in, att_in, router_buf, mid_buf, grad_in, output_buf = here
    x_ref, p_ref, s_ref, h_ref, l_ref, moe_ref, normed_ref, att_ref, weights_ref, mid_ref, grad_ref, output_ref = given
    parts = in_buf.shape[0]
    loads = {}
    for j in range(parts):
        loads["x", j] = move(x_ref.at[:, j], x_buf.at[j])
        for name, source, target in (
            ("p", p_ref, p_buf), ("s", s_ref, s_buf), ("h", h_ref, h_buf), ("l", l_ref, l_buf)
        ):
            loads[name, j] = move(source.at[j], target.at[j])
    for name, source, target in (
        ("moe", moe_ref, moe_buf), ("normed", normed_ref, normed_in), ("att", att_ref, att_in), ("mid", mid_ref, mid_buf),
        ("grad", grad_ref, grad_in), ("output", output_ref, output_buf)
    ):
        loads[name] = move(source, target)
    loads["router"] = move(weights_ref.at[:, pl.ds(KV_HEADS * PACK, EXTRA)], router_buf)
    stores = []

    def x_of(j, n):
        piece = x_buf[j, :, :, n * 256 : (n + 1) * 256]
        return piece.reshape(piece.shape[0] * piece.shape[1], 256)

    def in_job(j):
        loads["x", j].wait()
        loads["p", j].wait()

        for n in range(wide // 256):
            value = dot_tn(x_of(j, n), p_buf[j]).astype(low_type)
            in_buf[j, n, 0] = value[:128]
            in_buf[j, n, 1] = value[128:]
        core_copies["in", j] = send(in_buf.at[j, :, 1 - c], in_core.at[j], peer_on("core", 1))

    def down_job(j):
        for name in "shl":
            loads[name, j].wait()
        for n in range(wide // 256):
            cols = slice(n * 256, (n + 1) * 256)
            value = dot_tn(s_buf[j, :, cols], h_buf[j]).astype(low_type)
            down_buf[j, n, 0] = value[:128]
            down_buf[j, n, 1] = value[128:]
            part = dot_tn(x_of(j, n), l_buf[j])
            router_out[cols, :] = part if j == 0 else router_out[cols, :] + part
        core_copies["down", j] = send(
            down_buf.at[j, :, 1 - c], down_core.at[j], peer_on("core", 1)
        )

    core_copies, x_copies = {}, {}
    buffers = {
        "in": (in_buf, in_core, in_going, in_came, in_out),
        "down": (down_buf, down_core, down_going, down_came, down_out),
    }

    def across_job(name, j):
        own, core, going, came, _ = buffers[name]
        core_copies[name, j].wait_recv()
        for k in (1, 2, 3):
            there = lax.bitwise_xor(x, k)
            value = own[j, there, c].astype(full) + core[j, there].astype(full)
            going[j, k - 1] = value.astype(low_type)
            x_copies[name, j, k] = send(
                going.at[j, k - 1], came.at[j, k - 1], peer_on("x", k)
            )

    def total_job(name, j):
        own, core, _, came, out = buffers[name]
        value = own[j, x, c].astype(full) + core[j, x].astype(full)
        for k in (1, 2, 3):
            x_copies[name, j, k].wait_recv()
            value += came[j, k - 1].astype(full)
        out[j] = value

    def by_place(values, axes):
        strides = dict(x=32, core=16, y=4, z=1)
        counts = dict(x=4, core=2, y=4, z=4)
        places = [0]
        for axis in axes:
            places = [p + n * strides[axis] for p in places for n in range(counts[axis])]
        return jnp.concatenate([values[p * 8 : p * 8 + 8] for p in places], axis=0)

    def order_job():
        loads["normed"].wait()
        values = flip(normed_in[...])
        normed_buf[0] = values.astype(low_type)
        normed_buf[1] = by_place(values, ("y", "core", "z", "x")).astype(low_type)
        stores.append(move(normed_buf, normed_out))
        loads["att"].wait()
        attended = jnp.concatenate([att_in[g] for g in range(KV_HEADS)], axis=1)
        att_buf[...] = by_place(flip(attended), ("z", "core", "x", "y")).astype(low_type)
        stores.append(move(att_buf, att_out))

    def combine_job():
        loads["moe"].wait()
        loads["router"].wait()
        logits = dot(moe_buf[...], router_buf[...])
        lane = lax.broadcasted_iota(jnp.int32, logits.shape, 1)
        logits = jnp.where(lane < experts, logits, masked_score)
        shifted = jnp.exp(logits - jnp.max(logits, axis=-1, keepdims=True))
        routing = shifted / jnp.sum(shifted, axis=-1, keepdims=True)
        gates = flip(routing.astype(low_type))
        for e in range(experts):
            slot = lax.broadcasted_iota(jnp.int32, (slots, rows), 0).astype(full)
            combine_buf[e] = jnp.where(
                slot == slot_ref[e : e + 1, :], gates[e : e + 1, :], 0.0
            ).astype(low_type)
        stores.append(move(combine_buf, combine_out))

    second, kept = {}, {}

    def add_job(k):
        for side, (held, table, going, came, seat, mine, axis) in enumerate(
            (
                (held_a, left_ref, going_a, came_a, y, z, "y"),
                (held_b, right_ref, going_b, came_b, z, y, "z"),
            )
        ):
            source = lax.bitwise_xor(seat, k)
            total = jnp.zeros((rows, half), full)
            for n in (1, 2, 3):
                first[side, k, n].wait_recv()
            locals_[side, k].wait()
            for n in range(4):
                owner = lax.bitwise_xor(mine, n)
                placed = placed_of(table[source, owner], slots)
                total += dot_tn(placed, held[k, n].reshape(parts * slots, half))
            if k:
                going[k - 1] = total.astype(low_type)
                second[side, k] = send(going.at[k - 1], came.at[k - 1], peer_on(axis, k))
            else:
                kept[side] = total

    in_job(0)
    add_job(1)
    in_job(1)
    across_job("in", 0)
    add_job(2)
    down_job(0)
    across_job("in", 1)
    add_job(3)
    down_job(1)
    across_job("down", 0)
    add_job(0)
    order_job()
    across_job("down", 1)
    combine_job()
    sums = []
    for side, came in ((0, came_a), (1, came_b)):
        for k in (1, 2, 3):
            second[side, k].wait_recv()
        sums.append(
            kept[side] + came[0].astype(full) + came[1].astype(full) + came[2].astype(full)
        )
    moe_grad = jnp.concatenate(sums, axis=1)
    for name in ("mid", "grad", "output"):
        loads[name].wait()
    mid = mid_buf[...]
    inverse = lax.rsqrt(jnp.mean(mid * mid, axis=-1, keepdims=True) + norm_eps)
    scaled = moe_grad * gains_ref[1:2, :]
    shared = jnp.sum(scaled * mid, axis=-1, keepdims=True) * (inverse * inverse * inverse / wide)
    mid_grad = grad_in[...].astype(full) + (scaled * inverse - mid * shared)
    mid_grad_ref[...] = mid_grad
    low = mid_grad.astype(low_type)
    low_ref[...] = low
    ffn_ref[...] = jnp.sum(mid * inverse * moe_grad, axis=0, keepdims=True)
    third = []
    for k in (1, 2, 3, 4, 5, 6, 7, 0):
        g = lax.bitwise_xor(dp, k)
        piece = dot_nt(low, output_buf[pl.ds(pl.multiple_of(g * PAIR, PAIR), PAIR), :])
        piece = piece.astype(low_type)
        if k:
            grad_buf[g] = piece
            third.append(send(grad_buf.at[g], home_ref.at[dp], peers[5 + k]))
        else:
            home_ref[dp] = piece
    for j in range(parts):
        total_job("in", j)
        total_job("down", j)
    for copies in (first, second, core_copies, x_copies):
        for copy in copies.values():
            copy.wait_send()
    for copy in third:
        copy.wait()
    for copy in stores:
        copy.wait()


def collect(back, left, right, slot_of, gains, given, sizes, number):
    owners, parts, slots, wide = back.shape
    half = wide // 2
    rows = slot_of.shape[1]
    x, p, s, h, l, moe, normed, att, weights, mid, grad, output_proj = given
    split = lambda table: table.reshape(4, 4, parts, rows)

    def like(values, *shape):
        return pltpu.VMEM(shape or values.shape, values.dtype)

    outs = [
        jax.ShapeDtypeStruct((parts, wide // 8, p.shape[2]), full),
        jax.ShapeDtypeStruct((parts, wide // 8, h.shape[2]), full),
        jax.ShapeDtypeStruct((wide, EXTRA), full),
        jax.ShapeDtypeStruct((2, wide, rows), low_type),
        jax.ShapeDtypeStruct((wide, rows), low_type),
        jax.ShapeDtypeStruct((slot_of.shape[0], slots, rows), low_type),
        jax.ShapeDtypeStruct((rows, wide), full),
        jax.ShapeDtypeStruct((rows, wide), low_type),
        jax.ShapeDtypeStruct((1, wide), full),
        jax.ShapeDtypeStruct((KV_HEADS, rows, PAIR), low_type),
    ]
    return pl.pallas_call(
        functools.partial(collect_kernel, sizes),
        out_shape=outs,
        in_specs=[ANY, VMEM, VMEM, VMEM, VMEM] + [ANY] * 12,
        out_specs=[VMEM, VMEM, VMEM, ANY, ANY, ANY, VMEM, VMEM, VMEM, VMEM],
        scratch_shapes=[
            pltpu.VMEM((4, 4, parts, slots, half), low_type),
            pltpu.VMEM((4, 4, parts, slots, half), low_type),
            pltpu.VMEM((3, rows, half), low_type),
            pltpu.VMEM((3, rows, half), low_type),
            pltpu.VMEM((3, rows, half), low_type),
            pltpu.VMEM((3, rows, half), low_type),
            like(x, parts, owners, slots, wide),
            like(p), like(s), like(h), like(l), like(moe), like(normed), like(att),
            like(weights, wide, EXTRA),
            like(mid), like(grad), like(output_proj),
            pltpu.VMEM((parts, 4, 2, wide // 8, p.shape[2]), low_type),
            pltpu.VMEM((parts, 4, 2, wide // 8, h.shape[2]), low_type),
            *[pltpu.VMEM(o.shape, o.dtype) for o in (outs[3], outs[4], outs[5], outs[9])],
            *[
                pltpu.VMEM((parts, n, wide // 8, w.shape[2]), low_type)
                for n in (4, 3, 3)
                for w in (p, h)
            ],
            pltpu.SemaphoreType.DMA((37 + 8 * parts,)),
            pltpu.SemaphoreType.DMA((37 + 8 * parts,)),
            pltpu.SemaphoreType.DMA((8 + 5 * parts + 7 + 3,)),
        ],
        compiler_params=comm_params(number),
        cost_estimate=cost(55),
        name="collect",
    )(back.reshape(4, 4, parts, slots, wide), split(left), split(right), slot_of, gains, *given)


def allowed_of(shape, rows, length, i):
    key_at = lax.broadcasted_iota(jnp.int32, shape, 0)
    query_at = lax.broadcasted_iota(jnp.int32, shape, 1) % rows
    return (key_at <= query_at) & (key_at < length - i * rows)


def key_spread(width, wide):
    out = lax.broadcasted_iota(jnp.int32, (wide, width), 0)
    here = lax.broadcasted_iota(jnp.int32, (wide, width), 1)
    return jnp.where(out == (here // 4) * 8 + here % 4, 1.0, 0.0).astype(low_type)


def hand_over(sent, home, send_sem, recv_sem, i):
    dp, expert, _ = place_of()
    k = lax.bitwise_xor(dp, i)
    return pltpu.make_async_remote_copy(
        src_ref=sent.at[i],
        dst_ref=home.at[dp],
        send_sem=send_sem.at[k],
        recv_sem=recv_sem.at[k],
        device_id=(i, expert),
        device_id_type=MESH,
    )


def forward_kernel(
    length_ref, tokens_ref, weights_ref, cos_ref, sin_ref, slot_a, slot_b, third_ref,
    output_ref, normed_ref, raw_ref, pack_ref, gains_ref, held_ref, att_ref, log_ref, home_ref, got_a, got_b,
    sent, flip_ref, third_buf, send_one, recv_one, send_two, recv_two, send_sem, recv_sem, local_sem,
):
    dp, _, at = place_of()
    y, z = at["y"], at["z"]
    peers = dp_peers() + [peer_on(axis, k) for axis, k in PLANE]
    greet(peers)
    third = pltpu.make_async_copy(third_ref, third_buf, local_sem)
    third.start()
    blocks, rows = held_ref.shape[0], held_ref.shape[1]
    wide = tokens_ref.shape[1]
    width = KV_HEADS * HEAD_DIM
    extra = flip(weights_ref[:, KV_HEADS * PACK :])
    gains_ref[0:1, :] = extra[32:33]
    gains_ref[1:2, :] = extra[34:35]
    key_gain = dot(
        jnp.broadcast_to(extra[35:36], (8, wide)).astype(low_type), key_spread(width, wide)
    )[:1]
    for g in range(KV_HEADS):
        pack_ref[g, :, :PAIR] = extra[33:34, g * PAIR : (g + 1) * PAIR]
        pack_ref[g, :, PAIR:] = jnp.concatenate(
            [key_gain[:, g * HEAD_DIM : (g + 1) * HEAD_DIM], jnp.ones((1, HEAD_DIM), full)],
            axis=1,
        )
    values = tokens_ref[...].astype(full)
    inverse = lax.rsqrt(jnp.mean(values * values, axis=-1, keepdims=True) + norm_eps)
    normed = (values * inverse * gains_ref[0:1, :]).astype(low_type)
    normed_ref[...] = normed
    query_sum = jnp.zeros((rows, PAIR), full)
    key_sum = jnp.zeros((rows, PAIR), full)
    for g in range(KV_HEADS):
        raw = dot(normed, weights_ref[:, g * PACK : (g + 1) * PACK])
        raw_ref[g] = raw
        query_sum += raw[:, :PAIR] * raw[:, :PAIR]
        key_sum += raw[:, PAIR:] * raw[:, PAIR:]
    is_key = lax.broadcasted_iota(jnp.int32, key_sum.shape, 1) < HEAD_DIM
    query_inv = lax.rsqrt(
        jnp.sum(query_sum, axis=-1, keepdims=True) / (GROUP * width) + norm_eps
    )
    key_inv = lax.rsqrt(
        jnp.sum(jnp.where(is_key, key_sum, 0.0), axis=-1, keepdims=True) / width + norm_eps
    )
    pair_inv = jnp.where(is_key, key_inv, 1.0)
    meet(peers)
    send = Sender(send_sem, recv_sem)
    slots_sent = []
    for k in (1, 2, 3):
        slots_sent.append(send(slot_a.at[lax.bitwise_xor(y, k)], got_a.at[y], peer_on("y", k)))
        slots_sent.append(send(slot_b.at[lax.bitwise_xor(z, k)], got_b.at[z], peer_on("z", k)))
    got_a[y] = slot_a[y]
    got_b[z] = slot_b[z]
    handed = []
    for k in (1, 2, 3, 4, 5, 6, 7, 0):
        g = lax.bitwise_xor(dp, k)
        target = sent if k else held_ref
        for part, scale in ((0, query_inv), (1, pair_inv)):
            here = slice(part * PAIR, (part + 1) * PAIR)
            scaled = raw_ref[g, :, here] * scale * pack_ref[g, :, here]
            turned = scaled * cos_ref[:, here] + partner(scaled) * sin_ref[:, here]
            target[g, :, here] = turned.astype(low_type)
        if k:
            handed.append(hand_over(sent, held_ref, send_one, recv_one, g))
            handed[-1].start()
    wide_query = GROUP * rows
    third.wait()
    for n in range(4):
        pieces = [
            third_buf[p, m // 4, m % 4, n * 8 : n * 8 + 8, :].astype(full)
            for m in range(8)
            for p in range(4)
        ]
        output_ref[n * 256 : (n + 1) * 256, :] = jnp.concatenate(pieces, axis=0).astype(low_type)

    def step(i, _):
        @pl.when(i != dp)
        def _():
            hand_over(sent, held_ref, send_one, recv_one, i).wait_recv()

        flip_ref[i] = flip(held_ref[i, :, PAIR:]).astype(low_type)
        query = flip(held_ref[i, :, :PAIR]).astype(low_type)
        query = jnp.concatenate([query[:HEAD_DIM], query[HEAD_DIM:]], axis=1)

        def block(j, carry, masked):
            top, total, acc = carry
            key = held_ref[j, :, PAIR : PAIR + HEAD_DIM]
            scores = dot(key, query) * score_scale
            if masked:
                allowed = allowed_of(scores.shape, rows, length_ref[0], i)
                scores = jnp.where(allowed, scores, masked_score)
            new_top = jnp.maximum(top, jnp.max(scores, axis=0, keepdims=True))
            weights = jnp.exp(scores - new_top)
            shrink = jnp.exp(top - new_top)
            total = total * shrink + jnp.sum(weights, axis=0, keepdims=True)
            acc = acc * shrink + dot(flip_ref[j, HEAD_DIM:, :], weights.astype(low_type))
            return new_top, total, acc

        carry = (
            jnp.full((1, wide_query), masked_score, full),
            jnp.zeros((1, wide_query), full),
            jnp.zeros((HEAD_DIM, wide_query), full),
        )
        carry = block(i, carry, True)
        top, total, acc = lax.fori_loop(0, i, lambda j, c: block(j, c, False), carry)
        acc = acc / total
        both = jnp.concatenate([acc[:, :rows], acc[:, rows:]], axis=0)
        att_ref[i] = both.T.astype(low_type)
        log_ref[i] = jnp.broadcast_to(top + jnp.log(total), log_ref.shape[1:])

        @pl.when(i != dp)
        def _():
            hand_over(att_ref, home_ref, send_two, recv_two, i).start()

        @pl.when(i == dp)
        def _():
            home_ref[i] = att_ref[i]

        return 0

    lax.fori_loop(0, blocks, step, 0)
    for copy in handed:
        copy.wait_send()
    for copy in slots_sent:
        copy.wait()
    for k in range(1, 8):
        hand_over(att_ref, home_ref, send_two, recv_two, lax.bitwise_xor(dp, k)).wait()


def forward(lengths, tokens, weights, cosine, sine, slot_a, slot_b, third, number):
    rows, wide = tokens.shape
    shapes = [
        ((wide, wide), low_type),
        ((rows, wide), low_type),
        ((KV_HEADS, rows, PACK), full),
        ((KV_HEADS, 1, PACK), full),
        ((8, wide), full),
        ((8, rows, PACK), low_type),
        ((8, rows, PAIR), low_type),
        ((8, 8, GROUP * rows), full),
        ((KV_HEADS, rows, PAIR), low_type),
        (slot_a.shape, full),
        (slot_b.shape, full),
    ]
    return pl.pallas_call(
        forward_kernel,
        out_shape=[jax.ShapeDtypeStruct(*s) for s in shapes],
        in_specs=[SMEM] + [VMEM] * 6 + [ANY],
        out_specs=[VMEM] * len(shapes),
        scratch_shapes=[
            pltpu.VMEM((KV_HEADS, rows, PACK), low_type),
            pltpu.VMEM((8, PAIR, rows), low_type),
            pltpu.VMEM(third.shape, low_type),
            *[pltpu.SemaphoreType.DMA((8,))] * 4,
            *[pltpu.SemaphoreType.DMA((6,))] * 2,
            pltpu.SemaphoreType.DMA,
        ],
        compiler_params=comm_params(number),
        cost_estimate=cost(45),
        name="forward",
    )(lengths, tokens, weights, cosine, sine, slot_a, slot_b, third)


def backward_kernel(
    length_ref, held_ref, grad_ref, att_ref, log_ref, home_ref, sent, flip_ref, sum_ref, send_sem, recv_sem
):
    dp, _, _ = place_of()
    blocks, rows = held_ref.shape[0], held_ref.shape[1]
    peers = dp_peers()
    greet(peers)
    sum_ref[...] = jnp.zeros_like(sum_ref)
    for j in range(blocks):
        flip_ref[j] = flip(held_ref[j, :, PAIR:])[:HEAD_DIM].astype(low_type)
    meet(peers)
    none = jnp.zeros((rows, HEAD_DIM), low_type)
    key_scale = jnp.where(
        lax.broadcasted_iota(jnp.int32, (rows, PAIR), 1) < HEAD_DIM, score_scale, 1.0
    )

    def heads_beside(values):
        return jnp.concatenate([values[:HEAD_DIM], values[HEAD_DIM:]], axis=1)

    def step(n, _):
        i = blocks - 1 - n
        query_rows = held_ref[i, :, :PAIR]
        grad_rows = grad_ref[i]
        query = heads_beside(flip(query_rows)).astype(low_type)
        grad_full = heads_beside(flip(grad_rows))
        grad = grad_full.astype(low_type)
        inner = jnp.sum(grad_full * heads_beside(flip(att_ref[i])), axis=0, keepdims=True)
        log_total = log_ref[i, :1, :]
        query_side = jnp.concatenate(
            [
                jnp.concatenate([query_rows[:, :HEAD_DIM], none], axis=1),
                jnp.concatenate([query_rows[:, HEAD_DIM:], none], axis=1),
            ],
            axis=0,
        )
        grad_side = jnp.concatenate(
            [
                jnp.concatenate([none, grad_rows[:, :HEAD_DIM]], axis=1),
                jnp.concatenate([none, grad_rows[:, HEAD_DIM:]], axis=1),
            ],
            axis=0,
        )

        def block(j, acc, masked):
            key = held_ref[j, :, PAIR : PAIR + HEAD_DIM]
            value = held_ref[j, :, PAIR + HEAD_DIM :]
            scores = dot(key, query) * score_scale
            soft = jnp.exp(scores - log_total)
            if masked:
                allowed = allowed_of(scores.shape, rows, length_ref[0], i)
                soft = jnp.where(allowed, soft, 0.0)
            soft_grad = dot(value, grad)
            score_grad = (soft * (soft_grad - inner)).astype(low_type)
            sum_ref[j] += dot(score_grad, query_side) + dot(soft.astype(low_type), grad_side)
            return acc + dot(flip_ref[j], score_grad)

        acc = jnp.zeros((HEAD_DIM, GROUP * rows), full)
        acc = block(i, acc, True)
        acc = lax.fori_loop(0, i, lambda j, c: block(j, c, False), acc)
        both = jnp.concatenate([acc[:, :rows], acc[:, rows:]], axis=0) * score_scale
        sent[i, :, :PAIR] = both.T.astype(low_type)
        sent[i, :, PAIR:] = (sum_ref[i] * key_scale).astype(low_type)

        @pl.when(i != dp)
        def _():
            hand_over(sent, home_ref, send_sem, recv_sem, i).start()

        @pl.when(i == dp)
        def _():
            home_ref[i] = sent[i]

        return 0

    lax.fori_loop(0, blocks, step, 0)
    for k in range(1, 8):
        hand_over(sent, home_ref, send_sem, recv_sem, lax.bitwise_xor(dp, k)).wait()


def backward(lengths, held, grad, att, logs, number):
    blocks, rows, _ = held.shape
    return pl.pallas_call(
        backward_kernel,
        out_shape=jax.ShapeDtypeStruct((KV_HEADS, rows, PACK), low_type),
        in_specs=[SMEM] + [VMEM] * 4,
        out_specs=VMEM,
        scratch_shapes=[
            pltpu.VMEM((blocks, rows, PACK), low_type),
            pltpu.VMEM((blocks, HEAD_DIM, rows), low_type),
            pltpu.VMEM((blocks, rows, PAIR), full),
            pltpu.SemaphoreType.DMA((8,)),
            pltpu.SemaphoreType.DMA((8,)),
        ],
        compiler_params=comm_params(number),
        cost_estimate=cost(28),
        name="backward",
    )(lengths, held, grad, att, logs)


def finish_kernel(
    left_ref, right_ref, third_ref, mid_ref, combine_ref, made_ref,
    output_ref, query_ref, key_ref, value_ref, out_proj_ref, router_ref, attn_ref, ffn_ref, query_gain_ref, key_gain_ref,
):
    output_ref[...] = (mid_ref[...] + dot_tn(combine_ref[...], made_ref[...])).astype(low_type)
    out_proj_ref[...] = third_ref[...]
    for g in range(KV_HEADS):
        if g < KV_HEADS // 2:
            piece = left_ref[:, EXTRA + g * PACK : EXTRA + (g + 1) * PACK]
        else:
            piece = right_ref[:, (g - KV_HEADS // 2) * PACK : (g + 1 - KV_HEADS // 2) * PACK]
        head = slice(g * HEAD_DIM, (g + 1) * HEAD_DIM)
        query_ref[:, g * PAIR : (g + 1) * PAIR] = piece[:, :PAIR]
        key_ref[:, head] = piece[:, PAIR : PAIR + HEAD_DIM]
        value_ref[:, head] = piece[:, PAIR + HEAD_DIM :]
    extra = left_ref[:, :EXTRA]
    experts = router_ref.shape[1]
    router_ref[...] = extra[:, :experts]
    rows = extra.shape[0]
    lane = lax.broadcasted_iota(jnp.int32, (rows, rows), 1)
    row = lax.broadcasted_iota(jnp.int32, (rows, rows), 0)
    for n, ref in enumerate((attn_ref, query_gain_ref, ffn_ref, key_gain_ref)):
        column = jnp.broadcast_to(extra[:, experts + n : experts + n + 1], (rows, rows))
        flat = jnp.sum(jnp.where(lane == row, column, 0.0), axis=0, keepdims=True)
        ref[...] = flat[:, : ref.shape[1]]


def expert_kernel(
    experts, x_ref, grad_ref, in_ref, down_ref, router_ref, back_ref, y_ref, p_ref, s_ref, h_ref, l_ref
):
    which = pl.program_id(0)
    first, _, slots, width = x_ref.shape
    rows = first * slots
    x = x_ref[...].reshape(rows, width)
    grad_full = grad_ref[...].reshape(rows, width).astype(full)
    half = down_ref.shape[2]
    projected = dot(x, in_ref[0])
    gate_part, up = projected[:, :half], projected[:, half:]
    sigmoid = 1.0 / (1.0 + jnp.exp(-gate_part))
    silu = gate_part * sigmoid
    hidden = (silu * up).astype(low_type)
    h_ref[0] = hidden
    produced = dot_nt(hidden, down_ref[0]).astype(low_type)
    y_ref[...] = produced.reshape(y_ref.shape)
    logits = dot(x, router_ref[...])
    lane = lax.broadcasted_iota(jnp.int32, logits.shape, 1)
    logits = jnp.where(lane < experts, logits, masked_score)
    shifted = jnp.exp(logits - jnp.max(logits, axis=-1, keepdims=True))
    routing = shifted / jnp.sum(shifted, axis=-1, keepdims=True)
    mine = lane == 2 * lax.axis_index("expert") + which
    chosen = jnp.sum(jnp.where(mine, routing, 0.0), axis=-1, keepdims=True)
    gate = chosen.astype(low_type).astype(full)
    slot_grad = (grad_full * gate).astype(low_type)
    s_ref[0] = slot_grad
    gate_grad = jnp.sum(grad_full * produced.astype(full), axis=-1, keepdims=True)
    logit_grad = (gate_grad * chosen) * (jnp.where(mine, 1.0, 0.0) - routing)
    logit_grad = logit_grad.astype(low_type)
    l_ref[0] = logit_grad
    hidden_grad = dot(slot_grad, down_ref[0])
    gate_back = hidden_grad * up * (sigmoid * (1.0 + gate_part * (1.0 - sigmoid)))
    p_ref[0, :, :half] = gate_back.astype(low_type)
    p_ref[0, :, half:] = (hidden_grad * silu).astype(low_type)
    back = dot_nt(p_ref[0], in_ref[0]) + dot_nt(logit_grad, router_ref[...])
    back_ref[...] = back.astype(low_type).reshape(back_ref.shape)


def middle_back_kernel(
    moe_grad_ref, mid_ref, gain_ref, grad_ref, output_ref, mid_grad_ref, low_ref, att_ref, gain_grad_ref
):
    moe_grad = moe_grad_ref[...]
    mid = mid_ref[...]
    width = mid.shape[1]
    inverse = lax.rsqrt(jnp.mean(mid * mid, axis=-1, keepdims=True) + norm_eps)
    scaled = moe_grad * gain_ref[...]
    shared = jnp.sum(scaled * mid, axis=-1, keepdims=True) * (inverse * inverse * inverse / width)
    mid_grad = grad_ref[...].astype(full) + (scaled * inverse - mid * shared)
    mid_grad_ref[...] = mid_grad
    low = mid_grad.astype(low_type)
    low_ref[...] = low
    gain_grad_ref[...] = jnp.sum(mid * inverse * moe_grad, axis=0, keepdims=True)
    for g in range(KV_HEADS):
        att_ref[g] = dot_nt(low, output_ref[g * PAIR : (g + 1) * PAIR, :]).astype(low_type)


def project_back_kernel(
    back_ref,
    raw_ref,
    pack_ref,
    cos_ref,
    sin_ref,
    weights_ref,
    normed_ref,
    tokens_ref,
    gain_ref,
    mid_grad_ref,
    router_ref,
    ffn_ref,
    att_ref,
    mid_low_ref,
    out_ref,
    first_ref,
    second_ref,
    third_ref,
    low_ref,
):
    rows = tokens_ref.shape[0]
    width = KV_HEADS * HEAD_DIM
    lane = lax.broadcasted_iota(jnp.int32, (rows, PAIR), 1)
    is_key = lane < HEAD_DIM
    sums = [[jnp.zeros((rows, PAIR), full) for _ in range(2)] for _ in range(2)]

    def here_of(part):
        return slice(part * PAIR, (part + 1) * PAIR)

    def unturned(g, part):
        here = here_of(part)
        grad = back_ref[g, :, here].astype(full)
        return grad * cos_ref[:, here] - partner(grad) * sin_ref[:, here]

    def columns(g, part):
        return slice(g * PACK + part * PAIR, g * PACK + (part + 1) * PAIR)

    for g in range(KV_HEADS):
        for part in range(2):
            raw = raw_ref[g, :, here_of(part)]
            sums[part][0] += raw * raw
            sums[part][1] += raw * unturned(g, part) * pack_ref[g, :, here_of(part)]
    mean_of = [GROUP * width, width]
    inverses, shares = [], []
    for part in range(2):
        square, cross = sums[part]
        if part == 1:
            square, cross = jnp.where(is_key, square, 0.0), jnp.where(is_key, cross, 0.0)
        inverse = lax.rsqrt(
            jnp.sum(square, axis=-1, keepdims=True) / mean_of[part] + norm_eps
        )
        share = jnp.sum(cross, axis=-1, keepdims=True) * (
            inverse * inverse * inverse / mean_of[part]
        )
        if part == 1:
            inverse = jnp.where(is_key, inverse, 1.0)
            share = jnp.where(is_key, share, 0.0)
        inverses.append(inverse)
        shares.append(share)
    gains = [[], []]
    for g in range(KV_HEADS):
        for part in range(2):
            raw = raw_ref[g, :, here_of(part)]
            grad = unturned(g, part)
            gains[part].append(
                jnp.sum(raw * inverses[part] * grad, axis=0, keepdims=True)
            )
            result = grad * pack_ref[g, :, here_of(part)] * inverses[part] - raw * shares[part]
            low_ref[:, columns(g, part)] = result.astype(low_type)
    normed_grad = dot_nt(low_ref[...], weights_ref[:, : KV_HEADS * PACK])
    values = tokens_ref[...].astype(full)
    wide = values.shape[1]
    inverse = lax.rsqrt(jnp.mean(values * values, axis=-1, keepdims=True) + norm_eps)
    scaled = normed_grad * gain_ref[0:1, :]
    share = jnp.sum(scaled * values, axis=-1, keepdims=True) * (
        inverse * inverse * inverse / wide
    )
    out_ref[...] = (mid_grad_ref[...] + (scaled * inverse - values * share)).astype(low_type)
    attn_grad = jnp.sum(values * inverse * normed_grad, axis=0, keepdims=True)
    query_grad = jnp.concatenate(gains[0], axis=1)
    key_grad = jnp.concatenate(
        [jnp.concatenate(
            [gains[1][2 * g][:, :HEAD_DIM], gains[1][2 * g + 1][:, :HEAD_DIM]], axis=1
        ) for g in range(KV_HEADS // 2)],
        axis=1,
    )
    key_wide = dot_nt(
        jnp.broadcast_to(key_grad, (8, width)).astype(low_type), key_spread(width, wide)
    )[:1]
    extra = jnp.concatenate(
        [
            jnp.zeros((32, wide), full),
            attn_grad,
            query_grad,
            ffn_ref[...],
            key_wide,
            jnp.zeros((EXTRA - 36, wide), full),
        ],
        axis=0,
    )
    first_ref[:, :EXTRA] = (extra.T + router_ref[...]).astype(low_type)
    wing = KV_HEADS * PACK // 2
    for n in range(0, wing, 256):
        cols = slice(n, n + 256)
        first_ref[:, EXTRA + n : EXTRA + n + 256] = dot(normed_ref[0], low_ref[:, cols]).astype(
            low_type
        )
        second_ref[:, cols] = dot(normed_ref[1], low_ref[:, wing + n : wing + n + 256]).astype(
            low_type
        )
        third_ref[:, cols] = dot(att_ref[...], mid_low_ref[:, cols]).astype(low_type)


def on_device(
    tokens_in,
    lengths,
    routes,
    w_query,
    w_key,
    w_value,
    w_output,
    w_router,
    attn_gain,
    ffn_gain,
    query_gain,
    key_gain,
    expert_in,
    expert_down,
    out_grad,
):
    rows, wide = tokens_in.shape[1], tokens_in.shape[2]
    experts = w_router.shape[1]
    parts = expert_in.shape[0]
    owners = experts // parts
    slots = 5 * rows * routes.shape[2] // (4 * experts)
    tokens = tokens_in[0]
    grad_out = out_grad[0]

    place = lax.axis_index("dp") * rows + jnp.arange(rows)
    valid = (place < lengths[0]).astype(jnp.int32)
    ids = jnp.arange(experts)
    chosen = (
        jnp.sum((routes[0][:, :, None] == ids[None, None, :]).astype(jnp.int32), axis=1)
        * valid[:, None]
    )
    earlier = jnp.cumsum(chosen, axis=0) - chosen
    slot_of = jnp.where(chosen == 1, earlier, -1).T.astype(full)

    lane = jnp.arange(PACK)
    frequency = rope_base ** (
        -2.0 * (lane % (HEAD_DIM // 2)).astype(full) / HEAD_DIM
    )
    angles = place.astype(full)[:, None] * frequency[None, :]
    turning = (lane < PAIR + HEAD_DIM)[None, :]
    cosine = jnp.where(turning, jnp.cos(angles), 1.0)
    sign = jnp.where(lane % HEAD_DIM < HEAD_DIM // 2, -1.0, 1.0)
    sine = jnp.where(turning, jnp.sin(angles) * sign, 0.0)

    gains = jnp.concatenate([attn_gain, query_gain, ffn_gain, key_gain])
    gains = jnp.pad(gains, (0, EXTRA - gains.shape[0]))[None]
    weights, third, grad_slots = gather_dense(
        w_query, w_key, w_value, w_router, gains, slot_of, grad_out, w_output, parts, slots, 1
    )
    grad_held = lax.all_to_all(grad_slots, "expert", split_axis=0, concat_axis=0, tiled=True)

    slot_a = slot_of.reshape(4, 4 * parts, rows)
    slot_b = slot_of.reshape(4, 4, parts, rows).transpose(1, 0, 2, 3).reshape(4, 4 * parts, rows)
    output_proj, normed, raw, pack_row, gain_rows, held, att, logs, att_home, left, right = forward(
        lengths, tokens, weights, cosine, sine, slot_a, slot_b, third, 2
    )
    mid, moe, x = dispatch(
        att_home, output_proj, tokens, gain_rows, left, right, parts, slots, 3
    )
    x = x.reshape(owners, parts, slots, wide)
    step = 8
    total = owners * slots
    half = expert_down.shape[2]
    by_owner = pl.BlockSpec((step, 1, slots, wide), lambda j, s: (s, j, 0, 0))

    def flat(n):
        return pl.BlockSpec((1, step * slots, n), lambda j, s: (j, s, 0))

    def slot_shape(n):
        return jax.ShapeDtypeStruct((parts, total, n), low_type)

    back, made, p, s, h, l = pl.pallas_call(
        functools.partial(expert_kernel, experts),
        grid=(parts, owners // step),
        out_shape=(
            jax.ShapeDtypeStruct((owners, parts, slots, wide), low_type),
            jax.ShapeDtypeStruct((owners, parts, slots, wide), low_type),
            slot_shape(2 * half),
            slot_shape(wide),
            slot_shape(half),
            slot_shape(EXTRA),
        ),
        in_specs=[
            by_owner,
            by_owner,
            pl.BlockSpec((1, wide, 2 * half), lambda j, s: (j, 0, 0)),
            pl.BlockSpec((1, wide, half), lambda j, s: (j, 0, 0)),
            pl.BlockSpec((wide, EXTRA), lambda j, s: (0, KV_HEADS * PACK // EXTRA)),
        ],
        out_specs=(by_owner, by_owner, flat(2 * half), flat(wide), flat(half), flat(EXTRA)),
        name="experts",
        **params(42),
    )(x, grad_held, expert_in, expert_down, weights)

    in_grad, down_grad, router_grad, normed_rows, att_rows, combine, mid_grad, mid_low, ffn_grad, att_grad = collect(
        back, left, right, slot_of, gain_rows,
        (x, p, s, h, l, moe, normed, att_home, weights, mid, grad_out, output_proj),
        (experts, slots), 4,
    )
    made, _ = lax.optimization_barrier((made, mid_low))
    made = lax.all_to_all(made, "expert", split_axis=0, concat_axis=0, tiled=True)

    back = backward(lengths, held, att_grad, att, logs, 5)

    wing = KV_HEADS * PACK // 2
    grad_tokens, *thirds = pl.pallas_call(
        project_back_kernel,
        out_shape=(
            jax.ShapeDtypeStruct((rows, wide), low_type),
            jax.ShapeDtypeStruct((wide, EXTRA + wing), low_type),
            jax.ShapeDtypeStruct((wide, wing), low_type),
            jax.ShapeDtypeStruct((wide, wide), low_type),
        ),
        in_specs=[VMEM] * 14,
        out_specs=(VMEM,) * 4,
        scratch_shapes=[pltpu.VMEM((rows, KV_HEADS * PACK), low_type)],
        name="project_back",
        **params(13),
    )(
        back,
        raw,
        pack_row,
        cosine,
        sine,
        weights,
        normed_rows,
        tokens,
        gain_rows,
        mid_grad,
        router_grad,
        ffn_grad,
        att_rows,
        mid_low,
    )
    left, right, third = reduce_dense(thirds, 6)
    shapes = [
        ((rows, wide), low_type),
        (w_query.shape, full),
        (w_key.shape, full),
        (w_value.shape, full),
        (w_output.shape, full),
        (w_router.shape, full),
        ((1, attn_gain.shape[0]), full),
        ((1, ffn_gain.shape[0]), full),
        ((1, query_gain.shape[0]), full),
        ((1, key_gain.shape[0]), full),
    ]
    results = pl.pallas_call(
        finish_kernel,
        out_shape=[jax.ShapeDtypeStruct(*s) for s in shapes],
        in_specs=[VMEM] * 6,
        out_specs=[VMEM] * len(shapes),
        name="finish",
        **params(6),
    )(
        left,
        right,
        third,
        mid,
        combine.reshape(experts * slots, rows),
        made.reshape(experts * slots, wide),
    )
    return (
        results[0][None],
        grad_tokens[None],
        *results[1:6],
        *[row[0] for row in results[6:10]],
        in_grad,
        down_grad,
    )


def solution(mesh):
    in_specs = (
        P("expert", "dp", None),
        P("expert"),
        P("expert", "dp", None),
        P(("dp", "expert"), None),
        P(("dp", "expert"), None),
        P(("dp", "expert"), None),
        P(("dp", "expert"), None),
        P(("dp", "expert"), None),
        P(("dp", "expert")),
        P(("dp", "expert")),
        P(("dp", "expert")),
        P(("dp", "expert")),
        P("expert", None, None),
        P("expert", None, None),
        P("expert", "dp", None),
    )
    out_specs = (
        P("expert", "dp", None),
        P("expert", "dp", None),
        P(("dp", "expert"), None),
        P(("dp", "expert"), None),
        P(("dp", "expert"), None),
        P(("dp", "expert"), None),
        P(("dp", "expert"), None),
        P(("dp", "expert")),
        P(("dp", "expert")),
        P(("dp", "expert")),
        P(("dp", "expert")),
        P("expert", "dp", None),
        P("expert", "dp", None),
    )
    return jax.shard_map(
        on_device, mesh=mesh, in_specs=in_specs, out_specs=out_specs, check_vma=False
    )
```

```python
import functools

import jax
import jax.numpy as jnp
from jax import lax
from jax.experimental import pallas as pl
from jax.experimental.pallas import tpu as pltpu
from jax.sharding import PartitionSpec as P

HEADS = 16
HEAD_DIM = 64
KV_HEADS = 8
GROUP = HEADS // KV_HEADS
PAIR = GROUP * HEAD_DIM
PACK = PAIR + 2 * HEAD_DIM
EXTRA = 128

norm_eps = 1e-06
rope_base = 10000.0
masked_score = -1e30
score_scale = HEAD_DIM ** (-0.5)
low_type = jnp.bfloat16
full = jnp.float32

VMEM = pl.BlockSpec(memory_space=pltpu.VMEM)
SMEM = pl.BlockSpec(memory_space=pltpu.SMEM)
LIMIT = 56 * 1024 * 1024


def dot(left, right):
    return jnp.dot(left, right, preferred_element_type=full)


def dot_nt(left, right):
    return lax.dot_general(left, right, (((1,), (1,)), ((), ())), preferred_element_type=full)


def dot_tn(left, right):
    return lax.dot_general(left, right, (((0,), (0,)), ((), ())), preferred_element_type=full)


def partner(values):
    lane = lax.broadcasted_iota(jnp.int32, values.shape, 1)
    half = HEAD_DIM // 2
    return jnp.where(
        lane % HEAD_DIM < half, pltpu.roll(values, 128 - half, 1), pltpu.roll(values, half, 1)
    )


def flip(values):
    return values.astype(full).T


def cost(microseconds):
    return pl.CostEstimate(
        flops=int(microseconds * 1.15e9), bytes_accessed=1 << 20, transcendentals=0
    )


def params(microseconds):
    return dict(
        compiler_params=pltpu.CompilerParams(vmem_limit_bytes=LIMIT),
        cost_estimate=cost(microseconds),
    )


MESH = pl.DeviceIdType.MESH
ANY = pl.BlockSpec(memory_space=pl.ANY)


def comm_params(number):
    return pltpu.CompilerParams(
        collective_id=number, has_side_effects=True, vmem_limit_bytes=LIMIT
    )


def place_of():
    dp, expert = lax.axis_index("dp"), lax.axis_index("expert")
    return dp, expert, dict(x=dp // 2, core=dp % 2, y=expert // 4, z=expert % 4)


def peer_on(axis, step):
    dp, expert, _ = place_of()
    if axis == "core":
        return lax.bitwise_xor(dp, 1), expert
    if axis == "x":
        return lax.bitwise_xor(dp, 2 * step), expert
    if axis == "y":
        return dp, lax.bitwise_xor(expert, 4 * step)
    return dp, lax.bitwise_xor(expert, step)


def greet(peers):
    barrier = pltpu.get_barrier_semaphore()
    for device in peers:
        pl.semaphore_signal(barrier, inc=1, device_id=device, device_id_type=MESH)


def meet(peers):
    pl.semaphore_wait(pltpu.get_barrier_semaphore(), len(peers))


def dp_peers():
    dp, expert, _ = place_of()
    return [(lax.bitwise_xor(dp, k), expert) for k in range(1, 8)]


class Mover:
    def __init__(self, sems):
        self.sems, self.count = sems, 0

    def __call__(self, source, target):
        copy = pltpu.make_async_copy(source, target, self.sems.at[self.count])
        self.count += 1
        copy.start()
        return copy


class Sender:
    def __init__(self, send_sem, recv_sem):
        self.send_sem, self.recv_sem, self.count = send_sem, recv_sem, 0

    def __call__(self, source, target, device):
        copy = pltpu.make_async_remote_copy(
            src_ref=source,
            dst_ref=target,
            send_sem=self.send_sem.at[self.count],
            recv_sem=self.recv_sem.at[self.count],
            device_id=device,
            device_id_type=MESH,
        )
        self.count += 1
        copy.start()
        return copy


AXES = ("x", "y", "z")
CUBE = [("core", 1)] + [(axis, k) for axis in AXES for k in (1, 2, 3)]


def placed_rows(slot_row, slots):
    rows = slot_row.shape[1]
    slot = lax.broadcasted_iota(jnp.int32, (slots, rows), 0).astype(full)
    return jnp.where(slot == slot_row, 1.0, 0.0).astype(low_type)


def placed_of(table, slots):
    table = table.reshape(-1, table.shape[-1])
    return jnp.concatenate(
        [placed_rows(table[e : e + 1], slots) for e in range(table.shape[0])], axis=0
    )


def gather_kernel(
    cut, query_ref, key_ref, value_ref, router_ref, gains_ref, slot_a, slot_b, output_ref, out_ref, third_ref, got_a, got_b, shard_ref, shards_ref, mine_ref, others_ref, ours_ref, send_sem, recv_sem, local_sem
):
    _, _, at = place_of()
    x, y, z, c = at["x"], at["y"], at["z"], at["core"]
    columns = shard_ref.shape[1]
    sides = (pl.ds(0, cut), pl.ds(cut, columns - cut))
    peers = [peer_on(axis, k) for axis, k in CUBE]
    greet(peers)
    rows = shard_ref.shape[0]
    for g in range(KV_HEADS):
        here = g * PACK
        shard_ref[:, here : here + PAIR] = query_ref[:, g * PAIR : (g + 1) * PAIR]
        head = slice(g * HEAD_DIM, (g + 1) * HEAD_DIM)
        shard_ref[:, here + PAIR : here + PACK] = jnp.concatenate(
            [key_ref[:, head], value_ref[:, head]], axis=1
        )
    experts = router_ref.shape[1]
    lane = lax.broadcasted_iota(jnp.int32, (rows, EXTRA), 1)
    row = lax.broadcasted_iota(jnp.int32, (rows, EXTRA), 0)
    gains = jnp.broadcast_to(gains_ref[...], (rows, EXTRA))
    extra = jnp.concatenate(
        [router_ref[...], jnp.zeros((rows, EXTRA - experts), full)], axis=1
    )
    for n in range(4):
        column = jnp.sum(jnp.where(lane == row + n * rows, gains, 0.0), axis=1, keepdims=True)
        extra += jnp.where(lane == experts + n, column, 0.0)
    shard_ref[:, KV_HEADS * PACK :] = extra
    meet(peers)
    send = Sender(send_sem, recv_sem)
    first = [send(shard_ref, shards_ref.at[z], peer_on("z", k)) for k in (1, 2, 3)]
    first += [send(output_ref, others_ref.at[x], peer_on("x", k)) for k in (1, 2, 3)]
    shards_ref[z] = shard_ref[...]
    others_ref[x] = output_ref[...]
    move = Mover(local_sem)
    along = []
    for k in (1, 2, 3):
        along.append(send(slot_a.at[lax.bitwise_xor(y, k)], got_a.at[y], peer_on("y", k)))
        along.append(send(slot_b.at[lax.bitwise_xor(z, k)], got_b.at[z], peer_on("z", k)))
    got_a[y] = slot_a[y]
    got_b[z] = slot_b[z]
    for copy in first:
        copy.wait()
    mine_ref[...] = shards_ref[...].reshape(mine_ref.shape).astype(low_type)
    ours_ref[...] = others_ref[...].reshape(ours_ref.shape).astype(low_type)
    local = move(mine_ref, out_ref.at[x, c, y])
    local_third = move(ours_ref, third_ref.at[z, c, y])
    second = []
    for k in (1, 2, 3):
        for side, axis in ((0, "y"), (1, "x")):
            second.append(
                send(
                    mine_ref.at[:, sides[side]],
                    out_ref.at[x, c, y, :, sides[side]],
                    peer_on(axis, k),
                )
            )
        second.append(send(ours_ref, third_ref.at[z, c, y], peer_on("y", k)))
    local.wait()
    local_third.wait()
    for copy in second:
        copy.wait()
    third = []
    for k in (1, 2, 3):
        piece = out_ref.at[x, c, :, :, sides[0]]
        third.append(send(piece, piece, peer_on("x", k)))
        piece = out_ref.at[:, c, y, :, sides[1]]
        third.append(send(piece, piece, peer_on("y", k)))
        piece = third_ref.at[z, c]
        third.append(send(piece, piece, peer_on("z", k)))
    other = peer_on("core", 1)
    last = []
    for piece in (
        out_ref.at[x, c, :, :, sides[0]], out_ref.at[:, c, y, :, sides[1]], third_ref.at[z, c]
    ):
        last.append(send(piece, piece, other))
    for n, k in enumerate((1, 2, 3)):
        third[3 * n].wait_recv()
        piece = out_ref.at[lax.bitwise_xor(x, k), c, :, :, sides[0]]
        last.append(send(piece, piece, other))
        third[3 * n + 1].wait_recv()
        piece = out_ref.at[:, c, lax.bitwise_xor(y, k), :, sides[1]]
        last.append(send(piece, piece, other))
        third[3 * n + 2].wait_recv()
        piece = third_ref.at[lax.bitwise_xor(z, k), c]
        last.append(send(piece, piece, other))
    for copy in third:
        copy.wait_send()
    for copy in last:
        copy.wait()
    for copy in along:
        copy.wait()


def gather_dense(query, key, value, router, gains, slot_a, slot_b, output, number):
    rows = query.shape[0]
    columns = KV_HEADS * PACK + EXTRA
    cut = columns // 256 * 128
    out, third, *rest = pl.pallas_call(
        functools.partial(gather_kernel, cut),
        out_shape=(
            jax.ShapeDtypeStruct((4, 2, 4, 4 * rows, columns), low_type),
            jax.ShapeDtypeStruct((4, 2, 4, 4 * rows, output.shape[1]), low_type),
            jax.ShapeDtypeStruct(slot_a.shape, full),
            jax.ShapeDtypeStruct(slot_b.shape, full),
        ),
        in_specs=[VMEM] * 8,
        out_specs=(ANY, ANY, VMEM, VMEM),
        scratch_shapes=[
            pltpu.VMEM((rows, columns), full),
            pltpu.VMEM((4, rows, columns), full),
            pltpu.VMEM((4 * rows, columns), low_type),
            pltpu.VMEM((4,) + output.shape, full),
            pltpu.VMEM((4 * rows, output.shape[1]), low_type),
            pltpu.SemaphoreType.DMA((42,)),
            pltpu.SemaphoreType.DMA((42,)),
            pltpu.SemaphoreType.DMA((2,)),
        ],
        compiler_params=comm_params(number),
        cost_estimate=cost(36),
        name="gather_dense",
    )(query, key, value, router, gains, slot_a, slot_b, output)
    return out.reshape(128 * rows, columns), third, *rest


def reduce_kernel(
    in0, in1, in2, out0, out1, out2, core0, core1, core2, half0, half1, half2, row0, row1, row2, *rest
):
    (send0, send1, send2, sum0, sum1, sum2, tail0, tail1, tail2, send_sem, recv_sem) = rest
    parts = (
        (in0, out0, core0, half0, row0, send0, sum0, tail0, ("x", "y", "z")),
        (in1, out1, core1, half1, row1, send1, sum1, tail1, ("y", "z", "x")),
        (in2, out2, core2, half2, row2, send2, sum2, tail2, ("z", "x", "y")),
    )
    _, _, at = place_of()
    c = at["core"]
    other = 1 - c
    send = Sender(send_sem, recv_sem)

    def seat(axis, k):
        return lax.bitwise_xor(at[axis], k)

    first, second, third, fourth = {}, {}, {}, {}
    for k in (1, 2, 3, 0):
        for n, (given, _, core, _, _, _, _, _, axes) in enumerate(parts):
            a = seat(axes[0], k)
            first[n, k] = send(given.at[a, other], core.at[a], peer_on("core", 1))
    for k in (1, 2, 3):
        for n, (given, _, core, half, _, out_buf, _, _, axes) in enumerate(parts):
            a = seat(axes[0], k)
            first[n, k].wait_recv()
            out_buf[k - 1] = (given[a, c].astype(full) + core[a].astype(full)).astype(low_type)
            second[n, k] = send(out_buf.at[k - 1], half.at[k - 1], peer_on(axes[0], k))
    for n, (given, _, core, half, row, out_buf, total, _, axes) in enumerate(parts):
        a = seat(axes[0], 0)
        first[n, 0].wait_recv()
        for k in (1, 2, 3):
            second[n, k].wait()
        for k in (1, 2, 3, 0):
            b = seat(axes[1], k)
            value = given[a, c, b].astype(full) + core[a, b].astype(full)
            for m in range(3):
                value += half[m, b].astype(full)
            if k:
                out_buf[k - 1, 0] = value.astype(low_type)
                third[n, k] = send(out_buf.at[k - 1, 0], row.at[k - 1], peer_on(axes[1], k))
            else:
                total[...] = value.reshape(total.shape)
    for n, (_, _, _, _, row, _, total, tail, axes) in enumerate(parts):
        for k in (1, 2, 3):
            third[n, k].wait()
        value = total[...].reshape(row.shape[1:])
        for m in range(3):
            value += row[m].astype(full)
        total[...] = value.reshape(total.shape)
        for k in (1, 2, 3):
            d = seat(axes[2], k)
            fourth[n, k] = send(total.at[d], tail.at[k - 1], peer_on(axes[2], k))
    for n, (_, out, _, _, _, _, total, tail, axes) in enumerate(parts):
        for k in (1, 2, 3):
            fourth[n, k].wait()
        out[...] = total[at[axes[2]]] + tail[0] + tail[1] + tail[2]
    for copy in first.values():
        copy.wait_send()


PLANE = [(axis, k) for axis in ("y", "z") for k in (1, 2, 3)]


def spread_slots(send, move, tables, tokens_of, rows_bufs, out_ref):
    _, _, at = place_of()
    y, z = at["y"], at["z"]
    _, _, _, slots, half = rows_bufs[0].shape
    copies = []
    for k in range(4):
        for side, (rows, table, seat) in enumerate(zip(rows_bufs, tables, (y, z))):
            source = lax.bitwise_xor(seat, k)
            placed = placed_of(table[source], slots)
            rows[k] = dot(placed, tokens_of(side, k)).astype(low_type).reshape(rows.shape[1:])
            if side == 0:
                target = out_ref.at[source, z, :, :, pl.ds(0, half)]
            else:
                target = out_ref.at[y, source, :, :, pl.ds(half, half)]
            across, mine = ("z", z) if side == 0 else ("y", y)
            for n in (1, 2, 3):
                piece = rows.at[k, lax.bitwise_xor(mine, n)]
                copies.append(send(piece, target, peer_on(across, n)))
            copies.append(move(rows.at[k, mine], target))
    return copies


class Homeward:
    def __init__(self, send, move, back_ref, tables, held, going, came):
        _, _, at = place_of()
        self.seats = at["y"], at["z"]
        self.send, self.tables, self.held, self.going, self.came = send, tables, held, going, came
        self.first, self.local, self.second, self.kept = {}, {}, {}, {}
        y, z = self.seats
        half = held[0].shape[-1]
        sides = (pl.ds(0, half), pl.ds(half, half))
        for k in (1, 2, 3, 0):
            to_y, to_z = lax.bitwise_xor(y, k), lax.bitwise_xor(z, k)
            for n in (1, 2, 3):
                piece = back_ref.at[to_y, lax.bitwise_xor(z, n), :, :, sides[0]]
                self.first[0, k, n] = send(piece, held[0].at[k, n], peer_on("z", n))
                piece = back_ref.at[lax.bitwise_xor(y, n), to_z, :, :, sides[1]]
                self.first[1, k, n] = send(piece, held[1].at[k, n], peer_on("y", n))
            self.local[0, k] = move(back_ref.at[to_y, z, :, :, sides[0]], held[0].at[k, 0])
            self.local[1, k] = move(back_ref.at[y, to_z, :, :, sides[1]], held[1].at[k, 0])

    def add(self, k):
        for side, axis in ((0, "y"), (1, "z")):
            held, table = self.held[side], self.tables[side]
            seat, mine = self.seats[side], self.seats[1 - side]
            _, _, parts, slots, half = held.shape
            for n in (1, 2, 3):
                self.first[side, k, n].wait_recv()
            self.local[side, k].wait()
            source = lax.bitwise_xor(seat, k)
            total = jnp.zeros((table.shape[-1], half), full)
            for n in range(4):
                placed = placed_of(table[source, lax.bitwise_xor(mine, n)], slots)
                total += dot_tn(placed, held[k, n].reshape(parts * slots, half))
            if k:
                self.going[side][k - 1] = total.astype(low_type)
                self.second[side, k] = self.send(
                    self.going[side].at[k - 1], self.came[side].at[k - 1], peer_on(axis, k)
                )
            else:
                self.kept[side] = total

    def sums(self):
        for side in (0, 1):
            for k in (1, 2, 3):
                self.second[side, k].wait_recv()
        return jnp.concatenate(
            [
                self.kept[side] + sum(self.came[side][n].astype(full) for n in range(3))
                for side in (0, 1)
            ],
            axis=1,
        )

    def end(self):
        for copies in (self.first, self.second):
            for copy in copies.values():
                copy.wait_send()


def home_scratch(parts, slots, rows, half):
    return [pltpu.VMEM((4, 4, parts, slots, half), low_type)] * 2 + [
        pltpu.VMEM((3, rows, half), low_type)
    ] * 4


def dispatch_kernel(
    att_ref, output_ref, tokens_ref, gains_ref, left_ref, right_ref, mid_ref, moe_ref, out_ref, held_a, held_b, rows_a, rows_b, send_sem, recv_sem, local_sem
):
    _, _, at = place_of()
    y, z = at["y"], at["z"]
    peers = [peer_on(axis, k) for axis, k in PLANE]
    greet(peers)
    attended = jnp.concatenate([att_ref[g] for g in range(KV_HEADS)], axis=1)
    mid = tokens_ref[...].astype(full) + dot(attended, output_ref[...])
    mid_ref[...] = mid
    inverse = lax.rsqrt(jnp.mean(mid * mid, axis=-1, keepdims=True) + norm_eps)
    moe_ref[...] = (mid * inverse * gains_ref[1:2, :]).astype(low_type)
    half = moe_ref.shape[1] // 2
    sides = (pl.ds(0, half), pl.ds(half, half))
    meet(peers)
    send = Sender(send_sem, recv_sem)
    first = {}
    for k in (1, 2, 3):
        first[0, k] = send(moe_ref.at[:, sides[0]], held_a.at[k], peer_on("y", k))
        first[1, k] = send(moe_ref.at[:, sides[1]], held_b.at[k], peer_on("z", k))
    def tokens_of(side, k):
        if k == 0:
            return moe_ref[:, side * half : (side + 1) * half]
        first[side, k].wait_recv()
        return (held_a, held_b)[side][k]

    copies = spread_slots(
        send, Mover(local_sem), (left_ref, right_ref), tokens_of, (rows_a, rows_b), out_ref
    )
    for copy in first.values():
        copy.wait_send()
    for copy in copies:
        copy.wait()


def dispatch(att, output_proj, tokens, gains, left, right, parts, slots, number):
    rows, wide = tokens.shape
    half = wide // 2
    return pl.pallas_call(
        dispatch_kernel,
        out_shape=(
            jax.ShapeDtypeStruct((rows, wide), full),
            jax.ShapeDtypeStruct((rows, wide), low_type),
            jax.ShapeDtypeStruct((4, 4, parts, slots, wide), low_type),
        ),
        in_specs=[VMEM] * 6,
        out_specs=(VMEM, VMEM, ANY),
        scratch_shapes=[
            pltpu.VMEM((4, rows, half), low_type),
            pltpu.VMEM((4, rows, half), low_type),
            pltpu.VMEM((4, 4, parts, slots, half), low_type),
            pltpu.VMEM((4, 4, parts, slots, half), low_type),
            pltpu.SemaphoreType.DMA((30,)),
            pltpu.SemaphoreType.DMA((30,)),
            pltpu.SemaphoreType.DMA((8,)),
        ],
        compiler_params=comm_params(number),
        cost_estimate=cost(50),
        name="dispatch",
    )(att, output_proj, tokens, gains, left, right)


def collect_kernel(*refs):
    (back_ref, left_ref, right_ref, gains_ref, *given) = refs[:14]
    (in_out, down_out, router_out, normed_out, att_out, mid_grad_ref, low_ref, ffn_ref, home_ref) = refs[14:23]
    held_a, held_b, going_a, going_b, came_a, came_b = refs[23:29]
    here = refs[29:39]
    in_buf, down_buf, normed_buf, att_buf, grad_buf = refs[39:44]
    in_core, down_core, in_going, down_going, in_came, down_came = refs[44:50]
    send_sem, recv_sem, local_sem = refs[50:]
    dp, _, at = place_of()
    x, c = at["x"], at["core"]
    rows, wide = mid_grad_ref.shape
    peers = [peer_on(axis, k) for axis, k in PLANE] + dp_peers()
    greet(peers)
    meet(peers)
    send, move = Sender(send_sem, recv_sem), Mover(local_sem)
    homeward = Homeward(
        send, move, back_ref, (left_ref, right_ref), (held_a, held_b), (going_a, going_b), (came_a, came_b)
    )
    x_buf, p_buf, s_buf, h_buf, l_buf, normed_in, att_in, mid_buf, grad_in, output_buf = here
    x_ref, p_ref, s_ref, h_ref, l_ref, normed_ref, att_ref, mid_ref, grad_ref, output_ref = given
    parts = in_buf.shape[0]
    loads = {}
    for j in range(parts):
        loads["x", j] = move(x_ref.at[:, j], x_buf.at[j])
        for name, source, target in (
            ("p", p_ref, p_buf), ("s", s_ref, s_buf), ("h", h_ref, h_buf), ("l", l_ref, l_buf)
        ):
            loads[name, j] = move(source.at[j], target.at[j])
    for name, source, target in (
        ("normed", normed_ref, normed_in), ("att", att_ref, att_in), ("mid", mid_ref, mid_buf),
        ("grad", grad_ref, grad_in), ("output", output_ref, output_buf)
    ):
        loads[name] = move(source, target)
    stores = []

    def x_of(j, n):
        piece = x_buf[j, :, :, n * 256 : (n + 1) * 256]
        return piece.reshape(piece.shape[0] * piece.shape[1], 256)

    def in_job(j):
        loads["x", j].wait()
        loads["p", j].wait()

        for n in range(wide // 256):
            value = dot_tn(x_of(j, n), p_buf[j]).astype(low_type)
            in_buf[j, n, 0] = value[:128]
            in_buf[j, n, 1] = value[128:]
        core_copies["in", j] = send(in_buf.at[j, :, 1 - c], in_core.at[j], peer_on("core", 1))

    def down_job(j):
        for name in "shl":
            loads[name, j].wait()
        for n in range(wide // 256):
            cols = slice(n * 256, (n + 1) * 256)
            value = dot_tn(s_buf[j, :, cols], h_buf[j]).astype(low_type)
            down_buf[j, n, 0] = value[:128]
            down_buf[j, n, 1] = value[128:]
            part = dot_tn(x_of(j, n), l_buf[j])
            router_out[cols, :] = part if j == 0 else router_out[cols, :] + part
        core_copies["down", j] = send(
            down_buf.at[j, :, 1 - c], down_core.at[j], peer_on("core", 1)
        )

    core_copies, x_copies = {}, {}
    buffers = {
        "in": (in_buf, in_core, in_going, in_came, in_out),
        "down": (down_buf, down_core, down_going, down_came, down_out),
    }

    def across_job(name, j):
        own, core, going, came, _ = buffers[name]
        core_copies[name, j].wait_recv()
        for k in (1, 2, 3):
            there = lax.bitwise_xor(x, k)
            value = own[j, there, c].astype(full) + core[j, there].astype(full)
            going[j, k - 1] = value.astype(low_type)
            x_copies[name, j, k] = send(
                going.at[j, k - 1], came.at[j, k - 1], peer_on("x", k)
            )

    def total_job(name, j):
        own, core, _, came, out = buffers[name]
        value = own[j, x, c].astype(full) + core[j, x].astype(full)
        for k in (1, 2, 3):
            x_copies[name, j, k].wait_recv()
            value += came[j, k - 1].astype(full)
        out[j] = value

    def by_place(values, axes):
        strides = dict(x=32, core=16, y=4, z=1)
        counts = dict(x=4, core=2, y=4, z=4)
        places = [0]
        for axis in axes:
            places = [p + n * strides[axis] for p in places for n in range(counts[axis])]
        return jnp.concatenate([values[p * 8 : p * 8 + 8] for p in places], axis=0)

    def order_job():
        loads["normed"].wait()
        values = flip(normed_in[...])
        normed_buf[0] = values.astype(low_type)
        normed_buf[1] = by_place(values, ("y", "core", "z", "x")).astype(low_type)
        stores.append(move(normed_buf, normed_out))
        loads["att"].wait()
        attended = jnp.concatenate([att_in[g] for g in range(KV_HEADS)], axis=1)
        att_buf[...] = by_place(flip(attended), ("z", "core", "x", "y")).astype(low_type)
        stores.append(move(att_buf, att_out))

    in_job(0)
    homeward.add(1)
    in_job(1)
    across_job("in", 0)
    homeward.add(2)
    down_job(0)
    across_job("in", 1)
    homeward.add(3)
    down_job(1)
    across_job("down", 0)
    homeward.add(0)
    order_job()
    across_job("down", 1)
    moe_grad = homeward.sums()
    for name in ("mid", "grad", "output"):
        loads[name].wait()
    mid = mid_buf[...]
    inverse = lax.rsqrt(jnp.mean(mid * mid, axis=-1, keepdims=True) + norm_eps)
    scaled = moe_grad * gains_ref[1:2, :]
    shared = jnp.sum(scaled * mid, axis=-1, keepdims=True) * (inverse * inverse * inverse / wide)
    mid_grad = grad_in[...].astype(full) + (scaled * inverse - mid * shared)
    mid_grad_ref[...] = mid_grad
    low = mid_grad.astype(low_type)
    low_ref[...] = low
    ffn_ref[...] = jnp.sum(mid * inverse * moe_grad, axis=0, keepdims=True)
    third = []
    for k in (1, 2, 3, 4, 5, 6, 7, 0):
        g = lax.bitwise_xor(dp, k)
        piece = dot_nt(low, output_buf[pl.ds(pl.multiple_of(g * PAIR, PAIR), PAIR), :])
        piece = piece.astype(low_type)
        if k:
            grad_buf[g] = piece
            third.append(send(grad_buf.at[g], home_ref.at[dp], peers[5 + k]))
        else:
            home_ref[dp] = piece
    for j in range(parts):
        total_job("in", j)
        total_job("down", j)
    homeward.end()
    for copies in (core_copies, x_copies):
        for copy in copies.values():
            copy.wait_send()
    for copy in third:
        copy.wait()
    for copy in stores:
        copy.wait()


def collect(back, left, right, gains, given, number):
    owners, parts, slots, wide = back.shape
    half = wide // 2
    rows = left.shape[3]
    x, p, s, h, l, normed, att, mid, grad, output_proj = given

    def like(values, *shape):
        return pltpu.VMEM(shape or values.shape, values.dtype)

    outs = [
        jax.ShapeDtypeStruct((parts, wide // 8, p.shape[2]), full),
        jax.ShapeDtypeStruct((parts, wide // 8, h.shape[2]), full),
        jax.ShapeDtypeStruct((wide, EXTRA), full),
        jax.ShapeDtypeStruct((2, wide, rows), low_type),
        jax.ShapeDtypeStruct((wide, rows), low_type),
        jax.ShapeDtypeStruct((rows, wide), full),
        jax.ShapeDtypeStruct((rows, wide), low_type),
        jax.ShapeDtypeStruct((1, wide), full),
        jax.ShapeDtypeStruct((KV_HEADS, rows, PAIR), low_type),
    ]
    return pl.pallas_call(
        collect_kernel,
        out_shape=outs,
        in_specs=[ANY, VMEM, VMEM, VMEM] + [ANY] * 10,
        out_specs=[VMEM, VMEM, VMEM, ANY, ANY, VMEM, VMEM, VMEM, VMEM],
        scratch_shapes=[
            *home_scratch(parts, slots, rows, half),
            like(x, parts, owners, slots, wide),
            like(p), like(s), like(h), like(l), like(normed), like(att),
            like(mid), like(grad), like(output_proj),
            pltpu.VMEM((parts, 4, 2, wide // 8, p.shape[2]), low_type),
            pltpu.VMEM((parts, 4, 2, wide // 8, h.shape[2]), low_type),
            *[pltpu.VMEM(o.shape, o.dtype) for o in (outs[3], outs[4], outs[8])],
            *[
                pltpu.VMEM((parts, n, wide // 8, w.shape[2]), low_type)
                for n in (4, 3, 3)
                for w in (p, h)
            ],
            pltpu.SemaphoreType.DMA((37 + 8 * parts,)),
            pltpu.SemaphoreType.DMA((37 + 8 * parts,)),
            pltpu.SemaphoreType.DMA((8 + 5 * parts + 5 + 2,)),
        ],
        compiler_params=comm_params(number),
        cost_estimate=cost(55),
        name="collect",
    )(back.reshape(4, 4, parts, slots, wide), left, right, gains, *given)


def allowed_of(shape, rows, length, i):
    key_at = lax.broadcasted_iota(jnp.int32, shape, 0)
    query_at = lax.broadcasted_iota(jnp.int32, shape, 1) % rows
    return (key_at <= query_at) & (key_at < length - i * rows)


def key_spread(width, wide):
    out = lax.broadcasted_iota(jnp.int32, (wide, width), 0)
    here = lax.broadcasted_iota(jnp.int32, (wide, width), 1)
    return jnp.where(out == (here // 4) * 8 + here % 4, 1.0, 0.0).astype(low_type)


def hand_over(sent, home, send_sem, recv_sem, i):
    dp, expert, _ = place_of()
    k = lax.bitwise_xor(dp, i)
    return pltpu.make_async_remote_copy(
        src_ref=sent.at[i],
        dst_ref=home.at[dp],
        send_sem=send_sem.at[k],
        recv_sem=recv_sem.at[k],
        device_id=(i, expert),
        device_id_type=MESH,
    )


def forward_kernel(
    length_ref, tokens_ref, weights_ref, cos_ref, sin_ref, left_ref, right_ref, grad_ref, third_ref,
    output_ref, rows_ref, normed_ref, raw_ref, pack_ref, gains_ref, held_ref, att_ref, log_ref, home_ref,
    grad_bufs, rows_a, rows_b, sent, flip_ref, third_buf, send_one, recv_one, send_two, recv_two, send_sem, recv_sem, local_sem, move_sem,
):
    dp, _, at = place_of()
    y, z = at["y"], at["z"]
    peers = dp_peers() + [peer_on(axis, k) for axis, k in PLANE]
    greet(peers)
    third = pltpu.make_async_copy(third_ref, third_buf, local_sem)
    third.start()
    blocks, rows = held_ref.shape[0], held_ref.shape[1]
    wide = tokens_ref.shape[1]
    width = KV_HEADS * HEAD_DIM
    extra = flip(weights_ref[:, KV_HEADS * PACK :])
    gains_ref[0:1, :] = extra[32:33]
    gains_ref[1:2, :] = extra[34:35]
    key_gain = dot(
        jnp.broadcast_to(extra[35:36], (8, wide)).astype(low_type), key_spread(width, wide)
    )[:1]
    for g in range(KV_HEADS):
        pack_ref[g, :, :PAIR] = extra[33:34, g * PAIR : (g + 1) * PAIR]
        pack_ref[g, :, PAIR:] = jnp.concatenate(
            [key_gain[:, g * HEAD_DIM : (g + 1) * HEAD_DIM], jnp.ones((1, HEAD_DIM), full)],
            axis=1,
        )
    meet(peers)
    send = Sender(send_sem, recv_sem)
    half = wide // 2
    along = {}
    for k in (1, 2, 3):
        for side, axis in ((0, "y"), (1, "z")):
            piece = grad_ref.at[:, pl.ds(side * half, half)]
            along[side, k] = send(piece, grad_bufs.at[side, k - 1], peer_on(axis, k))
    values = tokens_ref[...].astype(full)
    inverse = lax.rsqrt(jnp.mean(values * values, axis=-1, keepdims=True) + norm_eps)
    normed = (values * inverse * gains_ref[0:1, :]).astype(low_type)
    normed_ref[...] = normed
    query_sum = jnp.zeros((rows, PAIR), full)
    key_sum = jnp.zeros((rows, PAIR), full)
    for g in range(KV_HEADS):
        raw = dot(normed, weights_ref[:, g * PACK : (g + 1) * PACK])
        raw_ref[g] = raw
        query_sum += raw[:, :PAIR] * raw[:, :PAIR]
        key_sum += raw[:, PAIR:] * raw[:, PAIR:]
    is_key = lax.broadcasted_iota(jnp.int32, key_sum.shape, 1) < HEAD_DIM
    query_inv = lax.rsqrt(
        jnp.sum(query_sum, axis=-1, keepdims=True) / (GROUP * width) + norm_eps
    )
    key_inv = lax.rsqrt(
        jnp.sum(jnp.where(is_key, key_sum, 0.0), axis=-1, keepdims=True) / width + norm_eps
    )
    pair_inv = jnp.where(is_key, key_inv, 1.0)
    move = Mover(move_sem)
    handed = []
    for k in (1, 2, 3, 4, 5, 6, 7, 0):
        g = lax.bitwise_xor(dp, k)
        target = sent if k else held_ref
        for part, scale in ((0, query_inv), (1, pair_inv)):
            here = slice(part * PAIR, (part + 1) * PAIR)
            scaled = raw_ref[g, :, here] * scale * pack_ref[g, :, here]
            turned = scaled * cos_ref[:, here] + partner(scaled) * sin_ref[:, here]
            target[g, :, here] = turned.astype(low_type)
        if k:
            handed.append(hand_over(sent, held_ref, send_one, recv_one, g))
            handed[-1].start()
    def tokens_of(side, k):
        if k == 0:
            return grad_ref[:, side * half : (side + 1) * half]
        along[side, k].wait_recv()
        return grad_bufs[side, k - 1]

    spread = spread_slots(
        send, move, (left_ref, right_ref), tokens_of, (rows_a, rows_b), rows_ref
    )
    wide_query = GROUP * rows
    third.wait()
    for n in range(4):
        pieces = [
            third_buf[p, m // 4, m % 4, n * 8 : n * 8 + 8, :].astype(full)
            for m in range(8)
            for p in range(4)
        ]
        output_ref[n * 256 : (n + 1) * 256, :] = jnp.concatenate(pieces, axis=0).astype(low_type)

    def step(i, _):
        @pl.when(i != dp)
        def _():
            hand_over(sent, held_ref, send_one, recv_one, i).wait_recv()

        flip_ref[i] = flip(held_ref[i, :, PAIR:]).astype(low_type)
        query = flip(held_ref[i, :, :PAIR]).astype(low_type)
        query = jnp.concatenate([query[:HEAD_DIM], query[HEAD_DIM:]], axis=1)

        def block(j, carry, masked):
            top, total, acc = carry
            key = held_ref[j, :, PAIR : PAIR + HEAD_DIM]
            scores = dot(key, query) * score_scale
            if masked:
                allowed = allowed_of(scores.shape, rows, length_ref[0], i)
                scores = jnp.where(allowed, scores, masked_score)
            new_top = jnp.maximum(top, jnp.max(scores, axis=0, keepdims=True))
            weights = jnp.exp(scores - new_top)
            shrink = jnp.exp(top - new_top)
            total = total * shrink + jnp.sum(weights, axis=0, keepdims=True)
            acc = acc * shrink + dot(flip_ref[j, HEAD_DIM:, :], weights.astype(low_type))
            return new_top, total, acc

        carry = (
            jnp.full((1, wide_query), masked_score, full),
            jnp.zeros((1, wide_query), full),
            jnp.zeros((HEAD_DIM, wide_query), full),
        )
        carry = block(i, carry, True)
        top, total, acc = lax.fori_loop(0, i, lambda j, c: block(j, c, False), carry)
        acc = acc / total
        both = jnp.concatenate([acc[:, :rows], acc[:, rows:]], axis=0)
        att_ref[i] = both.T.astype(low_type)
        log_ref[i] = jnp.broadcast_to(top + jnp.log(total), log_ref.shape[1:])

        @pl.when(i != dp)
        def _():
            hand_over(att_ref, home_ref, send_two, recv_two, i).start()

        @pl.when(i == dp)
        def _():
            home_ref[i] = att_ref[i]

        return 0

    lax.fori_loop(0, blocks, step, 0)
    for copy in handed:
        copy.wait_send()
    for copy in spread:
        copy.wait()
    for copy in along.values():
        copy.wait_send()
    for k in range(1, 8):
        hand_over(att_ref, home_ref, send_two, recv_two, lax.bitwise_xor(dp, k)).wait()


def forward(lengths, tokens, weights, cosine, sine, left, right, grad, third, parts, slots, number):
    rows, wide = tokens.shape
    shapes = [
        ((wide, wide), low_type),
        ((4, 4, parts, slots, wide), low_type),
        ((rows, wide), low_type),
        ((KV_HEADS, rows, PACK), full),
        ((KV_HEADS, 1, PACK), full),
        ((8, wide), full),
        ((8, rows, PACK), low_type),
        ((8, rows, PAIR), low_type),
        ((8, 8, GROUP * rows), full),
        ((KV_HEADS, rows, PAIR), low_type),
    ]
    return pl.pallas_call(
        forward_kernel,
        out_shape=[jax.ShapeDtypeStruct(*s) for s in shapes],
        in_specs=[SMEM] + [VMEM] * 7 + [ANY],
        out_specs=[VMEM, ANY] + [VMEM] * (len(shapes) - 2),
        scratch_shapes=[
            pltpu.VMEM((2, 3, rows, wide // 2), low_type),
            pltpu.VMEM((4, 4, parts, slots, wide // 2), low_type),
            pltpu.VMEM((4, 4, parts, slots, wide // 2), low_type),
            pltpu.VMEM((KV_HEADS, rows, PACK), low_type),
            pltpu.VMEM((8, PAIR, rows), low_type),
            pltpu.VMEM(third.shape, low_type),
            *[pltpu.SemaphoreType.DMA((8,))] * 4,
            *[pltpu.SemaphoreType.DMA((30,))] * 2,
            pltpu.SemaphoreType.DMA,
            pltpu.SemaphoreType.DMA((8,)),
        ],
        compiler_params=comm_params(number),
        cost_estimate=cost(45),
        name="forward",
    )(lengths, tokens, weights, cosine, sine, left, right, grad, third)


def backward_kernel(
    length_ref, held_ref, grad_ref, att_ref, log_ref, home_ref, sent, flip_ref, sum_ref, send_sem, recv_sem
):
    dp, _, _ = place_of()
    blocks, rows = held_ref.shape[0], held_ref.shape[1]
    sum_ref[...] = jnp.zeros_like(sum_ref)
    for j in range(blocks):
        flip_ref[j] = flip(held_ref[j, :, PAIR:])[:HEAD_DIM].astype(low_type)
    none = jnp.zeros((rows, HEAD_DIM), low_type)
    key_scale = jnp.where(
        lax.broadcasted_iota(jnp.int32, (rows, PAIR), 1) < HEAD_DIM, score_scale, 1.0
    )

    def heads_beside(values):
        return jnp.concatenate([values[:HEAD_DIM], values[HEAD_DIM:]], axis=1)

    def step(n, _):
        i = blocks - 1 - n
        query_rows = held_ref[i, :, :PAIR]
        grad_rows = grad_ref[i]
        query = heads_beside(flip(query_rows)).astype(low_type)
        grad_full = heads_beside(flip(grad_rows))
        grad = grad_full.astype(low_type)
        inner = jnp.sum(grad_full * heads_beside(flip(att_ref[i])), axis=0, keepdims=True)
        log_total = log_ref[i, :1, :]
        query_side = jnp.concatenate(
            [
                jnp.concatenate([query_rows[:, :HEAD_DIM], none], axis=1),
                jnp.concatenate([query_rows[:, HEAD_DIM:], none], axis=1),
            ],
            axis=0,
        )
        grad_side = jnp.concatenate(
            [
                jnp.concatenate([none, grad_rows[:, :HEAD_DIM]], axis=1),
                jnp.concatenate([none, grad_rows[:, HEAD_DIM:]], axis=1),
            ],
            axis=0,
        )

        def block(j, acc, masked):
            key = held_ref[j, :, PAIR : PAIR + HEAD_DIM]
            value = held_ref[j, :, PAIR + HEAD_DIM :]
            scores = dot(key, query) * score_scale
            soft = jnp.exp(scores - log_total)
            if masked:
                allowed = allowed_of(scores.shape, rows, length_ref[0], i)
                soft = jnp.where(allowed, soft, 0.0)
            soft_grad = dot(value, grad)
            score_grad = (soft * (soft_grad - inner)).astype(low_type)
            sum_ref[j] += dot(score_grad, query_side) + dot(soft.astype(low_type), grad_side)
            return acc + dot(flip_ref[j], score_grad)

        acc = jnp.zeros((HEAD_DIM, GROUP * rows), full)
        acc = block(i, acc, True)
        acc = lax.fori_loop(0, i, lambda j, c: block(j, c, False), acc)
        both = jnp.concatenate([acc[:, :rows], acc[:, rows:]], axis=0) * score_scale
        sent[i, :, :PAIR] = both.T.astype(low_type)
        sent[i, :, PAIR:] = (sum_ref[i] * key_scale).astype(low_type)

        @pl.when(i != dp)
        def _():
            hand_over(sent, home_ref, send_sem, recv_sem, i).start()

        @pl.when(i == dp)
        def _():
            home_ref[i] = sent[i]

        return 0

    lax.fori_loop(0, blocks, step, 0)


def tail_kernel(
    length_ref, held_ref, grad_ref, att_ref, log_ref, pack_ref, gains_ref, left_ref, right_ref, made_ref, *refs
):
    given, refs = refs[:12], refs[12:]
    (output_ref, tokens_ref, *sums), refs = refs[:5], refs[5:]
    here, refs = refs[:12], refs[12:]
    held, going, came, refs = refs[0:2], refs[2:4], refs[4:6], refs[6:]
    (home, sent, flip_ref, sum_ref, low_ref), refs = refs[:5], refs[5:]
    thirds, reduce_scratch, refs = refs[:3], refs[3:21], refs[21:]
    send_one, recv_one, send_two, recv_two, send_three, recv_three, local_sem = refs
    dp, _, _ = place_of()
    peers = dp_peers() + [peer_on(axis, k) for axis, k in PLANE]
    greet(peers)
    move = Mover(local_sem)
    loads = [move(source, target) for source, target in zip(given, here)]
    raw, cos, sin, weights, normed, tokens, mid_grad, router, ffn, att_rows, mid_low, mid = here
    meet(peers)
    homeward = Homeward(
        Sender(send_two, recv_two), move, made_ref, (left_ref, right_ref), held, going, came
    )
    backward_kernel(
        length_ref, held_ref, grad_ref, att_ref, log_ref, home, sent, flip_ref, sum_ref, send_one, recv_one
    )
    for k in (1, 2, 3, 0):
        homeward.add(k)
    for k in range(1, 8):
        hand_over(sent, home, send_one, recv_one, lax.bitwise_xor(dp, k)).wait()
    for load in loads:
        load.wait()
    project_back_kernel(
        home, raw, pack_ref, cos, sin, weights, normed, tokens, gains_ref, mid_grad, router, ffn, att_rows, mid_low,
        tokens_ref, *thirds, low_ref,
    )
    output_ref[...] = (mid[...] + homeward.sums()).astype(low_type)
    homeward.end()
    reduce_kernel(*thirds, *sums, *reduce_scratch, send_three, recv_three)


def tail(lengths, held, grad, att, logs, pack, gains, left, right, made, given, number):
    blocks, rows, _ = held.shape
    owners, parts, slots, wide = made.shape
    wing = KV_HEADS * PACK // 2
    widths = (EXTRA + wing, wing, wide)

    def each(*shape, kind=low_type):
        return [pltpu.VMEM(shape + (w,), kind) for w in widths]

    return pl.pallas_call(
        tail_kernel,
        out_shape=[
            jax.ShapeDtypeStruct((rows, wide), low_type),
            jax.ShapeDtypeStruct((rows, wide), low_type),
            *[jax.ShapeDtypeStruct((8, w), full) for w in widths],
        ],
        in_specs=[SMEM] + [VMEM] * 8 + [ANY] * 13,
        out_specs=[VMEM] * 5,
        scratch_shapes=[
            *[pltpu.VMEM(v.shape, v.dtype) for v in given],
            *home_scratch(parts, slots, rows, wide // 2),
            pltpu.VMEM((KV_HEADS, rows, PACK), low_type),
            pltpu.VMEM((blocks, rows, PACK), low_type),
            pltpu.VMEM((blocks, HEAD_DIM, rows), low_type),
            pltpu.VMEM((blocks, rows, PAIR), full),
            pltpu.VMEM((rows, KV_HEADS * PACK), low_type),
            *each(4, 2, 4, 32),
            *each(4, 4, 32),
            *each(3, 4, 32),
            *each(3, 32),
            *each(3, 4, 32),
            *each(4, 8, kind=full),
            *each(3, 8, kind=full),
            *[pltpu.SemaphoreType.DMA((8,))] * 2,
            *[pltpu.SemaphoreType.DMA((30,))] * 2,
            *[pltpu.SemaphoreType.DMA((39,))] * 2,
            pltpu.SemaphoreType.DMA((20,)),
        ],
        compiler_params=comm_params(number),
        cost_estimate=cost(90),
        name="tail",
    )(
        lengths, held, grad, att, logs, pack, gains, left, right,
        made.reshape(4, 4, parts, slots, wide), *given,
    )


def finish_kernel(
    left_ref, right_ref, third_ref, query_ref, key_ref, value_ref, out_proj_ref, router_ref, attn_ref, ffn_ref, query_gain_ref, key_gain_ref,
):
    out_proj_ref[...] = third_ref[...]
    for g in range(KV_HEADS):
        if g < KV_HEADS // 2:
            piece = left_ref[:, EXTRA + g * PACK : EXTRA + (g + 1) * PACK]
        else:
            piece = right_ref[:, (g - KV_HEADS // 2) * PACK : (g + 1 - KV_HEADS // 2) * PACK]
        head = slice(g * HEAD_DIM, (g + 1) * HEAD_DIM)
        query_ref[:, g * PAIR : (g + 1) * PAIR] = piece[:, :PAIR]
        key_ref[:, head] = piece[:, PAIR : PAIR + HEAD_DIM]
        value_ref[:, head] = piece[:, PAIR + HEAD_DIM :]
    extra = left_ref[:, :EXTRA]
    experts = router_ref.shape[1]
    router_ref[...] = extra[:, :experts]
    rows = extra.shape[0]
    lane = lax.broadcasted_iota(jnp.int32, (rows, rows), 1)
    row = lax.broadcasted_iota(jnp.int32, (rows, rows), 0)
    for n, ref in enumerate((attn_ref, query_gain_ref, ffn_ref, key_gain_ref)):
        column = jnp.broadcast_to(extra[:, experts + n : experts + n + 1], (rows, rows))
        flat = jnp.sum(jnp.where(lane == row, column, 0.0), axis=0, keepdims=True)
        ref[...] = flat[:, : ref.shape[1]]


def expert_kernel(
    experts, x_ref, grad_ref, in_ref, down_ref, router_ref, back_ref, y_ref, p_ref, s_ref, h_ref, l_ref
):
    which = pl.program_id(0)
    first, _, slots, width = x_ref.shape
    rows = first * slots
    x = x_ref[...].reshape(rows, width)
    grad_full = grad_ref[...].reshape(rows, width).astype(full)
    half = down_ref.shape[2]
    projected = dot(x, in_ref[0])
    gate_part, up = projected[:, :half], projected[:, half:]
    sigmoid = 1.0 / (1.0 + jnp.exp(-gate_part))
    silu = gate_part * sigmoid
    hidden = (silu * up).astype(low_type)
    h_ref[0] = hidden
    produced = dot_nt(hidden, down_ref[0]).astype(low_type)
    logits = dot(x, router_ref[...])
    lane = lax.broadcasted_iota(jnp.int32, logits.shape, 1)
    logits = jnp.where(lane < experts, logits, masked_score)
    shifted = jnp.exp(logits - jnp.max(logits, axis=-1, keepdims=True))
    routing = shifted / jnp.sum(shifted, axis=-1, keepdims=True)
    mine = lane == 2 * lax.axis_index("expert") + which
    chosen = jnp.sum(jnp.where(mine, routing, 0.0), axis=-1, keepdims=True)
    gate = chosen.astype(low_type).astype(full)
    y_ref[...] = (produced.astype(full) * gate).astype(low_type).reshape(y_ref.shape)
    slot_grad = (grad_full * gate).astype(low_type)
    s_ref[0] = slot_grad
    gate_grad = jnp.sum(grad_full * produced.astype(full), axis=-1, keepdims=True)
    logit_grad = (gate_grad * chosen) * (jnp.where(mine, 1.0, 0.0) - routing)
    logit_grad = logit_grad.astype(low_type)
    l_ref[0] = logit_grad
    hidden_grad = dot(slot_grad, down_ref[0])
    gate_back = hidden_grad * up * (sigmoid * (1.0 + gate_part * (1.0 - sigmoid)))
    p_ref[0, :, :half] = gate_back.astype(low_type)
    p_ref[0, :, half:] = (hidden_grad * silu).astype(low_type)
    back = dot_nt(p_ref[0], in_ref[0]) + dot_nt(logit_grad, router_ref[...])
    back_ref[...] = back.astype(low_type).reshape(back_ref.shape)


def middle_back_kernel(
    moe_grad_ref, mid_ref, gain_ref, grad_ref, output_ref, mid_grad_ref, low_ref, att_ref, gain_grad_ref
):
    moe_grad = moe_grad_ref[...]
    mid = mid_ref[...]
    width = mid.shape[1]
    inverse = lax.rsqrt(jnp.mean(mid * mid, axis=-1, keepdims=True) + norm_eps)
    scaled = moe_grad * gain_ref[...]
    shared = jnp.sum(scaled * mid, axis=-1, keepdims=True) * (inverse * inverse * inverse / width)
    mid_grad = grad_ref[...].astype(full) + (scaled * inverse - mid * shared)
    mid_grad_ref[...] = mid_grad
    low = mid_grad.astype(low_type)
    low_ref[...] = low
    gain_grad_ref[...] = jnp.sum(mid * inverse * moe_grad, axis=0, keepdims=True)
    for g in range(KV_HEADS):
        att_ref[g] = dot_nt(low, output_ref[g * PAIR : (g + 1) * PAIR, :]).astype(low_type)


def project_back_kernel(
    back_ref,
    raw_ref,
    pack_ref,
    cos_ref,
    sin_ref,
    weights_ref,
    normed_ref,
    tokens_ref,
    gain_ref,
    mid_grad_ref,
    router_ref,
    ffn_ref,
    att_ref,
    mid_low_ref,
    out_ref,
    first_ref,
    second_ref,
    third_ref,
    low_ref,
):
    rows = tokens_ref.shape[0]
    width = KV_HEADS * HEAD_DIM
    lane = lax.broadcasted_iota(jnp.int32, (rows, PAIR), 1)
    is_key = lane < HEAD_DIM
    sums = [[jnp.zeros((rows, PAIR), full) for _ in range(2)] for _ in range(2)]

    def here_of(part):
        return slice(part * PAIR, (part + 1) * PAIR)

    def unturned(g, part):
        here = here_of(part)
        grad = back_ref[g, :, here].astype(full)
        return grad * cos_ref[:, here] - partner(grad) * sin_ref[:, here]

    def columns(g, part):
        return slice(g * PACK + part * PAIR, g * PACK + (part + 1) * PAIR)

    for g in range(KV_HEADS):
        for part in range(2):
            raw = raw_ref[g, :, here_of(part)]
            sums[part][0] += raw * raw
            sums[part][1] += raw * unturned(g, part) * pack_ref[g, :, here_of(part)]
    mean_of = [GROUP * width, width]
    inverses, shares = [], []
    for part in range(2):
        square, cross = sums[part]
        if part == 1:
            square, cross = jnp.where(is_key, square, 0.0), jnp.where(is_key, cross, 0.0)
        inverse = lax.rsqrt(
            jnp.sum(square, axis=-1, keepdims=True) / mean_of[part] + norm_eps
        )
        share = jnp.sum(cross, axis=-1, keepdims=True) * (
            inverse * inverse * inverse / mean_of[part]
        )
        if part == 1:
            inverse = jnp.where(is_key, inverse, 1.0)
            share = jnp.where(is_key, share, 0.0)
        inverses.append(inverse)
        shares.append(share)
    gains = [[], []]
    for g in range(KV_HEADS):
        for part in range(2):
            raw = raw_ref[g, :, here_of(part)]
            grad = unturned(g, part)
            gains[part].append(
                jnp.sum(raw * inverses[part] * grad, axis=0, keepdims=True)
            )
            result = grad * pack_ref[g, :, here_of(part)] * inverses[part] - raw * shares[part]
            low_ref[:, columns(g, part)] = result.astype(low_type)
    normed_grad = dot_nt(low_ref[...], weights_ref[:, : KV_HEADS * PACK])
    values = tokens_ref[...].astype(full)
    wide = values.shape[1]
    inverse = lax.rsqrt(jnp.mean(values * values, axis=-1, keepdims=True) + norm_eps)
    scaled = normed_grad * gain_ref[0:1, :]
    share = jnp.sum(scaled * values, axis=-1, keepdims=True) * (
        inverse * inverse * inverse / wide
    )
    out_ref[...] = (mid_grad_ref[...] + (scaled * inverse - values * share)).astype(low_type)
    attn_grad = jnp.sum(values * inverse * normed_grad, axis=0, keepdims=True)
    query_grad = jnp.concatenate(gains[0], axis=1)
    key_grad = jnp.concatenate(
        [jnp.concatenate(
            [gains[1][2 * g][:, :HEAD_DIM], gains[1][2 * g + 1][:, :HEAD_DIM]], axis=1
        ) for g in range(KV_HEADS // 2)],
        axis=1,
    )
    key_wide = dot_nt(
        jnp.broadcast_to(key_grad, (8, width)).astype(low_type), key_spread(width, wide)
    )[:1]
    extra = jnp.concatenate(
        [
            jnp.zeros((32, wide), full),
            attn_grad,
            query_grad,
            ffn_ref[...],
            key_wide,
            jnp.zeros((EXTRA - 36, wide), full),
        ],
        axis=0,
    )
    places = first_ref.shape[:-1]
    first_ref[..., :EXTRA] = (
        (extra.T + router_ref[...]).astype(low_type).reshape(places + (EXTRA,))
    )
    wing = KV_HEADS * PACK // 2

    def put(ref, start, value):
        ref[..., start : start + 256] = value.astype(low_type).reshape(places + (256,))

    for n in range(0, wing, 256):
        put(first_ref, EXTRA + n, dot(normed_ref[0], low_ref[:, n : n + 256]))
        put(second_ref, n, dot(normed_ref[1], low_ref[:, wing + n : wing + n + 256]))
        put(third_ref, n, dot(att_ref[...], mid_low_ref[:, n : n + 256]))


def on_device(
    tokens_in,
    lengths,
    routes,
    w_query,
    w_key,
    w_value,
    w_output,
    w_router,
    attn_gain,
    ffn_gain,
    query_gain,
    key_gain,
    expert_in,
    expert_down,
    out_grad,
):
    rows, wide = tokens_in.shape[1], tokens_in.shape[2]
    experts = w_router.shape[1]
    parts = expert_in.shape[0]
    owners = experts // parts
    slots = 5 * rows * routes.shape[2] // (4 * experts)
    tokens = tokens_in[0]
    grad_out = out_grad[0]

    place = lax.axis_index("dp") * rows + jnp.arange(rows)
    valid = (place < lengths[0]).astype(jnp.int32)
    ids = jnp.arange(experts)
    chosen = (
        jnp.sum((routes[0][:, :, None] == ids[None, None, :]).astype(jnp.int32), axis=1)
        * valid[:, None]
    )
    earlier = jnp.cumsum(chosen, axis=0) - chosen
    slot_of = jnp.where(chosen == 1, earlier, -1).T.astype(full)

    lane = jnp.arange(PACK)
    frequency = rope_base ** (
        -2.0 * (lane % (HEAD_DIM // 2)).astype(full) / HEAD_DIM
    )
    angles = place.astype(full)[:, None] * frequency[None, :]
    turning = (lane < PAIR + HEAD_DIM)[None, :]
    cosine = jnp.where(turning, jnp.cos(angles), 1.0)
    sign = jnp.where(lane % HEAD_DIM < HEAD_DIM // 2, -1.0, 1.0)
    sine = jnp.where(turning, jnp.sin(angles) * sign, 0.0)

    gains = jnp.concatenate([attn_gain, query_gain, ffn_gain, key_gain])
    gains = jnp.pad(gains, (0, EXTRA - gains.shape[0]))[None]
    slot_a = slot_of.reshape(4, 4, parts, rows)
    slot_b = slot_a.transpose(1, 0, 2, 3)
    weights, third, left, right = gather_dense(
        w_query, w_key, w_value, w_router, gains, slot_a, slot_b, w_output, 1
    )
    output_proj, grad_held, normed, raw, pack_row, gain_rows, held, att, logs, att_home = forward(
        lengths, tokens, weights, cosine, sine, left, right, grad_out, third, parts, slots, 2
    )
    mid, moe, x = dispatch(
        att_home, output_proj, tokens, gain_rows, left, right, parts, slots, 3
    )
    grad_held = grad_held.reshape(owners, parts, slots, wide)
    x = x.reshape(owners, parts, slots, wide)
    step = 8
    total = owners * slots
    half = expert_down.shape[2]
    by_owner = pl.BlockSpec((step, 1, slots, wide), lambda j, s: (s, j, 0, 0))

    def flat(n):
        return pl.BlockSpec((1, step * slots, n), lambda j, s: (j, s, 0))

    def slot_shape(n):
        return jax.ShapeDtypeStruct((parts, total, n), low_type)

    back, made, p, s, h, l = pl.pallas_call(
        functools.partial(expert_kernel, experts),
        grid=(parts, owners // step),
        out_shape=(
            jax.ShapeDtypeStruct((owners, parts, slots, wide), low_type),
            jax.ShapeDtypeStruct((owners, parts, slots, wide), low_type),
            slot_shape(2 * half),
            slot_shape(wide),
            slot_shape(half),
            slot_shape(EXTRA),
        ),
        in_specs=[
            by_owner,
            by_owner,
            pl.BlockSpec((1, wide, 2 * half), lambda j, s: (j, 0, 0)),
            pl.BlockSpec((1, wide, half), lambda j, s: (j, 0, 0)),
            pl.BlockSpec((wide, EXTRA), lambda j, s: (0, KV_HEADS * PACK // EXTRA)),
        ],
        out_specs=(by_owner, by_owner, flat(2 * half), flat(wide), flat(half), flat(EXTRA)),
        name="experts",
        **params(42),
    )(x, grad_held, expert_in, expert_down, weights)

    in_grad, down_grad, router_grad, normed_rows, att_rows, mid_grad, mid_low, ffn_grad, att_grad = collect(
        back, left, right, gain_rows,
        (x, p, s, h, l, normed, att_home, mid, grad_out, output_proj), 4,
    )
    output, grad_tokens, *sums = tail(
        lengths, held, att_grad, att, logs, pack_row, gain_rows, left, right, made,
        (raw, cosine, sine, weights, normed_rows, tokens, mid_grad, router_grad, ffn_grad, att_rows, mid_low, mid), 5,
    )
    shapes = [
        (w_query.shape, full),
        (w_key.shape, full),
        (w_value.shape, full),
        (w_output.shape, full),
        (w_router.shape, full),
        ((1, attn_gain.shape[0]), full),
        ((1, ffn_gain.shape[0]), full),
        ((1, query_gain.shape[0]), full),
        ((1, key_gain.shape[0]), full),
    ]
    results = pl.pallas_call(
        finish_kernel,
        out_shape=[jax.ShapeDtypeStruct(*s) for s in shapes],
        in_specs=[VMEM] * 3,
        out_specs=[VMEM] * len(shapes),
        name="finish",
        **params(2),
    )(*sums)
    return (
        output[None],
        grad_tokens[None],
        *results[:5],
        *[row[0] for row in results[5:]],
        in_grad,
        down_grad,
    )


def solution(mesh):
    in_specs = (
        P("expert", "dp", None),
        P("expert"),
        P("expert", "dp", None),
        P(("dp", "expert"), None),
        P(("dp", "expert"), None),
        P(("dp", "expert"), None),
        P(("dp", "expert"), None),
        P(("dp", "expert"), None),
        P(("dp", "expert")),
        P(("dp", "expert")),
        P(("dp", "expert")),
        P(("dp", "expert")),
        P("expert", None, None),
        P("expert", None, None),
        P("expert", "dp", None),
    )
    out_specs = (
        P("expert", "dp", None),
        P("expert", "dp", None),
        P(("dp", "expert"), None),
        P(("dp", "expert"), None),
        P(("dp", "expert"), None),
        P(("dp", "expert"), None),
        P(("dp", "expert"), None),
        P(("dp", "expert")),
        P(("dp", "expert")),
        P(("dp", "expert")),
        P(("dp", "expert")),
        P("expert", "dp", None),
        P("expert", "dp", None),
    )
    return jax.shard_map(
        on_device, mesh=mesh, in_specs=in_specs, out_specs=out_specs, check_vma=False
    )
```

```python
import functools

import jax
import jax.numpy as jnp
from jax import lax
from jax.experimental import pallas as pl
from jax.experimental.pallas import tpu as pltpu
from jax.sharding import PartitionSpec as P

HEADS = 16
HEAD_DIM = 64
KV_HEADS = 8
GROUP = HEADS // KV_HEADS
PAIR = GROUP * HEAD_DIM
PACK = PAIR + 2 * HEAD_DIM
EXTRA = 128

norm_eps = 1e-06
rope_base = 10000.0
masked_score = -1e30
score_scale = HEAD_DIM ** (-0.5)
low_type = jnp.bfloat16
full = jnp.float32

VMEM = pl.BlockSpec(memory_space=pltpu.VMEM)
SMEM = pl.BlockSpec(memory_space=pltpu.SMEM)
LIMIT = 62 * 1024 * 1024


def dot(left, right):
    return jnp.dot(left, right, preferred_element_type=full)


def dot_nt(left, right):
    return lax.dot_general(left, right, (((1,), (1,)), ((), ())), preferred_element_type=full)


def dot_tn(left, right):
    return lax.dot_general(left, right, (((0,), (0,)), ((), ())), preferred_element_type=full)


def partner(values):
    lane = lax.broadcasted_iota(jnp.int32, values.shape, 1)
    half = HEAD_DIM // 2
    return jnp.where(
        lane % HEAD_DIM < half, pltpu.roll(values, 128 - half, 1), pltpu.roll(values, half, 1)
    )


def flip(values):
    return values.astype(full).T


def cost(microseconds):
    return pl.CostEstimate(
        flops=int(microseconds * 1.15e9), bytes_accessed=1 << 20, transcendentals=0
    )


def params(microseconds):
    return dict(
        compiler_params=pltpu.CompilerParams(vmem_limit_bytes=LIMIT),
        cost_estimate=cost(microseconds),
    )


MESH = pl.DeviceIdType.MESH
ANY = pl.BlockSpec(memory_space=pl.ANY)


def comm_params(number):
    return pltpu.CompilerParams(
        collective_id=number, has_side_effects=True, vmem_limit_bytes=LIMIT
    )


def place_of():
    dp, expert = lax.axis_index("dp"), lax.axis_index("expert")
    return dp, expert, dict(x=dp // 2, core=dp % 2, y=expert // 4, z=expert % 4)


def peer_on(axis, step):
    dp, expert, _ = place_of()
    if axis == "core":
        return lax.bitwise_xor(dp, 1), expert
    if axis == "x":
        return lax.bitwise_xor(dp, 2 * step), expert
    if axis == "y":
        return dp, lax.bitwise_xor(expert, 4 * step)
    return dp, lax.bitwise_xor(expert, step)


def greet(peers):
    barrier = pltpu.get_barrier_semaphore()
    for device in peers:
        pl.semaphore_signal(barrier, inc=1, device_id=device, device_id_type=MESH)


def meet(peers):
    pl.semaphore_wait(pltpu.get_barrier_semaphore(), len(peers))


def dp_peers():
    dp, expert, _ = place_of()
    return [(lax.bitwise_xor(dp, k), expert) for k in range(1, 8)]


class Mover:
    def __init__(self, sems):
        self.sems, self.count = sems, 0

    def __call__(self, source, target):
        copy = pltpu.make_async_copy(source, target, self.sems.at[self.count])
        self.count += 1
        copy.start()
        return copy


class Sender:
    def __init__(self, send_sem, recv_sem):
        self.send_sem, self.recv_sem, self.count = send_sem, recv_sem, 0

    def __call__(self, source, target, device):
        copy = pltpu.make_async_remote_copy(
            src_ref=source,
            dst_ref=target,
            send_sem=self.send_sem.at[self.count],
            recv_sem=self.recv_sem.at[self.count],
            device_id=device,
            device_id_type=MESH,
        )
        self.count += 1
        copy.start()
        return copy


AXES = ("x", "y", "z")
CUBE = [("core", 1)] + [(axis, k) for axis in AXES for k in (1, 2, 3)]


def placed_rows(slot_row, slots):
    rows = slot_row.shape[1]
    slot = lax.broadcasted_iota(jnp.int32, (slots, rows), 0).astype(full)
    return jnp.where(slot == slot_row, 1.0, 0.0).astype(low_type)


def placed_of(table, slots):
    table = table.reshape(-1, table.shape[-1])
    return jnp.concatenate(
        [placed_rows(table[e : e + 1], slots) for e in range(table.shape[0])], axis=0
    )


def gather_kernel(
    cut, query_ref, key_ref, value_ref, router_ref, gains_ref, slot_a, slot_b, output_ref, out_ref, third_ref, got_a, got_b, shard_ref, shards_ref, mine_ref, others_ref, ours_ref, send_sem, recv_sem, local_sem
):
    _, _, at = place_of()
    x, y, z, c = at["x"], at["y"], at["z"], at["core"]
    columns = shard_ref.shape[1]
    sides = (pl.ds(0, cut), pl.ds(cut, columns - cut))
    peers = [peer_on(axis, k) for axis, k in CUBE]
    greet(peers)
    rows = shard_ref.shape[0]
    for g in range(KV_HEADS):
        here = g * PACK
        shard_ref[:, here : here + PAIR] = query_ref[:, g * PAIR : (g + 1) * PAIR]
        head = slice(g * HEAD_DIM, (g + 1) * HEAD_DIM)
        shard_ref[:, here + PAIR : here + PACK] = jnp.concatenate(
            [key_ref[:, head], value_ref[:, head]], axis=1
        )
    experts = router_ref.shape[1]
    lane = lax.broadcasted_iota(jnp.int32, (rows, EXTRA), 1)
    row = lax.broadcasted_iota(jnp.int32, (rows, EXTRA), 0)
    gains = jnp.broadcast_to(gains_ref[...], (rows, EXTRA))
    extra = jnp.concatenate(
        [router_ref[...], jnp.zeros((rows, EXTRA - experts), full)], axis=1
    )
    for n in range(4):
        column = jnp.sum(jnp.where(lane == row + n * rows, gains, 0.0), axis=1, keepdims=True)
        extra += jnp.where(lane == experts + n, column, 0.0)
    shard_ref[:, KV_HEADS * PACK :] = extra
    meet(peers)
    send = Sender(send_sem, recv_sem)
    first = [send(shard_ref, shards_ref.at[z], peer_on("z", k)) for k in (1, 2, 3)]
    first += [send(output_ref, others_ref.at[x], peer_on("x", k)) for k in (1, 2, 3)]
    shards_ref[z] = shard_ref[...]
    others_ref[x] = output_ref[...]
    move = Mover(local_sem)
    along = []
    for k in (1, 2, 3):
        along.append(send(slot_a.at[lax.bitwise_xor(y, k)], got_a.at[y], peer_on("y", k)))
        along.append(send(slot_b.at[lax.bitwise_xor(z, k)], got_b.at[z], peer_on("z", k)))
    got_a[y] = slot_a[y]
    got_b[z] = slot_b[z]
    for copy in first:
        copy.wait()
    mine_ref[...] = shards_ref[...].reshape(mine_ref.shape).astype(low_type)
    ours_ref[...] = others_ref[...].reshape(ours_ref.shape).astype(low_type)
    local = move(mine_ref, out_ref.at[x, c, y])
    local_third = move(ours_ref, third_ref.at[z, c, y])
    second = []
    for k in (1, 2, 3):
        for side, axis in ((0, "y"), (1, "x")):
            second.append(
                send(
                    mine_ref.at[:, sides[side]],
                    out_ref.at[x, c, y, :, sides[side]],
                    peer_on(axis, k),
                )
            )
        second.append(send(ours_ref, third_ref.at[z, c, y], peer_on("y", k)))
    local.wait()
    local_third.wait()
    for copy in second:
        copy.wait()
    third = []
    for k in (1, 2, 3):
        piece = out_ref.at[x, c, :, :, sides[0]]
        third.append(send(piece, piece, peer_on("x", k)))
        piece = out_ref.at[:, c, y, :, sides[1]]
        third.append(send(piece, piece, peer_on("y", k)))
        piece = third_ref.at[z, c]
        third.append(send(piece, piece, peer_on("z", k)))
    other = peer_on("core", 1)
    last = []
    for piece in (
        out_ref.at[x, c, :, :, sides[0]], out_ref.at[:, c, y, :, sides[1]], third_ref.at[z, c]
    ):
        last.append(send(piece, piece, other))
    for n, k in enumerate((1, 2, 3)):
        third[3 * n].wait_recv()
        piece = out_ref.at[lax.bitwise_xor(x, k), c, :, :, sides[0]]
        last.append(send(piece, piece, other))
        third[3 * n + 1].wait_recv()
        piece = out_ref.at[:, c, lax.bitwise_xor(y, k), :, sides[1]]
        last.append(send(piece, piece, other))
        third[3 * n + 2].wait_recv()
        piece = third_ref.at[lax.bitwise_xor(z, k), c]
        last.append(send(piece, piece, other))
    for copy in third:
        copy.wait_send()
    for copy in last:
        copy.wait()
    for copy in along:
        copy.wait()


def gather_dense(query, key, value, router, gains, slot_a, slot_b, output, number):
    rows = query.shape[0]
    columns = KV_HEADS * PACK + EXTRA
    cut = columns // 256 * 128
    out, third, *rest = pl.pallas_call(
        functools.partial(gather_kernel, cut),
        out_shape=(
            jax.ShapeDtypeStruct((4, 2, 4, 4 * rows, columns), low_type),
            jax.ShapeDtypeStruct((4, 2, 4, 4 * rows, output.shape[1]), low_type),
            jax.ShapeDtypeStruct(slot_a.shape, full),
            jax.ShapeDtypeStruct(slot_b.shape, full),
        ),
        in_specs=[VMEM] * 8,
        out_specs=(ANY, ANY, VMEM, VMEM),
        scratch_shapes=[
            pltpu.VMEM((rows, columns), full),
            pltpu.VMEM((4, rows, columns), full),
            pltpu.VMEM((4 * rows, columns), low_type),
            pltpu.VMEM((4,) + output.shape, full),
            pltpu.VMEM((4 * rows, output.shape[1]), low_type),
            pltpu.SemaphoreType.DMA((42,)),
            pltpu.SemaphoreType.DMA((42,)),
            pltpu.SemaphoreType.DMA((2,)),
        ],
        compiler_params=comm_params(number),
        cost_estimate=cost(36),
        name="gather_dense",
    )(query, key, value, router, gains, slot_a, slot_b, output)
    return out.reshape(128 * rows, columns), third, *rest


def reduce_kernel(
    in0, in1, in2, out0, out1, out2, core0, core1, core2, half0, half1, half2, row0, row1, row2, *rest
):
    (send0, send1, send2, sum0, sum1, sum2, tail0, tail1, tail2, send_sem, recv_sem) = rest
    parts = (
        (in0, out0, core0, half0, row0, send0, sum0, tail0, ("x", "y", "z")),
        (in1, out1, core1, half1, row1, send1, sum1, tail1, ("y", "z", "x")),
        (in2, out2, core2, half2, row2, send2, sum2, tail2, ("z", "x", "y")),
    )
    _, _, at = place_of()
    c = at["core"]
    other = 1 - c
    send = Sender(send_sem, recv_sem)

    def seat(axis, k):
        return lax.bitwise_xor(at[axis], k)

    first, second, third, fourth = {}, {}, {}, {}
    for k in (1, 2, 3, 0):
        for n, (given, _, core, _, _, _, _, _, axes) in enumerate(parts):
            a = seat(axes[0], k)
            first[n, k] = send(given.at[a, other], core.at[a], peer_on("core", 1))
    for k in (1, 2, 3):
        for n, (given, _, core, half, _, out_buf, _, _, axes) in enumerate(parts):
            a = seat(axes[0], k)
            first[n, k].wait_recv()
            out_buf[k - 1] = (given[a, c].astype(full) + core[a].astype(full)).astype(low_type)
            second[n, k] = send(out_buf.at[k - 1], half.at[k - 1], peer_on(axes[0], k))
    for n, (given, _, core, half, row, out_buf, total, _, axes) in enumerate(parts):
        a = seat(axes[0], 0)
        first[n, 0].wait_recv()
        for k in (1, 2, 3):
            second[n, k].wait()
        for k in (1, 2, 3, 0):
            b = seat(axes[1], k)
            value = given[a, c, b].astype(full) + core[a, b].astype(full)
            for m in range(3):
                value += half[m, b].astype(full)
            if k:
                out_buf[k - 1, 0] = value.astype(low_type)
                third[n, k] = send(out_buf.at[k - 1, 0], row.at[k - 1], peer_on(axes[1], k))
            else:
                total[...] = value.reshape(total.shape)
    for n, (_, _, _, _, row, _, total, tail, axes) in enumerate(parts):
        for k in (1, 2, 3):
            third[n, k].wait()
        value = total[...].reshape(row.shape[1:])
        for m in range(3):
            value += row[m].astype(full)
        total[...] = value.reshape(total.shape)
        for k in (1, 2, 3):
            d = seat(axes[2], k)
            fourth[n, k] = send(total.at[d], tail.at[k - 1], peer_on(axes[2], k))
    for n, (_, out, _, _, _, _, total, tail, axes) in enumerate(parts):
        for k in (1, 2, 3):
            fourth[n, k].wait()
        out[...] = total[at[axes[2]]] + tail[0] + tail[1] + tail[2]
    for copy in first.values():
        copy.wait_send()


PLANE = [(axis, k) for axis in ("y", "z") for k in (1, 2, 3)]


def spread_slots(send, move, tables, tokens_of, rows_bufs, out_ref):
    _, _, at = place_of()
    y, z = at["y"], at["z"]
    _, _, _, slots, half = rows_bufs[0].shape
    copies = []
    for k in range(4):
        for side, (rows, table, seat) in enumerate(zip(rows_bufs, tables, (y, z))):
            source = lax.bitwise_xor(seat, k)
            placed = placed_of(table[source], slots)
            rows[k] = dot(placed, tokens_of(side, k)).astype(low_type).reshape(rows.shape[1:])
            if side == 0:
                target = out_ref.at[source, z, :, :, pl.ds(0, half)]
            else:
                target = out_ref.at[y, source, :, :, pl.ds(half, half)]
            across, mine = ("z", z) if side == 0 else ("y", y)
            for n in (1, 2, 3):
                piece = rows.at[k, lax.bitwise_xor(mine, n)]
                copies.append(send(piece, target, peer_on(across, n)))
            copies.append(move(rows.at[k, mine], target))
    return copies


class Homeward:
    def __init__(self, send, move, back_ref, tables, held, going, came):
        _, _, at = place_of()
        self.seats = at["y"], at["z"]
        self.send, self.tables, self.held, self.going, self.came = send, tables, held, going, came
        self.first, self.local, self.second, self.kept = {}, {}, {}, {}
        y, z = self.seats
        half = held[0].shape[-1]
        sides = (pl.ds(0, half), pl.ds(half, half))
        for k in (1, 2, 3, 0):
            to_y, to_z = lax.bitwise_xor(y, k), lax.bitwise_xor(z, k)
            for n in (1, 2, 3):
                piece = back_ref.at[to_y, lax.bitwise_xor(z, n), :, :, sides[0]]
                self.first[0, k, n] = send(piece, held[0].at[k, n], peer_on("z", n))
                piece = back_ref.at[lax.bitwise_xor(y, n), to_z, :, :, sides[1]]
                self.first[1, k, n] = send(piece, held[1].at[k, n], peer_on("y", n))
            self.local[0, k] = move(back_ref.at[to_y, z, :, :, sides[0]], held[0].at[k, 0])
            self.local[1, k] = move(back_ref.at[y, to_z, :, :, sides[1]], held[1].at[k, 0])

    def add(self, k):
        for side, axis in ((0, "y"), (1, "z")):
            held, table = self.held[side], self.tables[side]
            seat, mine = self.seats[side], self.seats[1 - side]
            _, _, parts, slots, half = held.shape
            for n in (1, 2, 3):
                self.first[side, k, n].wait_recv()
            self.local[side, k].wait()
            source = lax.bitwise_xor(seat, k)
            total = jnp.zeros((table.shape[-1], half), full)
            for n in range(4):
                placed = placed_of(table[source, lax.bitwise_xor(mine, n)], slots)
                total += dot_tn(placed, held[k, n].reshape(parts * slots, half))
            if k:
                self.going[side][k - 1] = total.astype(low_type)
                self.second[side, k] = self.send(
                    self.going[side].at[k - 1], self.came[side].at[k - 1], peer_on(axis, k)
                )
            else:
                self.kept[side] = total

    def sums(self):
        for side in (0, 1):
            for k in (1, 2, 3):
                self.second[side, k].wait_recv()
        return jnp.concatenate(
            [
                self.kept[side] + sum(self.came[side][n].astype(full) for n in range(3))
                for side in (0, 1)
            ],
            axis=1,
        )

    def end(self):
        for copies in (self.first, self.second):
            for copy in copies.values():
                copy.wait_send()


def home_scratch(parts, slots, rows, half):
    return [pltpu.VMEM((4, 4, parts, slots, half), low_type)] * 2 + [
        pltpu.VMEM((3, rows, half), low_type)
    ] * 4


def by_place(values, axes):
    strides = dict(x=32, core=16, y=4, z=1)
    counts = dict(x=4, core=2, y=4, z=4)
    places = [0]
    for axis in axes:
        places = [p + n * strides[axis] for p in places for n in range(counts[axis])]
    return jnp.concatenate([values[p * 8 : p * 8 + 8] for p in places], axis=0)


def expert_rows(x, grad_full, in_w, down_w, router_w, mine_at, experts):
    half = down_w.shape[1]
    projected = dot(x, in_w)
    gate_part, up = projected[:, :half], projected[:, half:]
    sigmoid = 1.0 / (1.0 + jnp.exp(-gate_part))
    silu = gate_part * sigmoid
    hidden = (silu * up).astype(low_type)
    produced = dot_nt(hidden, down_w).astype(low_type).astype(full)
    logits = dot(x, router_w)
    lane = lax.broadcasted_iota(jnp.int32, logits.shape, 1)
    logits = jnp.where(lane < experts, logits, masked_score)
    shifted = jnp.exp(logits - jnp.max(logits, axis=-1, keepdims=True))
    routing = shifted / jnp.sum(shifted, axis=-1, keepdims=True)
    mine = lane == mine_at
    chosen = jnp.sum(jnp.where(mine, routing, 0.0), axis=-1, keepdims=True)
    gate = chosen.astype(low_type).astype(full)
    slot_grad = (grad_full * gate).astype(low_type)
    gate_grad = jnp.sum(grad_full * produced, axis=-1, keepdims=True)
    logit_grad = (gate_grad * chosen) * (jnp.where(mine, 1.0, 0.0) - routing)
    logit_grad = logit_grad.astype(low_type)
    hidden_grad = dot(slot_grad, down_w)
    gate_back = hidden_grad * up * (sigmoid * (1.0 + gate_part * (1.0 - sigmoid)))
    projected_grad = jnp.concatenate([gate_back, hidden_grad * silu], axis=1).astype(low_type)
    back = dot_nt(projected_grad, in_w) + dot_nt(logit_grad, router_w)
    return produced * gate, back, projected_grad, slot_grad, hidden, logit_grad


def moe_kernel(experts, *refs):
    (att_ref, output_ref, tokens_ref, gains_ref, left_ref, right_ref, grad_ref, held_any, in_any, down_any, weights_any) = refs[:11]
    (mid_ref, made_ref, in_out, down_out, router_out, att_out, mid_grad_ref, low_ref, ffn_ref, home_ref) = refs[11:21]
    (moe_buf, token_bufs, rows_bufs, x_buf, g_buf, p_buf, h_buf, l_buf, y_buf, in_w, down_w, router_w) = refs[21:33]
    (back_bufs, going, came, in_buf, down_buf, in_core, down_core, in_came, down_came, grad_buf) = refs[33:43]
    send_sem, recv_sem, back_send, back_recv, y_sem, local_sem = refs[43:]
    dp, expert, at = place_of()
    x, y, z, c = at["x"], at["y"], at["z"], at["core"]
    tables = left_ref, right_ref
    seats = y, z
    rows, wide = mid_ref.shape
    half = wide // 2
    _, parts, _, _, slots, _ = rows_bufs.shape
    peers = [peer_on(axis, k) for axis, k in PLANE] + dp_peers()
    greet(peers)
    move, send = Mover(local_sem), Sender(send_sem, recv_sem)
    loads = {
        ("g", 0): move(held_any.at[:, :, 0], g_buf),
        ("in", 0): move(in_any.at[0], in_w),
        ("down", 0): move(down_any.at[0], down_w),
        "router": move(weights_any.at[:, pl.ds(KV_HEADS * PACK, EXTRA)], router_w),
    }
    attended = jnp.concatenate([att_ref[g] for g in range(KV_HEADS)], axis=1)
    mid = tokens_ref[...].astype(full) + dot(attended, output_ref[...])
    mid_ref[...] = mid
    inverse = lax.rsqrt(jnp.mean(mid * mid, axis=-1, keepdims=True) + norm_eps)
    moe_buf[...] = (mid * inverse * gains_ref[1:2, :]).astype(low_type)
    meet(peers)
    along = {}
    for k in (1, 2, 3):
        for side, axis in ((0, "y"), (1, "z")):
            piece = moe_buf.at[:, pl.ds(side * half, half)]
            along[side, k] = send(piece, token_bufs.at[side, k - 1], peer_on(axis, k))
    spread = [[] for _ in range(parts)]

    def spread_part(k, j):
        for side, across in ((0, "z"), (1, "y")):
            source, mine = lax.bitwise_xor(seats[side], k), seats[1 - side]
            cols = pl.ds(side * half, half)
            place = (source, z) if side == 0 else (y, source)
            target = x_buf.at[(j, *place, slice(None), cols)]
            for n in (1, 2, 3):
                piece = rows_bufs.at[side, j, k, lax.bitwise_xor(mine, n)]
                spread[j].append(send(piece, target, peer_on(across, n)))
            x_buf[(j, *place, slice(None), cols)] = rows_bufs[side, j, k, mine]

    for k in range(4):
        for side in (0, 1):
            source = lax.bitwise_xor(seats[side], k)
            placed = placed_of(tables[side][source], slots)
            if k:
                along[side, k].wait_recv()
                tokens = token_bufs[side, k - 1]
            else:
                tokens = moe_buf[:, side * half : (side + 1) * half]
            value = dot(placed, tokens).astype(low_type).reshape(4, parts, slots, half)
            for j in range(parts):
                rows_bufs[side, j, k] = value[:, j]
        spread_part(k, 0)
    for k in range(4):
        for j in range(1, parts):
            spread_part(k, j)
    att_out[...] = by_place(flip(attended), ("z", "core", "x", "y")).astype(low_type)
    loads["router"].wait()

    def back_copy(side, j, k, n):
        if side == 0:
            place = (lax.bitwise_xor(y, k), lax.bitwise_xor(z, n))
        else:
            place = (lax.bitwise_xor(y, n), lax.bitwise_xor(z, k))
        number = ((side * parts + j) * 4 + k) * 3 + n - 1
        return pltpu.make_async_remote_copy(
            src_ref=rows_bufs.at[(side, j, *place)],
            dst_ref=back_bufs.at[side, k, n - 1, j],
            send_sem=back_send.at[number],
            recv_sem=back_recv.at[number],
            device_id=peer_on(("z", "y")[side], n),
            device_id_type=MESH,
        )

    def y_copy(slot, there, j):
        return pltpu.make_async_copy(y_buf.at[slot], made_ref.at[there, :, j], y_sem.at[slot])

    def experts_job(j):
        for copy in spread[j]:
            copy.wait()
        for name in ("g", "in", "down"):
            loads[name, j].wait()

        def chunk(turn, _):
            k = lax.rem(turn + 1, 4)
            there = lax.bitwise_xor(y, k)
            count = 4 * slots
            grad_full = g_buf[there].reshape(count, wide).astype(full)
            made, back, p, s, h, l = expert_rows(
                x_buf[j, there].reshape(count, wide),
                grad_full,
                in_w[...],
                down_w[...],
                router_w[...],
                parts * expert + j,
                experts,
            )
            slot = lax.rem(turn, 2)

            @pl.when(turn >= 2)
            def _():
                y_copy(slot, lax.bitwise_xor(y, lax.rem(turn + 3, 4)), j).wait()

            y_buf[slot] = made.astype(low_type).reshape(y_buf.shape[1:])
            y_copy(slot, there, j).start()
            back = back.astype(low_type)
            for side in (0, 1):
                piece = back[:, side * half : (side + 1) * half]
                rows_bufs[side, j, there] = piece.reshape(4, slots, half)
            for n in (1, 2, 3):
                back_copy(0, j, k, n).start()

            @pl.when(k != 0)
            def _():
                for other in range(4):
                    back_copy(1, j, other, k).start()

            p_buf[there] = p
            g_buf[there] = s.reshape(g_buf.shape[1:])
            h_buf[there] = h
            l_buf[there] = l
            return 0

        lax.fori_loop(0, 4, chunk, 0)
        for turn in (2, 3):
            y_copy(turn % 2, lax.bitwise_xor(y, (turn + 1) % 4), j).wait()

    def stacked(values):
        return values.reshape(-1, values.shape[-1])

    def in_job(j):
        for n in range(wide // 256):
            cols = slice(n * 256, (n + 1) * 256)
            value = dot_tn(stacked(x_buf[j, :, :, :, cols]), stacked(p_buf[...])).astype(low_type)
            in_buf[j, n, 0] = value[:128]
            in_buf[j, n, 1] = value[128:]
        core_copies["in", j] = send(in_buf.at[j, :, 1 - c], in_core.at[j], peer_on("core", 1))

    def down_job(j):
        for n in range(wide // 256):
            cols = slice(n * 256, (n + 1) * 256)
            value = dot_tn(stacked(g_buf[:, :, :, cols]), stacked(h_buf[...])).astype(low_type)
            down_buf[j, n, 0] = value[:128]
            down_buf[j, n, 1] = value[128:]
            part = dot_tn(stacked(x_buf[j, :, :, :, cols]), stacked(l_buf[...]))
            router_out[cols, :] = part if j == 0 else router_out[cols, :] + part
        core_copies["down", j] = send(
            down_buf.at[j, :, 1 - c], down_core.at[j], peer_on("core", 1)
        )

    core_copies, x_copies = {}, {}
    buffers = {
        "in": (in_buf, in_core, in_came, in_out),
        "down": (down_buf, down_core, down_came, down_out),
    }

    def across_job(name, j):
        own, core, came_x, _ = buffers[name]
        core_copies[name, j].wait_recv()
        for k in (1, 2, 3):
            there = lax.bitwise_xor(x, k)
            value = own[j, there, c].astype(full) + core[j, there].astype(full)
            own[j, there, c] = value.astype(low_type)
            x_copies[name, j, k] = send(
                own.at[j, there, c], came_x.at[j, k - 1], peer_on("x", k)
            )

    def total_job(name, j):
        own, core, came_x, out = buffers[name]
        value = own[j, x, c].astype(full) + core[j, x].astype(full)
        for k in (1, 2, 3):
            x_copies[name, j, k].wait_recv()
            value += came_x[j, k - 1].astype(full)
        out[j] = value

    second, kept = {}, {}

    def add_job(k):
        for side, axis in ((0, "y"), (1, "z")):
            seat, mine = seats[side], seats[1 - side]
            source = lax.bitwise_xor(seat, k)
            total = jnp.zeros((rows, half), full)
            for n in range(4):
                if n:
                    for j in range(parts):
                        back_copy(side, j, k, n).wait_recv()
                    piece = back_bufs[side, k, n - 1].reshape(parts * slots, half)
                else:
                    place = (source, z) if side == 0 else (y, source)
                    piece = jnp.concatenate(
                        [rows_bufs[(side, j, *place)] for j in range(parts)], axis=0
                    )
                placed = placed_of(tables[side][source, lax.bitwise_xor(mine, n)], slots)
                total += dot_tn(placed, piece)
            if k:
                going[side, k - 1] = total.astype(low_type)
                second[side, k] = send(
                    going.at[side, k - 1], came.at[side, k - 1], peer_on(axis, k)
                )
            else:
                kept[side] = total

    experts_job(0)
    for j in range(1, parts):
        loads["in", j] = move(in_any.at[j], in_w)
        loads["down", j] = move(down_any.at[j], down_w)
        in_job(j - 1)
        down_job(j - 1)
        loads["g", j] = move(held_any.at[:, :, j], g_buf)
        across_job("in", j - 1)
        across_job("down", j - 1)
        experts_job(j)
        in_job(j)
    add_job(1)
    add_job(2)
    across_job("in", parts - 1)
    add_job(3)
    add_job(0)
    down_job(parts - 1)
    across_job("down", parts - 1)
    sums = []
    for side in (0, 1):
        for k in (1, 2, 3):
            second[side, k].wait_recv()
        sums.append(kept[side] + sum(came[side, n].astype(full) for n in range(3)))
    moe_grad = jnp.concatenate(sums, axis=1)
    mid = mid_ref[...]
    inverse = lax.rsqrt(jnp.mean(mid * mid, axis=-1, keepdims=True) + norm_eps)
    scaled = moe_grad * gains_ref[1:2, :]
    shared = jnp.sum(scaled * mid, axis=-1, keepdims=True) * (inverse * inverse * inverse / wide)
    mid_grad = grad_ref[...].astype(full) + (scaled * inverse - mid * shared)
    mid_grad_ref[...] = mid_grad
    low = mid_grad.astype(low_type)
    low_ref[...] = low
    ffn_ref[...] = jnp.sum(mid * inverse * moe_grad, axis=0, keepdims=True)
    third = []
    for k in (1, 2, 3, 4, 5, 6, 7, 0):
        g = lax.bitwise_xor(dp, k)
        piece = dot_nt(low, output_ref[pl.ds(pl.multiple_of(g * PAIR, PAIR), PAIR), :])
        if k:
            grad_buf[g] = piece.astype(low_type)
            third.append(send(grad_buf.at[g], home_ref.at[dp], peers[5 + k]))
        else:
            home_ref[dp] = piece.astype(low_type)
    for j in range(parts):
        total_job("in", j)
        total_job("down", j)
    for copies in (along, second, core_copies, x_copies):
        for copy in copies.values():
            copy.wait_send()
    for side in (0, 1):
        for j in range(parts):
            for k in range(4):
                for n in (1, 2, 3):
                    back_copy(side, j, k, n).wait_send()
    for copy in third:
        copy.wait()


def moe_layer(att, output_proj, tokens, gains, left, right, grad, held, in_w, down_w, weights, experts, number):
    rows, wide = tokens.shape
    _, _, parts, slots, _ = held.shape
    half = wide // 2
    hidden = down_w.shape[2]
    shapes = [
        ((rows, wide), full),
        (held.shape, low_type),
        ((parts, wide // 8, 2 * hidden), full),
        ((parts, wide // 8, hidden), full),
        ((wide, EXTRA), full),
        ((wide, rows), low_type),
        ((rows, wide), full),
        ((rows, wide), low_type),
        ((1, wide), full),
        ((KV_HEADS, rows, PAIR), low_type),
    ]
    scratch = [
        (rows, wide),
        (2, 3, rows, half),
        (2, parts, 4, 4, slots, half),
        (parts, 4, 4, slots, wide),
        (4, 4, slots, wide),
        (4, 4 * slots, 2 * hidden),
        (4, 4 * slots, hidden),
        (4, 4 * slots, EXTRA),
        (2, 4, slots, wide),
        in_w.shape[1:],
        down_w.shape[1:],
        (wide, EXTRA),
        (2, 4, 3, parts, slots, half),
        (2, 3, rows, half),
        (2, 3, rows, half),
        (parts, 4, 2, wide // 8, 2 * hidden),
        (parts, 4, 2, wide // 8, hidden),
        (parts, 4, wide // 8, 2 * hidden),
        (parts, 4, wide // 8, hidden),
        (parts, 3, wide // 8, 2 * hidden),
        (parts, 3, wide // 8, hidden),
        (KV_HEADS, rows, PAIR),
    ]
    copies = 6 + 24 * parts + 8 * parts + 6 + 7
    return pl.pallas_call(
        functools.partial(moe_kernel, experts),
        out_shape=[jax.ShapeDtypeStruct(*s) for s in shapes],
        in_specs=[VMEM] * 7 + [ANY] * 4,
        out_specs=[VMEM, ANY] + [VMEM] * 8,
        scratch_shapes=[
            *[pltpu.VMEM(s, low_type) for s in scratch],
            *[pltpu.SemaphoreType.DMA((copies,))] * 2,
            *[pltpu.SemaphoreType.DMA((24 * parts,))] * 2,
            pltpu.SemaphoreType.DMA((2,)),
            pltpu.SemaphoreType.DMA((3 * parts + 1,)),
        ],
        compiler_params=comm_params(number),
        cost_estimate=cost(120),
        name="moe_layer",
    )(att, output_proj, tokens, gains, left, right, grad, held, in_w, down_w, weights)


def allowed_of(shape, rows, length, i):
    key_at = lax.broadcasted_iota(jnp.int32, shape, 0)
    query_at = lax.broadcasted_iota(jnp.int32, shape, 1) % rows
    return (key_at <= query_at) & (key_at < length - i * rows)


def key_spread(width, wide):
    out = lax.broadcasted_iota(jnp.int32, (wide, width), 0)
    here = lax.broadcasted_iota(jnp.int32, (wide, width), 1)
    return jnp.where(out == (here // 4) * 8 + here % 4, 1.0, 0.0).astype(low_type)


def hand_over(sent, home, send_sem, recv_sem, i):
    dp, expert, _ = place_of()
    k = lax.bitwise_xor(dp, i)
    return pltpu.make_async_remote_copy(
        src_ref=sent.at[i],
        dst_ref=home.at[dp],
        send_sem=send_sem.at[k],
        recv_sem=recv_sem.at[k],
        device_id=(i, expert),
        device_id_type=MESH,
    )


def forward_kernel(
    length_ref, tokens_ref, weights_ref, cos_ref, sin_ref, left_ref, right_ref, grad_ref, third_ref,
    output_ref, rows_ref, normed_rows,  raw_ref, pack_ref, gains_ref, held_ref, att_ref, log_ref, home_ref,
    grad_bufs, rows_a, rows_b, sent, flip_ref, third_buf, send_one, recv_one, send_two, recv_two, send_sem, recv_sem, local_sem, move_sem,
):
    dp, _, at = place_of()
    y, z = at["y"], at["z"]
    peers = dp_peers() + [peer_on(axis, k) for axis, k in PLANE]
    greet(peers)
    third = pltpu.make_async_copy(third_ref, third_buf, local_sem)
    third.start()
    blocks, rows = held_ref.shape[0], held_ref.shape[1]
    wide = tokens_ref.shape[1]
    width = KV_HEADS * HEAD_DIM
    extra = flip(weights_ref[:, KV_HEADS * PACK :])
    gains_ref[0:1, :] = extra[32:33]
    gains_ref[1:2, :] = extra[34:35]
    key_gain = dot(
        jnp.broadcast_to(extra[35:36], (8, wide)).astype(low_type), key_spread(width, wide)
    )[:1]
    for g in range(KV_HEADS):
        pack_ref[g, :, :PAIR] = extra[33:34, g * PAIR : (g + 1) * PAIR]
        pack_ref[g, :, PAIR:] = jnp.concatenate(
            [key_gain[:, g * HEAD_DIM : (g + 1) * HEAD_DIM], jnp.ones((1, HEAD_DIM), full)],
            axis=1,
        )
    meet(peers)
    send = Sender(send_sem, recv_sem)
    half = wide // 2
    along = {}
    for k in (1, 2, 3):
        for side, axis in ((0, "y"), (1, "z")):
            piece = grad_ref.at[:, pl.ds(side * half, half)]
            along[side, k] = send(piece, grad_bufs.at[side, k - 1], peer_on(axis, k))
    values = tokens_ref[...].astype(full)
    inverse = lax.rsqrt(jnp.mean(values * values, axis=-1, keepdims=True) + norm_eps)
    normed = (values * inverse * gains_ref[0:1, :]).astype(low_type)
    query_sum = jnp.zeros((rows, PAIR), full)
    key_sum = jnp.zeros((rows, PAIR), full)
    for g in range(KV_HEADS):
        raw = dot(normed, weights_ref[:, g * PACK : (g + 1) * PACK])
        raw_ref[g] = raw
        query_sum += raw[:, :PAIR] * raw[:, :PAIR]
        key_sum += raw[:, PAIR:] * raw[:, PAIR:]
    is_key = lax.broadcasted_iota(jnp.int32, key_sum.shape, 1) < HEAD_DIM
    query_inv = lax.rsqrt(
        jnp.sum(query_sum, axis=-1, keepdims=True) / (GROUP * width) + norm_eps
    )
    key_inv = lax.rsqrt(
        jnp.sum(jnp.where(is_key, key_sum, 0.0), axis=-1, keepdims=True) / width + norm_eps
    )
    pair_inv = jnp.where(is_key, key_inv, 1.0)
    move = Mover(move_sem)
    handed = []
    for k in (1, 2, 3, 4, 5, 6, 7, 0):
        g = lax.bitwise_xor(dp, k)
        target = sent if k else held_ref
        for part, scale in ((0, query_inv), (1, pair_inv)):
            here = slice(part * PAIR, (part + 1) * PAIR)
            scaled = raw_ref[g, :, here] * scale * pack_ref[g, :, here]
            turned = scaled * cos_ref[:, here] + partner(scaled) * sin_ref[:, here]
            target[g, :, here] = turned.astype(low_type)
        if k:
            handed.append(hand_over(sent, held_ref, send_one, recv_one, g))
            handed[-1].start()
    def tokens_of(side, k):
        if k == 0:
            return grad_ref[:, side * half : (side + 1) * half]
        along[side, k].wait_recv()
        return grad_bufs[side, k - 1]

    spread = spread_slots(
        send, move, (left_ref, right_ref), tokens_of, (rows_a, rows_b), rows_ref
    )
    wide_query = GROUP * rows
    flat = flip(normed)
    normed_rows[0] = flat.astype(low_type)
    normed_rows[1] = by_place(flat, ("y", "core", "z", "x")).astype(low_type)
    third.wait()
    for n in range(4):
        pieces = [
            third_buf[p, m // 4, m % 4, n * 8 : n * 8 + 8, :].astype(full)
            for m in range(8)
            for p in range(4)
        ]
        output_ref[n * 256 : (n + 1) * 256, :] = jnp.concatenate(pieces, axis=0).astype(low_type)

    def step(i, _):
        @pl.when(i != dp)
        def _():
            hand_over(sent, held_ref, send_one, recv_one, i).wait_recv()

        flip_ref[i] = flip(held_ref[i, :, PAIR:]).astype(low_type)
        query = flip(held_ref[i, :, :PAIR]).astype(low_type)
        query = jnp.concatenate([query[:HEAD_DIM], query[HEAD_DIM:]], axis=1)

        def block(j, carry, masked):
            top, total, acc = carry
            key = held_ref[j, :, PAIR : PAIR + HEAD_DIM]
            scores = dot(key, query) * score_scale
            if masked:
                allowed = allowed_of(scores.shape, rows, length_ref[0], i)
                scores = jnp.where(allowed, scores, masked_score)
            new_top = jnp.maximum(top, jnp.max(scores, axis=0, keepdims=True))
            weights = jnp.exp(scores - new_top)
            shrink = jnp.exp(top - new_top)
            total = total * shrink + jnp.sum(weights, axis=0, keepdims=True)
            acc = acc * shrink + dot(flip_ref[j, HEAD_DIM:, :], weights.astype(low_type))
            return new_top, total, acc

        carry = (
            jnp.full((1, wide_query), masked_score, full),
            jnp.zeros((1, wide_query), full),
            jnp.zeros((HEAD_DIM, wide_query), full),
        )
        carry = block(i, carry, True)
        top, total, acc = lax.fori_loop(0, i, lambda j, c: block(j, c, False), carry)
        acc = acc / total
        both = jnp.concatenate([acc[:, :rows], acc[:, rows:]], axis=0)
        att_ref[i] = both.T.astype(low_type)
        log_ref[i] = jnp.broadcast_to(top + jnp.log(total), log_ref.shape[1:])

        @pl.when(i != dp)
        def _():
            hand_over(att_ref, home_ref, send_two, recv_two, i).start()

        @pl.when(i == dp)
        def _():
            home_ref[i] = att_ref[i]

        return 0

    lax.fori_loop(0, blocks, step, 0)
    for copy in handed:
        copy.wait_send()
    for copy in spread:
        copy.wait()
    for copy in along.values():
        copy.wait_send()
    for k in range(1, 8):
        hand_over(att_ref, home_ref, send_two, recv_two, lax.bitwise_xor(dp, k)).wait()


def forward(lengths, tokens, weights, cosine, sine, left, right, grad, third, parts, slots, number):
    rows, wide = tokens.shape
    shapes = [
        ((wide, wide), low_type),
        ((4, 4, parts, slots, wide), low_type),
        ((2, wide, rows), low_type),
        ((KV_HEADS, rows, PACK), full),
        ((KV_HEADS, 1, PACK), full),
        ((8, wide), full),
        ((8, rows, PACK), low_type),
        ((8, rows, PAIR), low_type),
        ((8, 8, GROUP * rows), full),
        ((KV_HEADS, rows, PAIR), low_type),
    ]
    return pl.pallas_call(
        forward_kernel,
        out_shape=[jax.ShapeDtypeStruct(*s) for s in shapes],
        in_specs=[SMEM] + [VMEM] * 7 + [ANY],
        out_specs=[VMEM, ANY] + [VMEM] * (len(shapes) - 2),
        scratch_shapes=[
            pltpu.VMEM((2, 3, rows, wide // 2), low_type),
            pltpu.VMEM((4, 4, parts, slots, wide // 2), low_type),
            pltpu.VMEM((4, 4, parts, slots, wide // 2), low_type),
            pltpu.VMEM((KV_HEADS, rows, PACK), low_type),
            pltpu.VMEM((8, PAIR, rows), low_type),
            pltpu.VMEM(third.shape, low_type),
            *[pltpu.SemaphoreType.DMA((8,))] * 4,
            *[pltpu.SemaphoreType.DMA((30,))] * 2,
            pltpu.SemaphoreType.DMA,
            pltpu.SemaphoreType.DMA((8,)),
        ],
        compiler_params=comm_params(number),
        cost_estimate=cost(45),
        name="forward",
    )(lengths, tokens, weights, cosine, sine, left, right, grad, third)


def backward_kernel(
    length_ref, held_ref, grad_ref, att_ref, log_ref, home_ref, sent, flip_ref, sum_ref, send_sem, recv_sem
):
    dp, _, _ = place_of()
    blocks, rows = held_ref.shape[0], held_ref.shape[1]
    sum_ref[...] = jnp.zeros_like(sum_ref)
    for j in range(blocks):
        flip_ref[j] = flip(held_ref[j, :, PAIR:])[:HEAD_DIM].astype(low_type)
    none = jnp.zeros((rows, HEAD_DIM), low_type)
    key_scale = jnp.where(
        lax.broadcasted_iota(jnp.int32, (rows, PAIR), 1) < HEAD_DIM, score_scale, 1.0
    )

    def heads_beside(values):
        return jnp.concatenate([values[:HEAD_DIM], values[HEAD_DIM:]], axis=1)

    def step(n, _):
        i = blocks - 1 - n
        query_rows = held_ref[i, :, :PAIR]
        grad_rows = grad_ref[i]
        query = heads_beside(flip(query_rows)).astype(low_type)
        grad_full = heads_beside(flip(grad_rows))
        grad = grad_full.astype(low_type)
        inner = jnp.sum(grad_full * heads_beside(flip(att_ref[i])), axis=0, keepdims=True)
        log_total = log_ref[i, :1, :]
        query_side = jnp.concatenate(
            [
                jnp.concatenate([query_rows[:, :HEAD_DIM], none], axis=1),
                jnp.concatenate([query_rows[:, HEAD_DIM:], none], axis=1),
            ],
            axis=0,
        )
        grad_side = jnp.concatenate(
            [
                jnp.concatenate([none, grad_rows[:, :HEAD_DIM]], axis=1),
                jnp.concatenate([none, grad_rows[:, HEAD_DIM:]], axis=1),
            ],
            axis=0,
        )

        def block(j, acc, masked):
            key = held_ref[j, :, PAIR : PAIR + HEAD_DIM]
            value = held_ref[j, :, PAIR + HEAD_DIM :]
            scores = dot(key, query) * score_scale
            soft = jnp.exp(scores - log_total)
            if masked:
                allowed = allowed_of(scores.shape, rows, length_ref[0], i)
                soft = jnp.where(allowed, soft, 0.0)
            soft_grad = dot(value, grad)
            score_grad = (soft * (soft_grad - inner)).astype(low_type)
            sum_ref[j] += dot(score_grad, query_side) + dot(soft.astype(low_type), grad_side)
            return acc + dot(flip_ref[j], score_grad)

        acc = jnp.zeros((HEAD_DIM, GROUP * rows), full)
        acc = block(i, acc, True)
        acc = lax.fori_loop(0, i, lambda j, c: block(j, c, False), acc)
        both = jnp.concatenate([acc[:, :rows], acc[:, rows:]], axis=0) * score_scale
        sent[i, :, :PAIR] = both.T.astype(low_type)
        sent[i, :, PAIR:] = (sum_ref[i] * key_scale).astype(low_type)

        @pl.when(i != dp)
        def _():
            hand_over(sent, home_ref, send_sem, recv_sem, i).start()

        @pl.when(i == dp)
        def _():
            home_ref[i] = sent[i]

        return 0

    lax.fori_loop(0, blocks, step, 0)


def tail_kernel(
    length_ref, held_ref, grad_ref, att_ref, log_ref, pack_ref, gains_ref, left_ref, right_ref, made_ref, *refs
):
    given, refs = refs[:12], refs[12:]
    (output_ref, tokens_ref, *sums), refs = refs[:5], refs[5:]
    here, refs = refs[:12], refs[12:]
    held, going, came, refs = refs[0:2], refs[2:4], refs[4:6], refs[6:]
    (home, sent, flip_ref, sum_ref, low_ref), refs = refs[:5], refs[5:]
    thirds, reduce_scratch, refs = refs[:3], refs[3:21], refs[21:]
    send_one, recv_one, send_two, recv_two, send_three, recv_three, local_sem = refs
    dp, _, _ = place_of()
    peers = dp_peers() + [peer_on(axis, k) for axis, k in PLANE]
    greet(peers)
    move = Mover(local_sem)
    loads = [move(source, target) for source, target in zip(given, here)]
    raw, cos, sin, weights, normed, tokens, mid_grad, router, ffn, att_rows, mid_low, mid = here
    meet(peers)
    homeward = Homeward(
        Sender(send_two, recv_two), move, made_ref, (left_ref, right_ref), held, going, came
    )
    backward_kernel(
        length_ref, held_ref, grad_ref, att_ref, log_ref, home, sent, flip_ref, sum_ref, send_one, recv_one
    )
    for k in (1, 2, 3, 0):
        homeward.add(k)
    for k in range(1, 8):
        hand_over(sent, home, send_one, recv_one, lax.bitwise_xor(dp, k)).wait()
    for load in loads:
        load.wait()
    project_back_kernel(
        home, raw, pack_ref, cos, sin, weights, normed, tokens, gains_ref, mid_grad, router, ffn, att_rows, mid_low,
        tokens_ref, *thirds, low_ref,
    )
    output_ref[...] = (mid[...] + homeward.sums()).astype(low_type)
    homeward.end()
    reduce_kernel(*thirds, *sums, *reduce_scratch, send_three, recv_three)


def tail(lengths, held, grad, att, logs, pack, gains, left, right, made, given, number):
    blocks, rows, _ = held.shape
    _, _, parts, slots, wide = made.shape
    wing = KV_HEADS * PACK // 2
    widths = (EXTRA + wing, wing, wide)

    def each(*shape, kind=low_type):
        return [pltpu.VMEM(shape + (w,), kind) for w in widths]

    return pl.pallas_call(
        tail_kernel,
        out_shape=[
            jax.ShapeDtypeStruct((rows, wide), low_type),
            jax.ShapeDtypeStruct((rows, wide), low_type),
            *[jax.ShapeDtypeStruct((8, w), full) for w in widths],
        ],
        in_specs=[SMEM] + [VMEM] * 8 + [ANY] * 13,
        out_specs=[VMEM] * 5,
        scratch_shapes=[
            *[pltpu.VMEM(v.shape, v.dtype) for v in given],
            *home_scratch(parts, slots, rows, wide // 2),
            pltpu.VMEM((KV_HEADS, rows, PACK), low_type),
            pltpu.VMEM((blocks, rows, PACK), low_type),
            pltpu.VMEM((blocks, HEAD_DIM, rows), low_type),
            pltpu.VMEM((blocks, rows, PAIR), full),
            pltpu.VMEM((rows, KV_HEADS * PACK), low_type),
            *each(4, 2, 4, 32),
            *each(4, 4, 32),
            *each(3, 4, 32),
            *each(3, 32),
            *each(3, 4, 32),
            *each(4, 8, kind=full),
            *each(3, 8, kind=full),
            *[pltpu.SemaphoreType.DMA((8,))] * 2,
            *[pltpu.SemaphoreType.DMA((30,))] * 2,
            *[pltpu.SemaphoreType.DMA((39,))] * 2,
            pltpu.SemaphoreType.DMA((20,)),
        ],
        compiler_params=comm_params(number),
        cost_estimate=cost(90),
        name="tail",
    )(
        lengths, held, grad, att, logs, pack, gains, left, right,
        made, *given,
    )


def finish_kernel(
    left_ref, right_ref, third_ref, query_ref, key_ref, value_ref, out_proj_ref, router_ref, attn_ref, ffn_ref, query_gain_ref, key_gain_ref,
):
    out_proj_ref[...] = third_ref[...]
    for g in range(KV_HEADS):
        if g < KV_HEADS // 2:
            piece = left_ref[:, EXTRA + g * PACK : EXTRA + (g + 1) * PACK]
        else:
            piece = right_ref[:, (g - KV_HEADS // 2) * PACK : (g + 1 - KV_HEADS // 2) * PACK]
        head = slice(g * HEAD_DIM, (g + 1) * HEAD_DIM)
        query_ref[:, g * PAIR : (g + 1) * PAIR] = piece[:, :PAIR]
        key_ref[:, head] = piece[:, PAIR : PAIR + HEAD_DIM]
        value_ref[:, head] = piece[:, PAIR + HEAD_DIM :]
    extra = left_ref[:, :EXTRA]
    experts = router_ref.shape[1]
    router_ref[...] = extra[:, :experts]
    rows = extra.shape[0]
    lane = lax.broadcasted_iota(jnp.int32, (rows, rows), 1)
    row = lax.broadcasted_iota(jnp.int32, (rows, rows), 0)
    for n, ref in enumerate((attn_ref, query_gain_ref, ffn_ref, key_gain_ref)):
        column = jnp.broadcast_to(extra[:, experts + n : experts + n + 1], (rows, rows))
        flat = jnp.sum(jnp.where(lane == row, column, 0.0), axis=0, keepdims=True)
        ref[...] = flat[:, : ref.shape[1]]


def project_back_kernel(
    back_ref,
    raw_ref,
    pack_ref,
    cos_ref,
    sin_ref,
    weights_ref,
    normed_ref,
    tokens_ref,
    gain_ref,
    mid_grad_ref,
    router_ref,
    ffn_ref,
    att_ref,
    mid_low_ref,
    out_ref,
    first_ref,
    second_ref,
    third_ref,
    low_ref,
):
    rows = tokens_ref.shape[0]
    width = KV_HEADS * HEAD_DIM
    lane = lax.broadcasted_iota(jnp.int32, (rows, PAIR), 1)
    is_key = lane < HEAD_DIM
    sums = [[jnp.zeros((rows, PAIR), full) for _ in range(2)] for _ in range(2)]

    def here_of(part):
        return slice(part * PAIR, (part + 1) * PAIR)

    def unturned(g, part):
        here = here_of(part)
        grad = back_ref[g, :, here].astype(full)
        return grad * cos_ref[:, here] - partner(grad) * sin_ref[:, here]

    def columns(g, part):
        return slice(g * PACK + part * PAIR, g * PACK + (part + 1) * PAIR)

    for g in range(KV_HEADS):
        for part in range(2):
            raw = raw_ref[g, :, here_of(part)]
            sums[part][0] += raw * raw
            sums[part][1] += raw * unturned(g, part) * pack_ref[g, :, here_of(part)]
    mean_of = [GROUP * width, width]
    inverses, shares = [], []
    for part in range(2):
        square, cross = sums[part]
        if part == 1:
            square, cross = jnp.where(is_key, square, 0.0), jnp.where(is_key, cross, 0.0)
        inverse = lax.rsqrt(
            jnp.sum(square, axis=-1, keepdims=True) / mean_of[part] + norm_eps
        )
        share = jnp.sum(cross, axis=-1, keepdims=True) * (
            inverse * inverse * inverse / mean_of[part]
        )
        if part == 1:
            inverse = jnp.where(is_key, inverse, 1.0)
            share = jnp.where(is_key, share, 0.0)
        inverses.append(inverse)
        shares.append(share)
    gains = [[], []]
    for g in range(KV_HEADS):
        for part in range(2):
            raw = raw_ref[g, :, here_of(part)]
            grad = unturned(g, part)
            gains[part].append(
                jnp.sum(raw * inverses[part] * grad, axis=0, keepdims=True)
            )
            result = grad * pack_ref[g, :, here_of(part)] * inverses[part] - raw * shares[part]
            low_ref[:, columns(g, part)] = result.astype(low_type)
    normed_grad = dot_nt(low_ref[...], weights_ref[:, : KV_HEADS * PACK])
    values = tokens_ref[...].astype(full)
    wide = values.shape[1]
    inverse = lax.rsqrt(jnp.mean(values * values, axis=-1, keepdims=True) + norm_eps)
    scaled = normed_grad * gain_ref[0:1, :]
    share = jnp.sum(scaled * values, axis=-1, keepdims=True) * (
        inverse * inverse * inverse / wide
    )
    out_ref[...] = (mid_grad_ref[...] + (scaled * inverse - values * share)).astype(low_type)
    attn_grad = jnp.sum(values * inverse * normed_grad, axis=0, keepdims=True)
    query_grad = jnp.concatenate(gains[0], axis=1)
    key_grad = jnp.concatenate(
        [jnp.concatenate(
            [gains[1][2 * g][:, :HEAD_DIM], gains[1][2 * g + 1][:, :HEAD_DIM]], axis=1
        ) for g in range(KV_HEADS // 2)],
        axis=1,
    )
    key_wide = dot_nt(
        jnp.broadcast_to(key_grad, (8, width)).astype(low_type), key_spread(width, wide)
    )[:1]
    extra = jnp.concatenate(
        [
            jnp.zeros((32, wide), full),
            attn_grad,
            query_grad,
            ffn_ref[...],
            key_wide,
            jnp.zeros((EXTRA - 36, wide), full),
        ],
        axis=0,
    )
    places = first_ref.shape[:-1]
    first_ref[..., :EXTRA] = (
        (extra.T + router_ref[...]).astype(low_type).reshape(places + (EXTRA,))
    )
    wing = KV_HEADS * PACK // 2

    def put(ref, start, value):
        ref[..., start : start + 256] = value.astype(low_type).reshape(places + (256,))

    for n in range(0, wing, 256):
        put(first_ref, EXTRA + n, dot(normed_ref[0], low_ref[:, n : n + 256]))
        put(second_ref, n, dot(normed_ref[1], low_ref[:, wing + n : wing + n + 256]))
        put(third_ref, n, dot(att_ref[...], mid_low_ref[:, n : n + 256]))


def on_device(
    tokens_in,
    lengths,
    routes,
    w_query,
    w_key,
    w_value,
    w_output,
    w_router,
    attn_gain,
    ffn_gain,
    query_gain,
    key_gain,
    expert_in,
    expert_down,
    out_grad,
):
    rows, wide = tokens_in.shape[1], tokens_in.shape[2]
    experts = w_router.shape[1]
    parts = expert_in.shape[0]
    owners = experts // parts
    slots = 5 * rows * routes.shape[2] // (4 * experts)
    tokens = tokens_in[0]
    grad_out = out_grad[0]

    place = lax.axis_index("dp") * rows + jnp.arange(rows)
    valid = (place < lengths[0]).astype(jnp.int32)
    ids = jnp.arange(experts)
    chosen = (
        jnp.sum((routes[0][:, :, None] == ids[None, None, :]).astype(jnp.int32), axis=1)
        * valid[:, None]
    )
    earlier = jnp.cumsum(chosen, axis=0) - chosen
    slot_of = jnp.where(chosen == 1, earlier, -1).T.astype(full)

    lane = jnp.arange(PACK)
    frequency = rope_base ** (
        -2.0 * (lane % (HEAD_DIM // 2)).astype(full) / HEAD_DIM
    )
    angles = place.astype(full)[:, None] * frequency[None, :]
    turning = (lane < PAIR + HEAD_DIM)[None, :]
    cosine = jnp.where(turning, jnp.cos(angles), 1.0)
    sign = jnp.where(lane % HEAD_DIM < HEAD_DIM // 2, -1.0, 1.0)
    sine = jnp.where(turning, jnp.sin(angles) * sign, 0.0)

    gains = jnp.concatenate([attn_gain, query_gain, ffn_gain, key_gain])
    gains = jnp.pad(gains, (0, EXTRA - gains.shape[0]))[None]
    slot_a = slot_of.reshape(4, 4, parts, rows)
    slot_b = slot_a.transpose(1, 0, 2, 3)
    weights, third, left, right = gather_dense(
        w_query, w_key, w_value, w_router, gains, slot_a, slot_b, w_output, 1
    )
    output_proj, grad_held, normed_rows, raw, pack_row, gain_rows, held, att, logs, att_home = forward(
        lengths, tokens, weights, cosine, sine, left, right, grad_out, third, parts, slots, 2
    )
    mid, made, in_grad, down_grad, router_grad, att_rows, mid_grad, mid_low, ffn_grad, att_grad = moe_layer(
        att_home, output_proj, tokens, gain_rows, left, right, grad_out, grad_held, expert_in, expert_down, weights, experts, 3
    )
    output, grad_tokens, *sums = tail(
        lengths, held, att_grad, att, logs, pack_row, gain_rows, left, right, made,
        (raw, cosine, sine, weights, normed_rows, tokens, mid_grad, router_grad, ffn_grad, att_rows, mid_low, mid), 4,
    )
    shapes = [
        (w_query.shape, full),
        (w_key.shape, full),
        (w_value.shape, full),
        (w_output.shape, full),
        (w_router.shape, full),
        ((1, attn_gain.shape[0]), full),
        ((1, ffn_gain.shape[0]), full),
        ((1, query_gain.shape[0]), full),
        ((1, key_gain.shape[0]), full),
    ]
    results = pl.pallas_call(
        finish_kernel,
        out_shape=[jax.ShapeDtypeStruct(*s) for s in shapes],
        in_specs=[VMEM] * 3,
        out_specs=[VMEM] * len(shapes),
        name="finish",
        **params(2),
    )(*sums)
    return (
        output[None],
        grad_tokens[None],
        *results[:5],
        *[row[0] for row in results[5:]],
        in_grad,
        down_grad,
    )


def solution(mesh):
    in_specs = (
        P("expert", "dp", None),
        P("expert"),
        P("expert", "dp", None),
        P(("dp", "expert"), None),
        P(("dp", "expert"), None),
        P(("dp", "expert"), None),
        P(("dp", "expert"), None),
        P(("dp", "expert"), None),
        P(("dp", "expert")),
        P(("dp", "expert")),
        P(("dp", "expert")),
        P(("dp", "expert")),
        P("expert", None, None),
        P("expert", None, None),
        P("expert", "dp", None),
    )
    out_specs = (
        P("expert", "dp", None),
        P("expert", "dp", None),
        P(("dp", "expert"), None),
        P(("dp", "expert"), None),
        P(("dp", "expert"), None),
        P(("dp", "expert"), None),
        P(("dp", "expert"), None),
        P(("dp", "expert")),
        P(("dp", "expert")),
        P(("dp", "expert")),
        P(("dp", "expert")),
        P("expert", "dp", None),
        P("expert", "dp", None),
    )
    return jax.shard_map(
        on_device, mesh=mesh, in_specs=in_specs, out_specs=out_specs, check_vma=False
    )
```

```python
import functools

import jax
import jax.numpy as jnp
from jax import lax
from jax.experimental import pallas as pl
from jax.experimental.pallas import tpu as pltpu
from jax.sharding import PartitionSpec as P

HEADS = 16
HEAD_DIM = 64
KV_HEADS = 8
GROUP = HEADS // KV_HEADS
PAIR = GROUP * HEAD_DIM
PACK = PAIR + 2 * HEAD_DIM
EXTRA = 128
LEFT = 5 * PACK

norm_eps = 1e-06
rope_base = 10000.0
masked_score = -1e30
score_scale = HEAD_DIM ** (-0.5)
low_type = jnp.bfloat16
full = jnp.float32

VMEM = pl.BlockSpec(memory_space=pltpu.VMEM)
SMEM = pl.BlockSpec(memory_space=pltpu.SMEM)
LIMIT = 62 * 1024 * 1024


def dot(left, right):
    return jnp.dot(left, right, preferred_element_type=full)


def dot_nt(left, right):
    return lax.dot_general(left, right, (((1,), (1,)), ((), ())), preferred_element_type=full)


def dot_tn(left, right):
    return lax.dot_general(left, right, (((0,), (0,)), ((), ())), preferred_element_type=full)


def partner(values):
    lane = lax.broadcasted_iota(jnp.int32, values.shape, 1)
    half = HEAD_DIM // 2
    return jnp.where(
        lane % HEAD_DIM < half, pltpu.roll(values, 128 - half, 1), pltpu.roll(values, half, 1)
    )


def flip(values):
    return values.astype(full).T


def cost(microseconds):
    return pl.CostEstimate(
        flops=int(microseconds * 1.15e9), bytes_accessed=1 << 20, transcendentals=0
    )


def params(microseconds):
    return dict(
        compiler_params=pltpu.CompilerParams(vmem_limit_bytes=LIMIT),
        cost_estimate=cost(microseconds),
    )


MESH = pl.DeviceIdType.MESH
ANY = pl.BlockSpec(memory_space=pl.ANY)


def comm_params(number):
    return pltpu.CompilerParams(
        collective_id=number, has_side_effects=True, vmem_limit_bytes=LIMIT
    )


def place_of():
    dp, expert = lax.axis_index("dp"), lax.axis_index("expert")
    return dp, expert, dict(x=dp // 2, core=dp % 2, y=expert // 4, z=expert % 4)


def peer_on(axis, step):
    dp, expert, _ = place_of()
    if axis == "core":
        return lax.bitwise_xor(dp, 1), expert
    if axis == "x":
        return lax.bitwise_xor(dp, 2 * step), expert
    if axis == "y":
        return dp, lax.bitwise_xor(expert, 4 * step)
    return dp, lax.bitwise_xor(expert, step)


def greet(peers):
    barrier = pltpu.get_barrier_semaphore()
    for device in peers:
        pl.semaphore_signal(barrier, inc=1, device_id=device, device_id_type=MESH)


def meet(peers):
    pl.semaphore_wait(pltpu.get_barrier_semaphore(), len(peers))


def dp_peers():
    dp, expert, _ = place_of()
    return [(lax.bitwise_xor(dp, k), expert) for k in range(1, 8)]


class Mover:
    def __init__(self, sems):
        self.sems, self.count = sems, 0

    def __call__(self, source, target):
        copy = pltpu.make_async_copy(source, target, self.sems.at[self.count])
        self.count += 1
        copy.start()
        return copy


class Sender:
    def __init__(self, send_sem, recv_sem):
        self.send_sem, self.recv_sem, self.count = send_sem, recv_sem, 0

    def __call__(self, source, target, device):
        copy = pltpu.make_async_remote_copy(
            src_ref=source,
            dst_ref=target,
            send_sem=self.send_sem.at[self.count],
            recv_sem=self.recv_sem.at[self.count],
            device_id=device,
            device_id_type=MESH,
        )
        self.count += 1
        copy.start()
        return copy


AXES = ("x", "y", "z")
CUBE = [("core", 1)] + [(axis, k) for axis in AXES for k in (1, 2, 3)]


def placed_rows(slot_row, slots):
    rows = slot_row.shape[1]
    slot = lax.broadcasted_iota(jnp.int32, (slots, rows), 0).astype(full)
    return jnp.where(slot == slot_row, 1.0, 0.0).astype(low_type)


def placed_of(table, slots):
    table = table.reshape(-1, table.shape[-1])
    return jnp.concatenate(
        [placed_rows(table[e : e + 1], slots) for e in range(table.shape[0])], axis=0
    )


class Reduce:
    ORDERS = (("x", "y", "z"), ("y", "z", "x"), ("z", "x", "y"))

    def __init__(self, given, scratch, send_sem, recv_sem):
        _, _, self.at = place_of()
        self.given = given
        self.core, self.half, self.row, self.going, self.total, self.last = (
            scratch[n : n + 3] for n in range(0, 18, 3)
        )
        self.send = Sender(send_sem, recv_sem)
        self.copies = {}

    def seat(self, n, axis, k):
        return lax.bitwise_xor(self.at[self.ORDERS[n][axis]], k)

    def peer(self, n, axis, k):
        return peer_on(self.ORDERS[n][axis], k)

    def cores(self, n):
        for k in (1, 2, 3, 0):
            a = self.seat(n, 0, k)
            piece = self.given[n].at[a, 1 - self.at["core"]]
            self.copies[n, 0, k] = self.send(piece, self.core[n].at[a], peer_on("core", 1))

    def pair(self, n, *place):
        a, *rest = place
        own, other = self.given[n][(a, self.at["core"], *rest)], self.core[n][place]
        return own.astype(full) + other.astype(full)

    def first(self, n):
        for k in (1, 2, 3):
            self.copies[n, 0, k].wait_recv()
            self.going[n][k - 1] = self.pair(n, self.seat(n, 0, k)).astype(low_type)
            self.copies[n, 1, k] = self.send(
                self.going[n].at[k - 1], self.half[n].at[k - 1], self.peer(n, 0, k)
            )

    def second(self, n):
        self.copies[n, 0, 0].wait_recv()
        for k in (1, 2, 3):
            self.copies[n, 1, k].wait()
        for k in (1, 2, 3, 0):
            b = self.seat(n, 1, k)
            value = self.pair(n, self.seat(n, 0, 0), b)
            for m in range(3):
                value += self.half[n][m, b].astype(full)
            if k:
                self.going[n][k - 1, 0] = value.astype(low_type)
                self.copies[n, 2, k] = self.send(
                    self.going[n].at[k - 1, 0], self.row[n].at[k - 1], self.peer(n, 1, k)
                )
            else:
                self.total[n][...] = value.reshape(self.total[n].shape)

    def third(self, n):
        for k in (1, 2, 3):
            self.copies[n, 2, k].wait()
        value = self.total[n][...].reshape(self.row[n].shape[1:])
        for m in range(3):
            value += self.row[n][m].astype(full)
        self.total[n][...] = value.reshape(self.total[n].shape)
        for k in (1, 2, 3):
            d = self.seat(n, 2, k)
            self.copies[n, 3, k] = self.send(
                self.total[n].at[d], self.last[n].at[k - 1], self.peer(n, 2, k)
            )

    def finish(self, n):
        for k in (1, 2, 3):
            self.copies[n, 3, k].wait()
        for k in range(4):
            self.copies[n, 0, k].wait_send()
        last = self.last[n]
        return self.total[n][self.seat(n, 2, 0)] + last[0] + last[1] + last[2]


PLANE = [(axis, k) for axis in ("y", "z") for k in (1, 2, 3)]


def spread_slots(send, move, tables, tokens_of, rows_bufs, out_ref):
    _, _, at = place_of()
    y, z = at["y"], at["z"]
    _, _, _, slots, half = rows_bufs[0].shape
    copies = []
    for k in range(4):
        for side, (rows, table, seat) in enumerate(zip(rows_bufs, tables, (y, z))):
            source = lax.bitwise_xor(seat, k)
            placed = placed_of(table[source], slots)
            rows[k] = dot(placed, tokens_of(side, k)).astype(low_type).reshape(rows.shape[1:])
            if side == 0:
                target = out_ref.at[source, z, :, :, pl.ds(0, half)]
            else:
                target = out_ref.at[y, source, :, :, pl.ds(half, half)]
            across, mine = ("z", z) if side == 0 else ("y", y)
            for n in (1, 2, 3):
                piece = rows.at[k, lax.bitwise_xor(mine, n)]
                copies.append(send(piece, target, peer_on(across, n)))
            copies.append(move(rows.at[k, mine], target))
    return copies


class Homeward:
    def __init__(self, send, move, back_ref, tables, held, going, came):
        _, _, at = place_of()
        self.seats = at["y"], at["z"]
        self.send, self.tables, self.held, self.going, self.came = send, tables, held, going, came
        self.first, self.local, self.second, self.kept = {}, {}, {}, {}
        y, z = self.seats
        half = held[0].shape[-1]
        sides = (pl.ds(0, half), pl.ds(half, half))
        for k in (1, 2, 3, 0):
            to_y, to_z = lax.bitwise_xor(y, k), lax.bitwise_xor(z, k)
            for n in (1, 2, 3):
                piece = back_ref.at[to_y, lax.bitwise_xor(z, n), :, :, sides[0]]
                self.first[0, k, n] = send(piece, held[0].at[k, n], peer_on("z", n))
                piece = back_ref.at[lax.bitwise_xor(y, n), to_z, :, :, sides[1]]
                self.first[1, k, n] = send(piece, held[1].at[k, n], peer_on("y", n))
            self.local[0, k] = move(back_ref.at[to_y, z, :, :, sides[0]], held[0].at[k, 0])
            self.local[1, k] = move(back_ref.at[y, to_z, :, :, sides[1]], held[1].at[k, 0])

    def add(self, k):
        for side, axis in ((0, "y"), (1, "z")):
            held, table = self.held[side], self.tables[side]
            seat, mine = self.seats[side], self.seats[1 - side]
            _, _, parts, slots, half = held.shape
            for n in (1, 2, 3):
                self.first[side, k, n].wait_recv()
            self.local[side, k].wait()
            source = lax.bitwise_xor(seat, k)
            total = jnp.zeros((table.shape[-1], half), full)
            for n in range(4):
                placed = placed_of(table[source, lax.bitwise_xor(mine, n)], slots)
                total += dot_tn(placed, held[k, n].reshape(parts * slots, half))
            if k:
                self.going[side][k - 1] = total.astype(low_type)
                self.second[side, k] = self.send(
                    self.going[side].at[k - 1], self.came[side].at[k - 1], peer_on(axis, k)
                )
            else:
                self.kept[side] = total

    def sums(self):
        for side in (0, 1):
            for k in (1, 2, 3):
                self.second[side, k].wait_recv()
        return jnp.concatenate(
            [
                self.kept[side] + sum(self.came[side][n].astype(full) for n in range(3))
                for side in (0, 1)
            ],
            axis=1,
        )

    def end(self):
        for copies in (self.first, self.second):
            for copy in copies.values():
                copy.wait_send()


def home_scratch(parts, slots, rows, half):
    return [pltpu.VMEM((4, 4, parts, slots, half), low_type)] * 2 + [
        pltpu.VMEM((3, rows, half), low_type)
    ] * 4


def by_place(values, axes):
    strides = dict(x=32, core=16, y=4, z=1)
    counts = dict(x=4, core=2, y=4, z=4)
    places = [0]
    for axis in axes:
        places = [p + n * strides[axis] for p in places for n in range(counts[axis])]
    return jnp.concatenate([values[p * 8 : p * 8 + 8] for p in places], axis=0)


def expert_rows(x, grad, in_w, down_w, router_w, mine_at, experts):
    half = down_w.shape[1]
    projected, logits, hidden_grad = dot(x, in_w), dot(x, router_w), dot(grad, down_w)
    gate_part, up = projected[:, :half], projected[:, half:]
    sigmoid = 1.0 / (1.0 + jnp.exp(-gate_part))
    silu = gate_part * sigmoid
    hidden = (silu * up).astype(low_type).astype(full)
    lane = lax.broadcasted_iota(jnp.int32, logits.shape, 1)
    logits = jnp.where(lane < experts, logits, masked_score)
    shifted = jnp.exp(logits - jnp.max(logits, axis=-1, keepdims=True))
    routing = shifted / jnp.sum(shifted, axis=-1, keepdims=True)
    mine = lane == mine_at
    chosen = jnp.sum(jnp.where(mine, routing, 0.0), axis=-1, keepdims=True)
    gate = chosen.astype(low_type).astype(full)
    gate_grad = jnp.sum(hidden * hidden_grad, axis=-1, keepdims=True)
    logit_grad = (gate_grad * chosen) * (jnp.where(mine, 1.0, 0.0) - routing)
    logit_grad = logit_grad.astype(low_type)
    hidden_grad = hidden_grad * gate
    gate_back = hidden_grad * up * (sigmoid * (1.0 + gate_part * (1.0 - sigmoid)))
    projected_grad = jnp.concatenate(
        [gate_back.astype(low_type), (hidden_grad * silu).astype(low_type)], axis=1
    )
    hidden = (hidden * gate).astype(low_type)
    made = dot_nt(hidden, down_w)
    back = dot_nt(projected_grad, in_w) + dot_nt(logit_grad, router_w)
    return made, back, projected_grad, hidden, logit_grad


def moe_kernel(experts, *refs):
    (att_ref, output_ref, tokens_ref, gains_ref, left_ref, right_ref, grad_ref, held_any, in_any, down_any, weights_any) = refs[:11]
    (mid_ref, made_ref, in_out, down_out, router_out, att_out, mid_grad_ref, low_ref, ffn_ref, home_ref) = refs[11:21]
    (moe_buf, token_bufs, rows_bufs, x_buf, g_buf, p_buf, h_buf, l_buf, y_buf, in_w, down_w, router_w) = refs[21:33]
    (back_bufs, going, came, in_buf, down_buf, in_core, down_core, in_came, down_came, grad_buf) = refs[33:43]
    send_sem, recv_sem, back_send, back_recv, y_sem, local_sem = refs[43:]
    dp, expert, at = place_of()
    x, y, z, c = at["x"], at["y"], at["z"], at["core"]
    tables = left_ref, right_ref
    seats = y, z
    rows, wide = mid_ref.shape
    half = wide // 2
    _, parts, _, _, slots, _ = rows_bufs.shape
    peers = [peer_on(axis, k) for axis, k in PLANE] + dp_peers()
    greet(peers)
    move, send = Mover(local_sem), Sender(send_sem, recv_sem)
    loads = {
        ("g", 0): move(held_any.at[:, :, 0], g_buf),
        ("in", 0): move(in_any.at[0], in_w),
        ("down", 0): move(down_any.at[0], down_w),
        "router": move(weights_any.at[:, pl.ds(KV_HEADS * PACK, EXTRA)], router_w),
    }
    attended = jnp.concatenate([att_ref[g] for g in range(KV_HEADS)], axis=1)
    mid = tokens_ref[...].astype(full) + dot(attended, output_ref[...])
    mid_ref[...] = mid
    inverse = lax.rsqrt(jnp.mean(mid * mid, axis=-1, keepdims=True) + norm_eps)
    moe_buf[...] = (mid * inverse * gains_ref[1:2, :]).astype(low_type)
    meet(peers)
    along = {}
    for k in (1, 2, 3):
        for side, axis in ((0, "y"), (1, "z")):
            piece = moe_buf.at[:, pl.ds(side * half, half)]
            along[side, k] = send(piece, token_bufs.at[side, k - 1], peer_on(axis, k))
    spread = [[] for _ in range(parts)]

    def spread_part(k, j):
        for side, across in ((0, "z"), (1, "y")):
            source, mine = lax.bitwise_xor(seats[side], k), seats[1 - side]
            cols = pl.ds(side * half, half)
            place = (source, z) if side == 0 else (y, source)
            target = x_buf.at[(j, *place, slice(None), cols)]
            for n in (1, 2, 3):
                piece = rows_bufs.at[side, j, k, lax.bitwise_xor(mine, n)]
                spread[j].append(send(piece, target, peer_on(across, n)))
            x_buf[(j, *place, slice(None), cols)] = rows_bufs[side, j, k, mine]

    for k in range(4):
        for side in (0, 1):
            source = lax.bitwise_xor(seats[side], k)
            placed = placed_of(tables[side][source], slots)
            if k:
                along[side, k].wait_recv()
                tokens = token_bufs[side, k - 1]
            else:
                tokens = moe_buf[:, side * half : (side + 1) * half]
            value = dot(placed, tokens).astype(low_type).reshape(4, parts, slots, half)
            for j in range(parts):
                rows_bufs[side, j, k] = value[:, j]
        spread_part(k, 0)
    for k in range(4):
        for j in range(1, parts):
            spread_part(k, j)
    att_out[...] = by_place(flip(attended), ("z", "core", "x", "y")).astype(low_type)
    loads["router"].wait()

    def back_copy(side, j, k, n):
        if side == 0:
            place = (lax.bitwise_xor(y, k), lax.bitwise_xor(z, n))
        else:
            place = (lax.bitwise_xor(y, n), lax.bitwise_xor(z, k))
        number = ((side * parts + j) * 4 + k) * 3 + n - 1
        return pltpu.make_async_remote_copy(
            src_ref=rows_bufs.at[(side, j, *place)],
            dst_ref=back_bufs.at[side, k, n - 1, j],
            send_sem=back_send.at[number],
            recv_sem=back_recv.at[number],
            device_id=peer_on(("z", "y")[side], n),
            device_id_type=MESH,
        )

    def y_copy(slot, there, j):
        return pltpu.make_async_copy(y_buf.at[slot], made_ref.at[there, :, j], y_sem.at[slot])

    def experts_job(j):
        for copy in spread[j]:
            copy.wait()
        for name in ("g", "in", "down"):
            loads[name, j].wait()

        for turn in range(4):
            k = (turn + 1) % 4
            there = lax.bitwise_xor(y, k)
            count = 4 * slots
            made, back, p, h, l = expert_rows(
                x_buf[j, there].reshape(count, wide),
                g_buf[there].reshape(count, wide),
                in_w[...],
                down_w[...],
                router_w[...],
                parts * expert + j,
                experts,
            )
            slot = turn % 2
            if turn >= 2:
                y_copy(slot, lax.bitwise_xor(y, (turn - 1) % 4), j).wait()
            y_buf[slot] = made.astype(low_type).reshape(y_buf.shape[1:])
            y_copy(slot, there, j).start()
            back = back.astype(low_type)
            for side in (0, 1):
                piece = back[:, side * half : (side + 1) * half]
                rows_bufs[side, j, there] = piece.reshape(4, slots, half)
            for n in (1, 2, 3):
                back_copy(0, j, k, n).start()
            if k:
                for other in range(4):
                    back_copy(1, j, other, k).start()
            p_buf[there] = p
            h_buf[there] = h
            l_buf[there] = l
        for turn in (2, 3):
            y_copy(turn % 2, lax.bitwise_xor(y, (turn + 1) % 4), j).wait()

    def stacked(values):
        return values.reshape(-1, values.shape[-1])

    def in_job(j):
        for n in range(wide // 256):
            cols = slice(n * 256, (n + 1) * 256)
            value = dot_tn(stacked(x_buf[j, :, :, :, cols]), stacked(p_buf[...])).astype(low_type)
            in_buf[j, n, 0] = value[:128]
            in_buf[j, n, 1] = value[128:]
        core_copies["in", j] = send(in_buf.at[j, :, 1 - c], in_core.at[j], peer_on("core", 1))

    def down_job(j):
        for n in range(wide // 256):
            cols = slice(n * 256, (n + 1) * 256)
            value = dot_tn(stacked(g_buf[:, :, :, cols]), stacked(h_buf[...])).astype(low_type)
            down_buf[j, n, 0] = value[:128]
            down_buf[j, n, 1] = value[128:]
            part = dot_tn(stacked(x_buf[j, :, :, :, cols]), stacked(l_buf[...]))
            router_out[cols, :] = part if j == 0 else router_out[cols, :] + part
        core_copies["down", j] = send(
            down_buf.at[j, :, 1 - c], down_core.at[j], peer_on("core", 1)
        )

    core_copies, x_copies = {}, {}
    buffers = {
        "in": (in_buf, in_core, in_came, in_out),
        "down": (down_buf, down_core, down_came, down_out),
    }

    def across_job(name, j):
        own, core, came_x, _ = buffers[name]
        core_copies[name, j].wait_recv()
        for k in (1, 2, 3):
            there = lax.bitwise_xor(x, k)
            value = own[j, there, c].astype(full) + core[j, there].astype(full)
            own[j, there, c] = value.astype(low_type)
            x_copies[name, j, k] = send(
                own.at[j, there, c], came_x.at[j, k - 1], peer_on("x", k)
            )

    def total_job(name, j):
        own, core, came_x, out = buffers[name]
        value = own[j, x, c].astype(full) + core[j, x].astype(full)
        for k in (1, 2, 3):
            x_copies[name, j, k].wait_recv()
            value += came_x[j, k - 1].astype(full)
        out[j] = value

    second, kept = {}, {}

    def add_job(k):
        for side, axis in ((0, "y"), (1, "z")):
            seat, mine = seats[side], seats[1 - side]
            source = lax.bitwise_xor(seat, k)
            total = jnp.zeros((rows, half), full)
            for n in range(4):
                if n:
                    for j in range(parts):
                        back_copy(side, j, k, n).wait_recv()
                    piece = back_bufs[side, k, n - 1].reshape(parts * slots, half)
                else:
                    place = (source, z) if side == 0 else (y, source)
                    piece = jnp.concatenate(
                        [rows_bufs[(side, j, *place)] for j in range(parts)], axis=0
                    )
                placed = placed_of(tables[side][source, lax.bitwise_xor(mine, n)], slots)
                total += dot_tn(placed, piece)
            if k:
                going[side, k - 1] = total.astype(low_type)
                second[side, k] = send(
                    going.at[side, k - 1], came.at[side, k - 1], peer_on(axis, k)
                )
            else:
                kept[side] = total

    experts_job(0)
    for j in range(1, parts):
        loads["in", j] = move(in_any.at[j], in_w)
        loads["down", j] = move(down_any.at[j], down_w)
        in_job(j - 1)
        down_job(j - 1)
        loads["g", j] = move(held_any.at[:, :, j], g_buf)
        across_job("in", j - 1)
        across_job("down", j - 1)
        experts_job(j)
        in_job(j)
    add_job(1)
    add_job(2)
    across_job("in", parts - 1)
    add_job(3)
    add_job(0)
    down_job(parts - 1)
    across_job("down", parts - 1)
    sums = []
    for side in (0, 1):
        for k in (1, 2, 3):
            second[side, k].wait_recv()
        sums.append(kept[side] + sum(came[side, n].astype(full) for n in range(3)))
    moe_grad = jnp.concatenate(sums, axis=1)
    mid = mid_ref[...]
    inverse = lax.rsqrt(jnp.mean(mid * mid, axis=-1, keepdims=True) + norm_eps)
    scaled = moe_grad * gains_ref[1:2, :]
    shared = jnp.sum(scaled * mid, axis=-1, keepdims=True) * (inverse * inverse * inverse / wide)
    mid_grad = grad_ref[...].astype(full) + (scaled * inverse - mid * shared)
    mid_grad_ref[...] = mid_grad
    low = mid_grad.astype(low_type)
    low_ref[...] = low
    ffn_ref[...] = jnp.sum(mid * inverse * moe_grad, axis=0, keepdims=True)
    third = []
    for k in (1, 2, 3, 4, 5, 6, 7, 0):
        g = lax.bitwise_xor(dp, k)
        piece = dot_nt(low, output_ref[pl.ds(pl.multiple_of(g * PAIR, PAIR), PAIR), :])
        if k:
            grad_buf[g] = piece.astype(low_type)
            third.append(send(grad_buf.at[g], home_ref.at[dp], peers[5 + k]))
        else:
            home_ref[dp] = piece.astype(low_type)
    for j in range(parts):
        total_job("in", j)
        total_job("down", j)
    for copies in (along, second, core_copies, x_copies):
        for copy in copies.values():
            copy.wait_send()
    for side in (0, 1):
        for j in range(parts):
            for k in range(4):
                for n in (1, 2, 3):
                    back_copy(side, j, k, n).wait_send()
    for copy in third:
        copy.wait()


def moe_layer(att, output_proj, tokens, gains, left, right, grad, held, in_w, down_w, weights, experts, number):
    rows, wide = tokens.shape
    _, _, parts, slots, _ = held.shape
    half = wide // 2
    hidden = down_w.shape[2]
    shapes = [
        ((rows, wide), full),
        (held.shape, low_type),
        ((parts, wide // 8, 2 * hidden), full),
        ((parts, wide // 8, hidden), full),
        ((wide, EXTRA), full),
        ((wide, rows), low_type),
        ((rows, wide), full),
        ((rows, wide), low_type),
        ((1, wide), full),
        ((KV_HEADS, rows, PAIR), low_type),
    ]
    scratch = [
        (rows, wide),
        (2, 3, rows, half),
        (2, parts, 4, 4, slots, half),
        (parts, 4, 4, slots, wide),
        (4, 4, slots, wide),
        (4, 4 * slots, 2 * hidden),
        (4, 4 * slots, hidden),
        (4, 4 * slots, EXTRA),
        (2, 4, slots, wide),
        in_w.shape[1:],
        down_w.shape[1:],
        (wide, EXTRA),
        (2, 4, 3, parts, slots, half),
        (2, 3, rows, half),
        (2, 3, rows, half),
        (parts, 4, 2, wide // 8, 2 * hidden),
        (parts, 4, 2, wide // 8, hidden),
        (parts, 4, wide // 8, 2 * hidden),
        (parts, 4, wide // 8, hidden),
        (parts, 3, wide // 8, 2 * hidden),
        (parts, 3, wide // 8, hidden),
        (KV_HEADS, rows, PAIR),
    ]
    copies = 6 + 24 * parts + 8 * parts + 6 + 7
    return pl.pallas_call(
        functools.partial(moe_kernel, experts),
        out_shape=[jax.ShapeDtypeStruct(*s) for s in shapes],
        in_specs=[VMEM] * 7 + [ANY] * 4,
        out_specs=[VMEM, ANY] + [VMEM] * 8,
        scratch_shapes=[
            *[pltpu.VMEM(s, low_type) for s in scratch],
            *[pltpu.SemaphoreType.DMA((copies,))] * 2,
            *[pltpu.SemaphoreType.DMA((24 * parts,))] * 2,
            pltpu.SemaphoreType.DMA((2,)),
            pltpu.SemaphoreType.DMA((3 * parts + 1,)),
        ],
        compiler_params=comm_params(number),
        cost_estimate=cost(120),
        name="moe_layer",
    )(att, output_proj, tokens, gains, left, right, grad, held, in_w, down_w, weights)


def allowed_of(shape, rows, length, i):
    key_at = lax.broadcasted_iota(jnp.int32, shape, 0)
    query_at = lax.broadcasted_iota(jnp.int32, shape, 1) % rows
    return (key_at <= query_at) & (key_at < length - i * rows)


def key_spread(width, wide):
    out = lax.broadcasted_iota(jnp.int32, (wide, width), 0)
    here = lax.broadcasted_iota(jnp.int32, (wide, width), 1)
    return jnp.where(out == (here // 4) * 8 + here % 4, 1.0, 0.0).astype(low_type)


def hand_over(sent, home, send_sem, recv_sem, i):
    dp, expert, _ = place_of()
    k = lax.bitwise_xor(dp, i)
    return pltpu.make_async_remote_copy(
        src_ref=sent.at[i],
        dst_ref=home.at[dp],
        send_sem=send_sem.at[k],
        recv_sem=recv_sem.at[k],
        device_id=(i, expert),
        device_id_type=MESH,
    )


def gather_weights(
    at, meet_all, query_ref, key_ref, value_ref, router_ref, gains_row, slot_a, slot_b, master_ref, buf, third, got_a, got_b,
    shard_ref, shards_ref, mine_ref, others_ref, ours_ref, send,
):
    x, y, z, c = at["x"], at["y"], at["z"], at["core"]
    rows, columns = shard_ref.shape
    cut = columns // 256 * 128
    sides = (pl.ds(0, cut), pl.ds(cut, columns - cut))
    for g in range(KV_HEADS):
        here = g * PACK
        shard_ref[:, here : here + PAIR] = query_ref[:, g * PAIR : (g + 1) * PAIR]
        head = slice(g * HEAD_DIM, (g + 1) * HEAD_DIM)
        shard_ref[:, here + PAIR : here + PACK] = jnp.concatenate(
            [key_ref[:, head], value_ref[:, head]], axis=1
        )
    experts = router_ref.shape[1]
    lane = lax.broadcasted_iota(jnp.int32, (rows, EXTRA), 1)
    row = lax.broadcasted_iota(jnp.int32, (rows, EXTRA), 0)
    gains = jnp.broadcast_to(gains_row, (rows, EXTRA))
    extra = jnp.concatenate(
        [router_ref[...], jnp.zeros((rows, EXTRA - experts), full)], axis=1
    )
    for n in range(4):
        column = jnp.sum(jnp.where(lane == row + n * rows, gains, 0.0), axis=1, keepdims=True)
        extra += jnp.where(lane == experts + n, column, 0.0)
    shard_ref[:, KV_HEADS * PACK :] = extra
    meet_all()
    first = [send(shard_ref, shards_ref.at[z], peer_on("z", k)) for k in (1, 2, 3)]
    first += [send(master_ref, others_ref.at[x], peer_on("x", k)) for k in (1, 2, 3)]
    shards_ref[z] = shard_ref[...]
    others_ref[x] = master_ref[...]
    slots = []
    for k in (1, 2, 3):
        slots.append(send(slot_a.at[lax.bitwise_xor(y, k)], got_a.at[y], peer_on("y", k)))
        slots.append(send(slot_b.at[lax.bitwise_xor(z, k)], got_b.at[z], peer_on("z", k)))
    got_a[y] = slot_a[y]
    got_b[z] = slot_b[z]
    for copy in first:
        copy.wait()
    mine = shards_ref[...].reshape(mine_ref.shape).astype(low_type)
    mine_ref[...] = mine
    buf[x, c, y] = mine
    ours = others_ref[...].reshape(ours_ref.shape).astype(low_type)
    ours_ref[...] = ours
    third[z, c, y] = ours
    second = []
    for k in (1, 2, 3):
        for side, axis in ((0, "y"), (1, "x")):
            second.append(
                send(
                    mine_ref.at[:, sides[side]],
                    buf.at[x, c, y, :, sides[side]],
                    peer_on(axis, k),
                )
            )
        second.append(send(ours_ref, third.at[z, c, y], peer_on("y", k)))
    for copy in second:
        copy.wait()
    final = []
    for k in (1, 2, 3):
        piece = buf.at[x, c, :, :, sides[0]]
        final.append(send(piece, piece, peer_on("x", k)))
        piece = buf.at[:, c, y, :, sides[1]]
        final.append(send(piece, piece, peer_on("y", k)))
        piece = third.at[z, c]
        final.append(send(piece, piece, peer_on("z", k)))
    other = peer_on("core", 1)
    last = []
    for piece in (buf.at[x, c, :, :, sides[0]], buf.at[:, c, y, :, sides[1]], third.at[z, c]):
        last.append(send(piece, piece, other))
    for n, k in enumerate((1, 2, 3)):
        final[3 * n].wait_recv()
        piece = buf.at[lax.bitwise_xor(x, k), c, :, :, sides[0]]
        last.append(send(piece, piece, other))
        final[3 * n + 1].wait_recv()
        piece = buf.at[:, c, lax.bitwise_xor(y, k), :, sides[1]]
        last.append(send(piece, piece, other))
        final[3 * n + 2].wait_recv()
        piece = third.at[lax.bitwise_xor(z, k), c]
        last.append(send(piece, piece, other))
    return slots, final, last


def forward_kernel(
    length_ref, query_ref, key_ref, value_ref, router_ref, gains_row, slot_a, slot_b, master_ref, tokens_ref, cos_ref, sin_ref, grad_ref,
    weights_out, rows_ref, output_ref, normed_rows, raw_ref, pack_ref, gains_ref, held_ref, att_ref, log_ref, home_ref, left_ref, right_ref,
    shard_ref, shards_ref, mine_ref, others_ref, ours_ref, weights_ref, third_buf,
    grad_bufs, rows_a, rows_b, sent, flip_ref, score_ref,
    gather_send, gather_recv, send_one, recv_one, send_two, recv_two, send_sem, recv_sem, move_sem,
):
    dp, _, at = place_of()
    y, z = at["y"], at["z"]
    peers = dp_peers() + [peer_on(axis, k) for axis, k in PLANE]
    greet(peers)
    blocks, rows = held_ref.shape[0], held_ref.shape[1]
    wide = tokens_ref.shape[1]
    width = KV_HEADS * HEAD_DIM
    half = wide // 2
    slots_sent, final, last = gather_weights(
        at, lambda: meet(peers), query_ref, key_ref, value_ref, router_ref, gains_row[...], slot_a, slot_b, master_ref,
        weights_ref, third_buf, left_ref, right_ref, shard_ref, shards_ref, mine_ref, others_ref, ours_ref,
        Sender(gather_send, gather_recv),
    )
    send, move = Sender(send_sem, recv_sem), Mover(move_sem)
    along = {}
    for k in (1, 2, 3):
        for side, axis in ((0, "y"), (1, "z")):
            piece = grad_ref.at[:, pl.ds(side * half, half)]
            along[side, k] = send(piece, grad_bufs.at[side, k - 1], peer_on(axis, k))
    for copy in last:
        copy.wait()
    stored = move(weights_ref, weights_out)

    def weights_of(start, count):
        return weights_ref[..., start : start + count].reshape(wide, count)

    extra = flip(weights_of(KV_HEADS * PACK, EXTRA))
    gains_ref[0:1, :] = extra[32:33]
    gains_ref[1:2, :] = extra[34:35]
    key_gain = dot(
        jnp.broadcast_to(extra[35:36], (8, wide)).astype(low_type), key_spread(width, wide)
    )[:1]
    for g in range(KV_HEADS):
        pack_ref[g, :, :PAIR] = extra[33:34, g * PAIR : (g + 1) * PAIR]
        pack_ref[g, :, PAIR:] = jnp.concatenate(
            [key_gain[:, g * HEAD_DIM : (g + 1) * HEAD_DIM], jnp.ones((1, HEAD_DIM), full)],
            axis=1,
        )
    values = tokens_ref[...].astype(full)
    inverse = lax.rsqrt(jnp.mean(values * values, axis=-1, keepdims=True) + norm_eps)
    normed = (values * inverse * gains_ref[0:1, :]).astype(low_type)
    query_sum = jnp.zeros((rows, PAIR), full)
    key_sum = jnp.zeros((rows, PAIR), full)
    for g in range(KV_HEADS):
        raw = dot(normed, weights_of(g * PACK, PACK))
        raw_ref[g] = raw
        query_sum += raw[:, :PAIR] * raw[:, :PAIR]
        key_sum += raw[:, PAIR:] * raw[:, PAIR:]
    is_key = lax.broadcasted_iota(jnp.int32, key_sum.shape, 1) < HEAD_DIM
    query_inv = lax.rsqrt(
        jnp.sum(query_sum, axis=-1, keepdims=True) / (GROUP * width) + norm_eps
    )
    key_inv = lax.rsqrt(
        jnp.sum(jnp.where(is_key, key_sum, 0.0), axis=-1, keepdims=True) / width + norm_eps
    )
    pair_inv = jnp.where(is_key, key_inv, 1.0)
    handed = []
    for k in (1, 2, 3, 4, 5, 6, 7, 0):
        g = lax.bitwise_xor(dp, k)
        target = sent if k else held_ref
        for part, scale in ((0, query_inv), (1, pair_inv)):
            here = slice(part * PAIR, (part + 1) * PAIR)
            scaled = raw_ref[g, :, here] * scale * pack_ref[g, :, here]
            turned = scaled * cos_ref[:, here] + partner(scaled) * sin_ref[:, here]
            target[g, :, here] = turned.astype(low_type)
        if k:
            handed.append(hand_over(sent, held_ref, send_one, recv_one, g))
            handed[-1].start()
    def tokens_of(side, k):
        if k == 0:
            return grad_ref[:, side * half : (side + 1) * half]
        along[side, k].wait_recv()
        return grad_bufs[side, k - 1]

    for copy in slots_sent:
        copy.wait()
    spread = spread_slots(
        send, move, (left_ref, right_ref), tokens_of, (rows_a, rows_b), rows_ref
    )
    wide_query = GROUP * rows
    flat = flip(normed)
    normed_rows[0] = flat.astype(low_type)
    normed_rows[1] = by_place(flat, ("y", "core", "z", "x")).astype(low_type)
    for n in range(4):
        pieces = [
            third_buf[p, m // 4, m % 4, n * 8 : n * 8 + 8, :].astype(full)
            for m in range(8)
            for p in range(4)
        ]
        output_ref[n * 256 : (n + 1) * 256, :] = jnp.concatenate(pieces, axis=0).astype(low_type)

    for i in range(blocks):

        @pl.when(i != dp)
        def _():
            hand_over(sent, held_ref, send_one, recv_one, i).wait_recv()

        span = slice(i * rows, (i + 1) * rows)
        flip_ref[:, span] = flip(held_ref[i, :, PAIR + HEAD_DIM :]).astype(low_type)
        query = flip(held_ref[i, :, :PAIR]).astype(low_type)
        query = jnp.concatenate([query[:HEAD_DIM], query[HEAD_DIM:]], axis=1)
        top = jnp.full((1, wide_query), masked_score, full)
        for j in range(i + 1):
            scores = dot(held_ref[j, :, PAIR : PAIR + HEAD_DIM], query) * score_scale
            if j == i:
                allowed = allowed_of(scores.shape, rows, length_ref[0], i)
                scores = jnp.where(allowed, scores, masked_score)
            score_ref[j * rows : (j + 1) * rows] = scores
            top = jnp.maximum(top, jnp.max(scores, axis=0, keepdims=True))
        soft = jnp.exp(score_ref[: (i + 1) * rows] - top)
        total = jnp.sum(soft, axis=0, keepdims=True)
        acc = dot(flip_ref[:, : (i + 1) * rows], soft.astype(low_type)) / total
        both = jnp.concatenate([acc[:, :rows], acc[:, rows:]], axis=0)
        att_ref[i] = both.T.astype(low_type)
        log_ref[i] = jnp.broadcast_to(top + jnp.log(total), log_ref.shape[1:])

        @pl.when(i != dp)
        def _():
            hand_over(att_ref, home_ref, send_two, recv_two, i).start()

        @pl.when(i == dp)
        def _():
            home_ref[i] = att_ref[i]

    for copy in handed:
        copy.wait_send()
    for copy in spread:
        copy.wait()
    for copies in (along.values(), final):
        for copy in copies:
            copy.wait_send()
    stored.wait()
    for k in range(1, 8):
        hand_over(att_ref, home_ref, send_two, recv_two, lax.bitwise_xor(dp, k)).wait()


def forward(lengths, masters, gains_row, slot_a, slot_b, tokens, cosine, sine, grad, slots, number):
    rows, wide = tokens.shape
    query, key, value, output, router = masters
    share, columns = query.shape[0], KV_HEADS * PACK + EXTRA
    _, _, parts, _ = slot_a.shape
    shapes = [
        ((4, 2, 4, 4 * share, columns), low_type),
        ((4, 4, parts, slots, wide), low_type),
        ((wide, wide), low_type),
        ((2, wide, rows), low_type),
        ((KV_HEADS, rows, PACK), full),
        ((KV_HEADS, 1, PACK), full),
        ((8, wide), full),
        ((8, rows, PACK), low_type),
        ((8, rows, PAIR), low_type),
        ((8, 8, GROUP * rows), full),
        ((KV_HEADS, rows, PAIR), low_type),
        (slot_a.shape, full),
        (slot_b.shape, full),
    ]
    return pl.pallas_call(
        forward_kernel,
        out_shape=[jax.ShapeDtypeStruct(*s) for s in shapes],
        in_specs=[SMEM] + [VMEM] * 12,
        out_specs=[ANY] * 2 + [VMEM] * (len(shapes) - 2),
        scratch_shapes=[
            pltpu.VMEM((share, columns), full),
            pltpu.VMEM((4, share, columns), full),
            pltpu.VMEM((4 * share, columns), low_type),
            pltpu.VMEM((4, share, wide), full),
            pltpu.VMEM((4 * share, wide), low_type),
            pltpu.VMEM((4, 2, 4, 4 * share, columns), low_type),
            pltpu.VMEM((4, 2, 4, 4 * share, wide), low_type),
            pltpu.VMEM((2, 3, rows, wide // 2), low_type),
            pltpu.VMEM((4, 4, parts, slots, wide // 2), low_type),
            pltpu.VMEM((4, 4, parts, slots, wide // 2), low_type),
            pltpu.VMEM((KV_HEADS, rows, PACK), low_type),
            pltpu.VMEM((HEAD_DIM, 8 * rows), low_type),
            pltpu.VMEM((8 * rows, GROUP * rows), full),
            *[pltpu.SemaphoreType.DMA((42,))] * 2,
            *[pltpu.SemaphoreType.DMA((8,))] * 4,
            *[pltpu.SemaphoreType.DMA((30,))] * 2,
            pltpu.SemaphoreType.DMA((9,)),
        ],
        compiler_params=comm_params(number),
        cost_estimate=cost(75),
        name="forward",
    )(lengths, query, key, value, router, gains_row, slot_a, slot_b, output, tokens, cosine, sine, grad)


def backward_kernel(
    length_ref, held_ref, grad_ref, att_ref, log_ref, home_ref, sent, flip_ref, sum_ref, back_ref, send_sem, recv_sem
):
    dp, _, _ = place_of()
    blocks, rows = held_ref.shape[0], held_ref.shape[1]
    for j in range(blocks):
        flip_ref[:, j * rows : (j + 1) * rows] = flip(held_ref[j, :, PAIR:])[:HEAD_DIM].astype(
            low_type
        )
    none = jnp.zeros((rows, HEAD_DIM), low_type)
    key_scale = jnp.where(
        lax.broadcasted_iota(jnp.int32, (rows, PAIR), 1) < HEAD_DIM, score_scale, 1.0
    )

    def heads_beside(values):
        return jnp.concatenate([values[:HEAD_DIM], values[HEAD_DIM:]], axis=1)

    for i in range(blocks - 1, -1, -1):
        query_rows = held_ref[i, :, :PAIR]
        grad_rows = grad_ref[i]
        query = heads_beside(flip(query_rows)).astype(low_type)
        grad_full = heads_beside(flip(grad_rows))
        grad = grad_full.astype(low_type)
        inner = jnp.sum(grad_full * heads_beside(flip(att_ref[i])), axis=0, keepdims=True)
        log_total = log_ref[i, :1, :]
        query_side = jnp.concatenate(
            [
                jnp.concatenate([query_rows[:, :HEAD_DIM], none], axis=1),
                jnp.concatenate([query_rows[:, HEAD_DIM:], none], axis=1),
            ],
            axis=0,
        )
        grad_side = jnp.concatenate(
            [
                jnp.concatenate([none, grad_rows[:, :HEAD_DIM]], axis=1),
                jnp.concatenate([none, grad_rows[:, HEAD_DIM:]], axis=1),
            ],
            axis=0,
        )
        for j in range(i + 1):
            key = held_ref[j, :, PAIR : PAIR + HEAD_DIM]
            value = held_ref[j, :, PAIR + HEAD_DIM :]
            soft = jnp.exp(dot(key, query) * score_scale - log_total)
            if j == i:
                allowed = allowed_of(soft.shape, rows, length_ref[0], i)
                soft = jnp.where(allowed, soft, 0.0)
            score_grad = (soft * (dot(value, grad) - inner)).astype(low_type)
            back_ref[j * rows : (j + 1) * rows] = score_grad
            part = dot(score_grad, query_side) + dot(soft.astype(low_type), grad_side)
            sum_ref[j] = part if i == blocks - 1 else sum_ref[j] + part
        acc = dot(flip_ref[:, : (i + 1) * rows], back_ref[: (i + 1) * rows])
        both = jnp.concatenate([acc[:, :rows], acc[:, rows:]], axis=0) * score_scale
        sent[i, :, :PAIR] = both.T.astype(low_type)
        sent[i, :, PAIR:] = (sum_ref[i] * key_scale).astype(low_type)

        @pl.when(i != dp)
        def _():
            hand_over(sent, home_ref, send_sem, recv_sem, i).start()

        @pl.when(i == dp)
        def _():
            home_ref[i] = sent[i]


def tail_kernel(
    length_ref, held_ref, grad_ref, att_ref, log_ref, pack_ref, gains_ref, left_ref, right_ref, made_ref, *refs
):
    given, refs = refs[:12], refs[12:]
    (output_ref, tokens_ref, *sums), refs = refs[:5], refs[5:]
    here, refs = refs[:12], refs[12:]
    held, going, came, refs = refs[0:2], refs[2:4], refs[4:6], refs[6:]
    (home, sent, flip_ref, sum_ref, back_ref, low_ref), refs = refs[:6], refs[6:]
    thirds, reduce_scratch, refs = refs[:3], refs[3:21], refs[21:]
    send_one, recv_one, send_two, recv_two, send_three, recv_three, local_sem = refs
    dp, _, _ = place_of()
    peers = dp_peers() + [peer_on(axis, k) for axis, k in PLANE]
    greet(peers)
    move = Mover(local_sem)
    loads = [move(source, target) for source, target in zip(given, here)]
    att_rows, mid_low, raw, cos, sin, weights, normed, tokens, mid_grad, router, ffn, mid = here
    wide = tokens.shape[1]
    width = KV_HEADS * HEAD_DIM
    meet(peers)
    homeward = Homeward(
        Sender(send_two, recv_two), move, made_ref, (left_ref, right_ref), held, going, came
    )
    reduce = Reduce(thirds, reduce_scratch, send_three, recv_three)
    loads[0].wait()
    loads[1].wait()
    put_product(thirds[2], 0, att_rows[...], mid_low, 0, wide)
    reduce.cores(2)
    backward_kernel(
        length_ref, held_ref, grad_ref, att_ref, log_ref, home, sent, flip_ref, sum_ref, back_ref, send_one, recv_one
    )
    reduce.first(2)
    for load in loads[2:]:
        load.wait()
    for k in range(1, 8):
        hand_over(sent, home, send_one, recv_one, lax.bitwise_xor(dp, k)).wait()
    query_grad, key_grad = raw_gradients(home, raw, pack_ref, cos, sin, low_ref)
    put_product(thirds[1], 0, normed[1], low_ref, LEFT, KV_HEADS * PACK - LEFT)
    reduce.cores(1)
    put_product(thirds[0], EXTRA, normed[0], low_ref, 0, LEFT)
    attn_grad = token_gradients(low_ref, weights, tokens, gains_ref, mid_grad, tokens_ref)
    key_wide = dot_nt(
        jnp.broadcast_to(key_grad, (8, width)).astype(low_type), key_spread(width, wide)
    )[:1]
    extra = jnp.concatenate(
        [
            jnp.zeros((32, wide), full),
            attn_grad,
            query_grad,
            ffn[...],
            key_wide,
            jnp.zeros((EXTRA - 36, wide), full),
        ],
        axis=0,
    )
    extra = (extra.T + router[...]).astype(low_type)
    thirds[0][..., :EXTRA] = extra.reshape(thirds[0].shape[:-1] + (EXTRA,))
    reduce.cores(0)
    reduce.first(1)
    reduce.first(0)
    for k in (1, 2, 3):
        homeward.add(k)
    reduce.second(2)
    reduce.second(1)
    reduce.second(0)
    homeward.add(0)
    for n in (2, 1, 0):
        reduce.third(n)
    output_ref[...] = (mid[...] + homeward.sums()).astype(low_type)
    for n in (2, 1, 0):
        sums[n][...] = reduce.finish(n)
    homeward.end()


def tail(lengths, held, grad, att, logs, pack, gains, left, right, made, given, number):
    blocks, rows, _ = held.shape
    _, _, parts, slots, wide = made.shape
    widths = (EXTRA + LEFT, KV_HEADS * PACK - LEFT, wide)

    def each(*shape, kind=low_type):
        return [pltpu.VMEM(shape + (w,), kind) for w in widths]

    return pl.pallas_call(
        tail_kernel,
        out_shape=[
            jax.ShapeDtypeStruct((rows, wide), low_type),
            jax.ShapeDtypeStruct((rows, wide), low_type),
            *[jax.ShapeDtypeStruct((8, w), full) for w in widths],
        ],
        in_specs=[SMEM] + [VMEM] * 8 + [ANY] * 13,
        out_specs=[VMEM] * 5,
        scratch_shapes=[
            *[pltpu.VMEM(v.shape, v.dtype) for v in given],
            *home_scratch(parts, slots, rows, wide // 2),
            pltpu.VMEM((KV_HEADS, rows, PACK), low_type),
            pltpu.VMEM((blocks, rows, PACK), low_type),
            pltpu.VMEM((HEAD_DIM, blocks * rows), low_type),
            pltpu.VMEM((blocks, rows, PAIR), full),
            pltpu.VMEM((blocks * rows, GROUP * rows), low_type),
            pltpu.VMEM((rows, KV_HEADS * PACK), low_type),
            *each(4, 2, 4, 32),
            *each(4, 4, 32),
            *each(3, 4, 32),
            *each(3, 32),
            *each(3, 4, 32),
            *each(4, 8, kind=full),
            *each(3, 8, kind=full),
            *[pltpu.SemaphoreType.DMA((8,))] * 2,
            *[pltpu.SemaphoreType.DMA((30,))] * 2,
            *[pltpu.SemaphoreType.DMA((39,))] * 2,
            pltpu.SemaphoreType.DMA((20,)),
        ],
        compiler_params=comm_params(number),
        cost_estimate=cost(90),
        name="tail",
    )(
        lengths, held, grad, att, logs, pack, gains, left, right,
        made, *given,
    )


def finish_kernel(
    left_ref, right_ref, third_ref, query_ref, key_ref, value_ref, out_proj_ref, router_ref, attn_ref, ffn_ref, query_gain_ref, key_gain_ref,
):
    out_proj_ref[...] = third_ref[...]
    for g in range(KV_HEADS):
        start = g * PACK
        if start < LEFT:
            piece = left_ref[:, EXTRA + start : EXTRA + start + PACK]
        else:
            piece = right_ref[:, start - LEFT : start - LEFT + PACK]
        head = slice(g * HEAD_DIM, (g + 1) * HEAD_DIM)
        query_ref[:, g * PAIR : (g + 1) * PAIR] = piece[:, :PAIR]
        key_ref[:, head] = piece[:, PAIR : PAIR + HEAD_DIM]
        value_ref[:, head] = piece[:, PAIR + HEAD_DIM :]
    extra = left_ref[:, :EXTRA]
    experts = router_ref.shape[1]
    router_ref[...] = extra[:, :experts]
    rows = extra.shape[0]
    lane = lax.broadcasted_iota(jnp.int32, (rows, rows), 1)
    row = lax.broadcasted_iota(jnp.int32, (rows, rows), 0)
    for n, ref in enumerate((attn_ref, query_gain_ref, ffn_ref, key_gain_ref)):
        column = jnp.broadcast_to(extra[:, experts + n : experts + n + 1], (rows, rows))
        flat = jnp.sum(jnp.where(lane == row, column, 0.0), axis=0, keepdims=True)
        ref[...] = flat[:, : ref.shape[1]]


def raw_gradients(back_ref, raw_ref, pack_ref, cos_ref, sin_ref, low_ref):
    rows = back_ref.shape[1]
    width = KV_HEADS * HEAD_DIM
    is_key = lax.broadcasted_iota(jnp.int32, (rows, PAIR), 1) < HEAD_DIM
    sums = [[jnp.zeros((rows, PAIR), full) for _ in range(2)] for _ in range(2)]

    def here_of(part):
        return slice(part * PAIR, (part + 1) * PAIR)

    def unturned(g, part):
        here = here_of(part)
        grad = back_ref[g, :, here].astype(full)
        return grad * cos_ref[:, here] - partner(grad) * sin_ref[:, here]

    for g in range(KV_HEADS):
        for part in range(2):
            raw = raw_ref[g, :, here_of(part)]
            sums[part][0] += raw * raw
            sums[part][1] += raw * unturned(g, part) * pack_ref[g, :, here_of(part)]
    mean_of = [GROUP * width, width]
    inverses, shares = [], []
    for part in range(2):
        square, cross = sums[part]
        if part == 1:
            square, cross = jnp.where(is_key, square, 0.0), jnp.where(is_key, cross, 0.0)
        inverse = lax.rsqrt(jnp.sum(square, axis=-1, keepdims=True) / mean_of[part] + norm_eps)
        share = jnp.sum(cross, axis=-1, keepdims=True) * (
            inverse * inverse * inverse / mean_of[part]
        )
        if part == 1:
            inverse = jnp.where(is_key, inverse, 1.0)
            share = jnp.where(is_key, share, 0.0)
        inverses.append(inverse)
        shares.append(share)
    gains = [[], []]
    for g in range(KV_HEADS):
        for part in range(2):
            raw = raw_ref[g, :, here_of(part)]
            grad = unturned(g, part)
            gains[part].append(jnp.sum(raw * inverses[part] * grad, axis=0, keepdims=True))
            result = grad * pack_ref[g, :, here_of(part)] * inverses[part] - raw * shares[part]
            start = g * PACK + part * PAIR
            low_ref[:, start : start + PAIR] = result.astype(low_type)
    query_grad = jnp.concatenate(gains[0], axis=1)
    key_grad = jnp.concatenate(
        [
            jnp.concatenate(
                [gains[1][2 * g][:, :HEAD_DIM], gains[1][2 * g + 1][:, :HEAD_DIM]], axis=1
            )
            for g in range(KV_HEADS // 2)
        ],
        axis=1,
    )
    return query_grad, key_grad


def token_gradients(low_ref, weights_ref, tokens_ref, gains_ref, mid_grad_ref, out_ref):
    normed_grad = dot_nt(low_ref[...], weights_ref[:, : KV_HEADS * PACK])
    values = tokens_ref[...].astype(full)
    wide = values.shape[1]
    inverse = lax.rsqrt(jnp.mean(values * values, axis=-1, keepdims=True) + norm_eps)
    scaled = normed_grad * gains_ref[0:1, :]
    share = jnp.sum(scaled * values, axis=-1, keepdims=True) * (
        inverse * inverse * inverse / wide
    )
    out_ref[...] = (mid_grad_ref[...] + (scaled * inverse - values * share)).astype(low_type)
    return jnp.sum(values * inverse * normed_grad, axis=0, keepdims=True)


def put_product(ref, start, left, right_ref, at, count):
    places = ref.shape[:-1]
    for n in range(0, count, 256):
        value = dot(left, right_ref[:, at + n : at + n + 256]).astype(low_type)
        ref[..., start + n : start + n + 256] = value.reshape(places + (256,))


def on_device(
    tokens_in,
    lengths,
    routes,
    w_query,
    w_key,
    w_value,
    w_output,
    w_router,
    attn_gain,
    ffn_gain,
    query_gain,
    key_gain,
    expert_in,
    expert_down,
    out_grad,
):
    rows, wide = tokens_in.shape[1], tokens_in.shape[2]
    experts = w_router.shape[1]
    parts = expert_in.shape[0]
    owners = experts // parts
    slots = 5 * rows * routes.shape[2] // (4 * experts)
    tokens = tokens_in[0]
    grad_out = out_grad[0]

    place = lax.axis_index("dp") * rows + jnp.arange(rows)
    valid = (place < lengths[0]).astype(jnp.int32)
    ids = jnp.arange(experts)
    chosen = (
        jnp.sum((routes[0][:, :, None] == ids[None, None, :]).astype(jnp.int32), axis=1)
        * valid[:, None]
    )
    earlier = jnp.cumsum(chosen, axis=0) - chosen
    slot_of = jnp.where(chosen == 1, earlier, -1).T.astype(full)

    lane = jnp.arange(PACK)
    frequency = rope_base ** (
        -2.0 * (lane % (HEAD_DIM // 2)).astype(full) / HEAD_DIM
    )
    angles = place.astype(full)[:, None] * frequency[None, :]
    turning = (lane < PAIR + HEAD_DIM)[None, :]
    cosine = jnp.where(turning, jnp.cos(angles), 1.0)
    sign = jnp.where(lane % HEAD_DIM < HEAD_DIM // 2, -1.0, 1.0)
    sine = jnp.where(turning, jnp.sin(angles) * sign, 0.0)

    gains = jnp.concatenate([attn_gain, query_gain, ffn_gain, key_gain])
    gains = jnp.pad(gains, (0, EXTRA - gains.shape[0]))[None]
    slot_a = slot_of.reshape(4, 4, parts, rows)
    slot_b = slot_a.transpose(1, 0, 2, 3)
    (weights, grad_held, output_proj, normed_rows, raw, pack_row, gain_rows, held, att, logs, att_home, left, right) = forward(
        lengths, (w_query, w_key, w_value, w_output, w_router), gains, slot_a, slot_b, tokens, cosine, sine, grad_out, slots, 1
    )
    weights = weights.reshape(wide, KV_HEADS * PACK + EXTRA)
    mid, made, in_grad, down_grad, router_grad, att_rows, mid_grad, mid_low, ffn_grad, att_grad = moe_layer(
        att_home, output_proj, tokens, gain_rows, left, right, grad_out, grad_held, expert_in, expert_down, weights, experts, 2
    )
    output, grad_tokens, *sums = tail(
        lengths, held, att_grad, att, logs, pack_row, gain_rows, left, right, made,
        (att_rows, mid_low, raw, cosine, sine, weights, normed_rows, tokens, mid_grad, router_grad, ffn_grad, mid), 3,
    )
    shapes = [
        (w_query.shape, full),
        (w_key.shape, full),
        (w_value.shape, full),
        (w_output.shape, full),
        (w_router.shape, full),
        ((1, attn_gain.shape[0]), full),
        ((1, ffn_gain.shape[0]), full),
        ((1, query_gain.shape[0]), full),
        ((1, key_gain.shape[0]), full),
    ]
    results = pl.pallas_call(
        finish_kernel,
        out_shape=[jax.ShapeDtypeStruct(*s) for s in shapes],
        in_specs=[VMEM] * 3,
        out_specs=[VMEM] * len(shapes),
        name="finish",
        **params(2),
    )(*sums)
    return (
        output[None],
        grad_tokens[None],
        *results[:5],
        *[row[0] for row in results[5:]],
        in_grad,
        down_grad,
    )


def solution(mesh):
    in_specs = (
        P("expert", "dp", None),
        P("expert"),
        P("expert", "dp", None),
        P(("dp", "expert"), None),
        P(("dp", "expert"), None),
        P(("dp", "expert"), None),
        P(("dp", "expert"), None),
        P(("dp", "expert"), None),
        P(("dp", "expert")),
        P(("dp", "expert")),
        P(("dp", "expert")),
        P(("dp", "expert")),
        P("expert", None, None),
        P("expert", None, None),
        P("expert", "dp", None),
    )
    out_specs = (
        P("expert", "dp", None),
        P("expert", "dp", None),
        P(("dp", "expert"), None),
        P(("dp", "expert"), None),
        P(("dp", "expert"), None),
        P(("dp", "expert"), None),
        P(("dp", "expert"), None),
        P(("dp", "expert")),
        P(("dp", "expert")),
        P(("dp", "expert")),
        P(("dp", "expert")),
        P("expert", "dp", None),
        P("expert", "dp", None),
    )
    return jax.shard_map(
        on_device, mesh=mesh, in_specs=in_specs, out_specs=out_specs, check_vma=False
    )
```

```python
import functools

import jax
import jax.numpy as jnp
from jax import lax
from jax.experimental import pallas as pl
from jax.experimental.pallas import tpu as pltpu
from jax.sharding import PartitionSpec as P

HEADS = 16
HEAD_DIM = 64
KV_HEADS = 8
GROUP = HEADS // KV_HEADS
PAIR = GROUP * HEAD_DIM
PACK = PAIR + 2 * HEAD_DIM
EXTRA = 128
CUTS = (0, 4 * PACK, 6 * PACK, 8 * PACK)

norm_eps = 1e-06
rope_base = 10000.0
masked_score = -1e30
score_scale = HEAD_DIM ** (-0.5)
low_type = jnp.bfloat16
full = jnp.float32

VMEM = pl.BlockSpec(memory_space=pltpu.VMEM)
SMEM = pl.BlockSpec(memory_space=pltpu.SMEM)
LIMIT = 62 * 1024 * 1024


def dot(left, right):
    return jnp.dot(left, right, preferred_element_type=full)


def dot_nt(left, right):
    return lax.dot_general(left, right, (((1,), (1,)), ((), ())), preferred_element_type=full)


def dot_tn(left, right):
    return lax.dot_general(left, right, (((0,), (0,)), ((), ())), preferred_element_type=full)


def partner(values):
    lane = lax.broadcasted_iota(jnp.int32, values.shape, 1)
    half = HEAD_DIM // 2
    return jnp.where(
        lane % HEAD_DIM < half, pltpu.roll(values, 128 - half, 1), pltpu.roll(values, half, 1)
    )


def flip(values):
    return values.astype(full).T


def cost(microseconds):
    return pl.CostEstimate(
        flops=int(microseconds * 1.15e9), bytes_accessed=1 << 20, transcendentals=0
    )


def params(microseconds):
    return dict(
        compiler_params=pltpu.CompilerParams(vmem_limit_bytes=LIMIT),
        cost_estimate=cost(microseconds),
    )


MESH = pl.DeviceIdType.MESH
ANY = pl.BlockSpec(memory_space=pl.ANY)


def comm_params(number):
    return pltpu.CompilerParams(
        collective_id=number, has_side_effects=True, vmem_limit_bytes=LIMIT
    )


def place_of():
    dp, expert = lax.axis_index("dp"), lax.axis_index("expert")
    return dp, expert, dict(x=dp // 2, core=dp % 2, y=expert // 4, z=expert % 4)


def peer_on(axis, step):
    dp, expert, _ = place_of()
    if axis == "core":
        return lax.bitwise_xor(dp, 1), expert
    if axis == "x":
        return lax.bitwise_xor(dp, 2 * step), expert
    if axis == "y":
        return dp, lax.bitwise_xor(expert, 4 * step)
    return dp, lax.bitwise_xor(expert, step)


def greet(peers):
    barrier = pltpu.get_barrier_semaphore()
    for device in peers:
        pl.semaphore_signal(barrier, inc=1, device_id=device, device_id_type=MESH)


def meet(peers):
    pl.semaphore_wait(pltpu.get_barrier_semaphore(), len(peers))


def dp_peers():
    dp, expert, _ = place_of()
    return [(lax.bitwise_xor(dp, k), expert) for k in range(1, 8)]


class Mover:
    def __init__(self, sems):
        self.sems, self.count = sems, 0

    def __call__(self, source, target):
        copy = pltpu.make_async_copy(source, target, self.sems.at[self.count])
        self.count += 1
        copy.start()
        return copy


class Sender:
    def __init__(self, send_sem, recv_sem):
        self.send_sem, self.recv_sem, self.count = send_sem, recv_sem, 0

    def __call__(self, source, target, device):
        copy = pltpu.make_async_remote_copy(
            src_ref=source,
            dst_ref=target,
            send_sem=self.send_sem.at[self.count],
            recv_sem=self.recv_sem.at[self.count],
            device_id=device,
            device_id_type=MESH,
        )
        self.count += 1
        copy.start()
        return copy


AXES = ("x", "y", "z")
CUBE = [("core", 1)] + [(axis, k) for axis in AXES for k in (1, 2, 3)]


def placed_rows(slot_row, slots):
    rows = slot_row.shape[1]
    slot = lax.broadcasted_iota(jnp.int32, (slots, rows), 0).astype(full)
    return jnp.where(slot == slot_row, 1.0, 0.0).astype(low_type)


def placed_of(table, slots):
    table = table.reshape(-1, table.shape[-1])
    return jnp.concatenate(
        [placed_rows(table[e : e + 1], slots) for e in range(table.shape[0])], axis=0
    )


class Reduce:
    ORDERS = (("x", "y", "z"), ("y", "z", "x"), ("z", "x", "y"), ("z", "x", "y"), ("x", "y", "z"))

    def __init__(self, given, scratch, send_sem, recv_sem):
        _, _, self.at = place_of()
        self.given = given
        self.core, self.half, self.row, self.going, self.total, self.last = (
            scratch[n : n + len(given)] for n in range(0, len(scratch), len(given))
        )
        self.send = Sender(send_sem, recv_sem)
        self.copies = {}

    def seat(self, n, axis, k):
        return lax.bitwise_xor(self.at[self.ORDERS[n][axis]], k)

    def peer(self, n, axis, k):
        return peer_on(self.ORDERS[n][axis], k)

    def cores(self, n):
        for k in (1, 2, 3, 0):
            a = self.seat(n, 0, k)
            piece = self.given[n].at[a, 1 - self.at["core"]]
            self.copies[n, 0, k] = self.send(piece, self.core[n].at[a], peer_on("core", 1))

    def pair(self, n, *place):
        a, *rest = place
        own, other = self.given[n][(a, self.at["core"], *rest)], self.core[n][place]
        return own.astype(full) + other.astype(full)

    def first(self, n):
        for k in (1, 2, 3):
            self.copies[n, 0, k].wait_recv()
            self.going[n][k - 1] = self.pair(n, self.seat(n, 0, k)).astype(low_type)
            self.copies[n, 1, k] = self.send(
                self.going[n].at[k - 1], self.half[n].at[k - 1], self.peer(n, 0, k)
            )

    def second(self, n):
        self.copies[n, 0, 0].wait_recv()
        for k in (1, 2, 3):
            self.copies[n, 1, k].wait()
        for k in (1, 2, 3, 0):
            b = self.seat(n, 1, k)
            value = self.pair(n, self.seat(n, 0, 0), b)
            for m in range(3):
                value += self.half[n][m, b].astype(full)
            if k:
                self.going[n][k - 1, 0] = value.astype(low_type)
                self.copies[n, 2, k] = self.send(
                    self.going[n].at[k - 1, 0], self.row[n].at[k - 1], self.peer(n, 1, k)
                )
            else:
                self.total[n][...] = value.reshape(self.total[n].shape)

    def third(self, n):
        for k in (1, 2, 3):
            self.copies[n, 2, k].wait()
        value = self.total[n][...].reshape(self.row[n].shape[1:])
        for m in range(3):
            value += self.row[n][m].astype(full)
        self.total[n][...] = value.reshape(self.total[n].shape)
        for k in (1, 2, 3):
            d = self.seat(n, 2, k)
            self.copies[n, 3, k] = self.send(
                self.total[n].at[d], self.last[n].at[k - 1], self.peer(n, 2, k)
            )

    def finish(self, n):
        for k in (1, 2, 3):
            self.copies[n, 3, k].wait()
        for k in range(4):
            self.copies[n, 0, k].wait_send()
        last = self.last[n]
        return self.total[n][self.seat(n, 2, 0)] + last[0] + last[1] + last[2]


PLANE = [(axis, k) for axis in ("y", "z") for k in (1, 2, 3)]


def spread_slots(send, move, tables, tokens_of, rows_bufs, out_ref):
    _, _, at = place_of()
    y, z = at["y"], at["z"]
    _, _, _, slots, half = rows_bufs[0].shape
    copies = []
    for k in range(4):
        for side, (rows, table, seat) in enumerate(zip(rows_bufs, tables, (y, z))):
            source = lax.bitwise_xor(seat, k)
            placed = placed_of(table[source], slots)
            rows[k] = dot(placed, tokens_of(side, k)).astype(low_type).reshape(rows.shape[1:])
            if side == 0:
                target = out_ref.at[source, z, :, :, pl.ds(0, half)]
            else:
                target = out_ref.at[y, source, :, :, pl.ds(half, half)]
            across, mine = ("z", z) if side == 0 else ("y", y)
            for n in (1, 2, 3):
                piece = rows.at[k, lax.bitwise_xor(mine, n)]
                copies.append(send(piece, target, peer_on(across, n)))
            copies.append(move(rows.at[k, mine], target))
    return copies


class Homeward:
    def __init__(self, send, move, back_ref, tables, held, going, came):
        _, _, at = place_of()
        self.seats = at["y"], at["z"]
        self.send, self.tables, self.held, self.going, self.came = send, tables, held, going, came
        self.first, self.local, self.second, self.kept = {}, {}, {}, {}
        y, z = self.seats
        half = held[0].shape[-1]
        sides = (pl.ds(0, half), pl.ds(half, half))
        for k in (1, 2, 3, 0):
            to_y, to_z = lax.bitwise_xor(y, k), lax.bitwise_xor(z, k)
            for n in (1, 2, 3):
                piece = back_ref.at[to_y, lax.bitwise_xor(z, n), :, :, sides[0]]
                self.first[0, k, n] = send(piece, held[0].at[k, n], peer_on("z", n))
                piece = back_ref.at[lax.bitwise_xor(y, n), to_z, :, :, sides[1]]
                self.first[1, k, n] = send(piece, held[1].at[k, n], peer_on("y", n))
            self.local[0, k] = move(back_ref.at[to_y, z, :, :, sides[0]], held[0].at[k, 0])
            self.local[1, k] = move(back_ref.at[y, to_z, :, :, sides[1]], held[1].at[k, 0])

    def add(self, k):
        for side, axis in ((0, "y"), (1, "z")):
            held, table = self.held[side], self.tables[side]
            seat, mine = self.seats[side], self.seats[1 - side]
            _, _, parts, slots, half = held.shape
            for n in (1, 2, 3):
                self.first[side, k, n].wait_recv()
            self.local[side, k].wait()
            source = lax.bitwise_xor(seat, k)
            total = jnp.zeros((table.shape[-1], half), full)
            for n in range(4):
                placed = placed_of(table[source, lax.bitwise_xor(mine, n)], slots)
                total += dot_tn(placed, held[k, n].reshape(parts * slots, half))
            if k:
                self.going[side][k - 1] = total.astype(low_type)
                self.second[side, k] = self.send(
                    self.going[side].at[k - 1], self.came[side].at[k - 1], peer_on(axis, k)
                )
            else:
                self.kept[side] = total

    def sums(self):
        for side in (0, 1):
            for k in (1, 2, 3):
                self.second[side, k].wait_recv()
        return jnp.concatenate(
            [
                self.kept[side] + sum(self.came[side][n].astype(full) for n in range(3))
                for side in (0, 1)
            ],
            axis=1,
        )

    def end(self):
        for copies in (self.first, self.second):
            for copy in copies.values():
                copy.wait_send()


def home_scratch(parts, slots, rows, half):
    return [pltpu.VMEM((4, 4, parts, slots, half), low_type)] * 2 + [
        pltpu.VMEM((3, rows, half), low_type)
    ] * 4


def by_place(values, axes):
    strides = dict(x=32, core=16, y=4, z=1)
    counts = dict(x=4, core=2, y=4, z=4)
    places = [0]
    for axis in axes:
        places = [p + n * strides[axis] for p in places for n in range(counts[axis])]
    return jnp.concatenate([values[p * 8 : p * 8 + 8] for p in places], axis=0)


def expert_rows(x, grad, in_w, down_w, router_w, mine_at, experts):
    half = down_w.shape[1]
    projected, logits, hidden_grad = dot(x, in_w), dot(x, router_w), dot(grad, down_w)
    gate_part, up = projected[:, :half], projected[:, half:]
    sigmoid = 1.0 / (1.0 + jnp.exp(-gate_part))
    silu = gate_part * sigmoid
    hidden = (silu * up).astype(low_type).astype(full)
    lane = lax.broadcasted_iota(jnp.int32, logits.shape, 1)
    logits = jnp.where(lane < experts, logits, masked_score)
    shifted = jnp.exp(logits - jnp.max(logits, axis=-1, keepdims=True))
    routing = shifted / jnp.sum(shifted, axis=-1, keepdims=True)
    mine = lane == mine_at
    chosen = jnp.sum(jnp.where(mine, routing, 0.0), axis=-1, keepdims=True)
    gate = chosen.astype(low_type).astype(full)
    gate_grad = jnp.sum(hidden * hidden_grad, axis=-1, keepdims=True)
    logit_grad = (gate_grad * chosen) * (jnp.where(mine, 1.0, 0.0) - routing)
    logit_grad = logit_grad.astype(low_type)
    hidden_grad = hidden_grad * gate
    gate_back = hidden_grad * up * (sigmoid * (1.0 + gate_part * (1.0 - sigmoid)))
    projected_grad = jnp.concatenate(
        [gate_back.astype(low_type), (hidden_grad * silu).astype(low_type)], axis=1
    )
    hidden = (hidden * gate).astype(low_type)
    made = dot_nt(hidden, down_w)
    back = dot_nt(projected_grad, in_w) + dot_nt(logit_grad, router_w)
    return made, back, projected_grad, hidden, logit_grad


def moe_kernel(experts, *refs):
    (att_ref, output_ref, tokens_ref, gains_ref, left_ref, right_ref, grad_ref, held_any, in_any, down_any, weights_any) = refs[:11]
    (mid_ref, made_ref, in_out, down_out, router_out, att_out, mid_grad_ref, low_ref, ffn_ref, att_grad_ref) = refs[11:21]
    (moe_buf, token_bufs, rows_bufs, x_buf, g_buf, p_buf, h_buf, l_buf, y_buf, in_w, down_w, router_w) = refs[21:33]
    (back_bufs, going, came, in_buf, down_buf, in_core, down_core, in_came, down_came) = refs[33:42]
    send_sem, recv_sem, back_send, back_recv, y_sem, local_sem = refs[42:]
    _, expert, at = place_of()
    x, y, z, c = at["x"], at["y"], at["z"], at["core"]
    tables = left_ref, right_ref
    seats = y, z
    rows, wide = mid_ref.shape
    half = wide // 2
    _, parts, _, _, slots, _ = rows_bufs.shape
    peers = [peer_on(axis, k) for axis, k in CUBE]
    greet(peers)
    move, send = Mover(local_sem), Sender(send_sem, recv_sem)
    loads = {
        ("g", 0): move(held_any.at[:, :, 0], g_buf),
        ("in", 0): move(in_any.at[0], in_w),
        ("down", 0): move(down_any.at[0], down_w),
        "router": move(weights_any.at[:, pl.ds(KV_HEADS * PACK, EXTRA)], router_w),
    }
    attended = jnp.concatenate([att_ref[g] for g in range(KV_HEADS)], axis=1)
    mid = tokens_ref[...].astype(full) + dot(attended, output_ref[...])
    mid_ref[...] = mid
    inverse = lax.rsqrt(jnp.mean(mid * mid, axis=-1, keepdims=True) + norm_eps)
    moe_buf[...] = (mid * inverse * gains_ref[1:2, :]).astype(low_type)
    meet(peers)
    along = {}
    for k in (1, 2, 3):
        for side, axis in ((0, "y"), (1, "z")):
            piece = moe_buf.at[:, pl.ds(side * half, half)]
            along[side, k] = send(piece, token_bufs.at[side, k - 1], peer_on(axis, k))
    spread = [[] for _ in range(parts)]

    def spread_part(k, j):
        for side, across in ((0, "z"), (1, "y")):
            source, mine = lax.bitwise_xor(seats[side], k), seats[1 - side]
            cols = pl.ds(side * half, half)
            place = (source, z) if side == 0 else (y, source)
            target = x_buf.at[(j, *place, slice(None), cols)]
            for n in (1, 2, 3):
                piece = rows_bufs.at[side, j, k, lax.bitwise_xor(mine, n)]
                spread[j].append(send(piece, target, peer_on(across, n)))
            x_buf[(j, *place, slice(None), cols)] = rows_bufs[side, j, k, mine]

    for k in range(4):
        for side in (0, 1):
            source = lax.bitwise_xor(seats[side], k)
            placed = placed_of(tables[side][source], slots)
            if k:
                along[side, k].wait_recv()
                tokens = token_bufs[side, k - 1]
            else:
                tokens = moe_buf[:, side * half : (side + 1) * half]
            value = dot(placed, tokens).astype(low_type).reshape(4, parts, slots, half)
            for j in range(parts):
                rows_bufs[side, j, k] = value[:, j]
        spread_part(k, 0)
    for k in range(4):
        for j in range(1, parts):
            spread_part(k, j)
    att_out[...] = by_place(flip(attended), ("z", "core", "x", "y")).astype(low_type)
    loads["router"].wait()

    def back_copy(side, j, k, n):
        if side == 0:
            place = (lax.bitwise_xor(y, k), lax.bitwise_xor(z, n))
        else:
            place = (lax.bitwise_xor(y, n), lax.bitwise_xor(z, k))
        number = ((side * parts + j) * 4 + k) * 3 + n - 1
        return pltpu.make_async_remote_copy(
            src_ref=rows_bufs.at[(side, j, *place)],
            dst_ref=back_bufs.at[side, k, n - 1, j],
            send_sem=back_send.at[number],
            recv_sem=back_recv.at[number],
            device_id=peer_on(("z", "y")[side], n),
            device_id_type=MESH,
        )

    def y_copy(slot, there, j):
        return pltpu.make_async_copy(y_buf.at[slot], made_ref.at[there, :, j], y_sem.at[slot])

    def experts_job(j):
        for copy in spread[j]:
            copy.wait()
        for name in ("g", "in", "down"):
            loads[name, j].wait()

        for turn in range(4):
            k = (turn + 1) % 4
            there = lax.bitwise_xor(y, k)
            count = 4 * slots
            made, back, p, h, l = expert_rows(
                x_buf[j, there].reshape(count, wide),
                g_buf[there].reshape(count, wide),
                in_w[...],
                down_w[...],
                router_w[...],
                parts * expert + j,
                experts,
            )
            slot = turn % 2
            if turn >= 2:
                y_copy(slot, lax.bitwise_xor(y, (turn - 1) % 4), j).wait()
            y_buf[slot] = made.astype(low_type).reshape(y_buf.shape[1:])
            y_copy(slot, there, j).start()
            back = back.astype(low_type)
            for side in (0, 1):
                piece = back[:, side * half : (side + 1) * half]
                rows_bufs[side, j, there] = piece.reshape(4, slots, half)
            for n in (1, 2, 3):
                back_copy(0, j, k, n).start()
            if k:
                for other in range(4):
                    back_copy(1, j, other, k).start()
            p_buf[there] = p
            h_buf[there] = h
            l_buf[there] = l
        for turn in (2, 3):
            y_copy(turn % 2, lax.bitwise_xor(y, (turn + 1) % 4), j).wait()

    def stacked(values):
        return values.reshape(-1, values.shape[-1])

    def in_job(j):
        for n in range(wide // 256):
            cols = slice(n * 256, (n + 1) * 256)
            value = dot_tn(stacked(x_buf[j, :, :, :, cols]), stacked(p_buf[...])).astype(low_type)
            in_buf[j, n, 0] = value[:128]
            in_buf[j, n, 1] = value[128:]
        core_copies["in", j] = send(in_buf.at[j, :, 1 - c], in_core.at[j], peer_on("core", 1))

    def down_job(j):
        for n in range(wide // 256):
            cols = slice(n * 256, (n + 1) * 256)
            value = dot_tn(stacked(g_buf[:, :, :, cols]), stacked(h_buf[...])).astype(low_type)
            down_buf[j, n, 0] = value[:128]
            down_buf[j, n, 1] = value[128:]
            part = dot_tn(stacked(x_buf[j, :, :, :, cols]), stacked(l_buf[...]))
            router_out[cols, :] = part if j == 0 else router_out[cols, :] + part
        core_copies["down", j] = send(
            down_buf.at[j, :, 1 - c], down_core.at[j], peer_on("core", 1)
        )

    core_copies, x_copies = {}, {}
    buffers = {
        "in": (in_buf, in_core, in_came, in_out),
        "down": (down_buf, down_core, down_came, down_out),
    }

    def across_job(name, j):
        own, core, came_x, _ = buffers[name]
        core_copies[name, j].wait_recv()
        for k in (1, 2, 3):
            there = lax.bitwise_xor(x, k)
            value = own[j, there, c].astype(full) + core[j, there].astype(full)
            own[j, there, c] = value.astype(low_type)
            x_copies[name, j, k] = send(
                own.at[j, there, c], came_x.at[j, k - 1], peer_on("x", k)
            )

    def total_job(name, j):
        own, core, came_x, out = buffers[name]
        value = own[j, x, c].astype(full) + core[j, x].astype(full)
        for k in (1, 2, 3):
            x_copies[name, j, k].wait_recv()
            value += came_x[j, k - 1].astype(full)
        out[j] = value

    second, kept = {}, {}

    def add_job(k):
        for side, axis in ((0, "y"), (1, "z")):
            seat, mine = seats[side], seats[1 - side]
            source = lax.bitwise_xor(seat, k)
            total = jnp.zeros((rows, half), full)
            for n in range(4):
                if n:
                    for j in range(parts):
                        back_copy(side, j, k, n).wait_recv()
                    piece = back_bufs[side, k, n - 1].reshape(parts * slots, half)
                else:
                    place = (source, z) if side == 0 else (y, source)
                    piece = jnp.concatenate(
                        [rows_bufs[(side, j, *place)] for j in range(parts)], axis=0
                    )
                placed = placed_of(tables[side][source, lax.bitwise_xor(mine, n)], slots)
                total += dot_tn(placed, piece)
            if k:
                going[side, k - 1] = total.astype(low_type)
                second[side, k] = send(
                    going.at[side, k - 1], came.at[side, k - 1], peer_on(axis, k)
                )
            else:
                kept[side] = total

    experts_job(0)
    for j in range(1, parts):
        loads["in", j] = move(in_any.at[j], in_w)
        loads["down", j] = move(down_any.at[j], down_w)
        in_job(j - 1)
        down_job(j - 1)
        loads["g", j] = move(held_any.at[:, :, j], g_buf)
        across_job("in", j - 1)
        across_job("down", j - 1)
        experts_job(j)
        in_job(j)
        down_job(j)
    add_job(1)
    across_job("in", parts - 1)
    add_job(2)
    across_job("down", parts - 1)
    add_job(3)
    add_job(0)
    sums = []
    for side in (0, 1):
        for k in (1, 2, 3):
            second[side, k].wait_recv()
        sums.append(kept[side] + sum(came[side, n].astype(full) for n in range(3)))
    moe_grad = jnp.concatenate(sums, axis=1)
    mid = mid_ref[...]
    inverse = lax.rsqrt(jnp.mean(mid * mid, axis=-1, keepdims=True) + norm_eps)
    scaled = moe_grad * gains_ref[1:2, :]
    shared = jnp.sum(scaled * mid, axis=-1, keepdims=True) * (inverse * inverse * inverse / wide)
    mid_grad = grad_ref[...].astype(full) + (scaled * inverse - mid * shared)
    mid_grad_ref[...] = mid_grad
    low = mid_grad.astype(low_type)
    low_ref[...] = low
    ffn_ref[...] = jnp.sum(mid * inverse * moe_grad, axis=0, keepdims=True)
    for g in range(KV_HEADS):
        att_grad_ref[g] = dot_nt(low, output_ref[g * PAIR : (g + 1) * PAIR, :]).astype(low_type)
    for j in range(parts):
        total_job("in", j)
        total_job("down", j)
    for copies in (along, second, core_copies, x_copies):
        for copy in copies.values():
            copy.wait_send()
    for side in (0, 1):
        for j in range(parts):
            for k in range(4):
                for n in (1, 2, 3):
                    back_copy(side, j, k, n).wait_send()


def moe_layer(att, output_proj, tokens, gains, left, right, grad, held, in_w, down_w, weights, experts, number):
    rows, wide = tokens.shape
    _, _, parts, slots, _ = held.shape
    half = wide // 2
    hidden = down_w.shape[2]
    shapes = [
        ((rows, wide), full),
        (held.shape, low_type),
        ((parts, wide // 8, 2 * hidden), full),
        ((parts, wide // 8, hidden), full),
        ((wide, EXTRA), full),
        ((wide, rows), low_type),
        ((rows, wide), full),
        ((rows, wide), low_type),
        ((1, wide), full),
        ((KV_HEADS, rows, PAIR), low_type),
    ]
    scratch = [
        (rows, wide),
        (2, 3, rows, half),
        (2, parts, 4, 4, slots, half),
        (parts, 4, 4, slots, wide),
        (4, 4, slots, wide),
        (4, 4 * slots, 2 * hidden),
        (4, 4 * slots, hidden),
        (4, 4 * slots, EXTRA),
        (2, 4, slots, wide),
        in_w.shape[1:],
        down_w.shape[1:],
        (wide, EXTRA),
        (2, 4, 3, parts, slots, half),
        (2, 3, rows, half),
        (2, 3, rows, half),
        (parts, 4, 2, wide // 8, 2 * hidden),
        (parts, 4, 2, wide // 8, hidden),
        (parts, 4, wide // 8, 2 * hidden),
        (parts, 4, wide // 8, hidden),
        (parts, 3, wide // 8, 2 * hidden),
        (parts, 3, wide // 8, hidden),
    ]
    copies = 6 + 24 * parts + 8 * parts + 6
    return pl.pallas_call(
        functools.partial(moe_kernel, experts),
        out_shape=[jax.ShapeDtypeStruct(*s) for s in shapes],
        in_specs=[VMEM] * 7 + [ANY] * 4,
        out_specs=[VMEM, ANY] + [VMEM] * 8,
        scratch_shapes=[
            *[pltpu.VMEM(s, low_type) for s in scratch],
            *[pltpu.SemaphoreType.DMA((copies,))] * 2,
            *[pltpu.SemaphoreType.DMA((24 * parts,))] * 2,
            pltpu.SemaphoreType.DMA((2,)),
            pltpu.SemaphoreType.DMA((3 * parts + 1,)),
        ],
        compiler_params=comm_params(number),
        cost_estimate=cost(120),
        name="moe_layer",
    )(att, output_proj, tokens, gains, left, right, grad, held, in_w, down_w, weights)


def allowed_of(shape, rows, length, i):
    key_at = lax.broadcasted_iota(jnp.int32, shape, 0)
    query_at = lax.broadcasted_iota(jnp.int32, shape, 1) % rows
    return (key_at <= query_at) & (key_at < length - i * rows)


def key_spread(width, wide):
    out = lax.broadcasted_iota(jnp.int32, (wide, width), 0)
    here = lax.broadcasted_iota(jnp.int32, (wide, width), 1)
    return jnp.where(out == (here // 4) * 8 + here % 4, 1.0, 0.0).astype(low_type)


def hand_over(sent, home, send_sem, recv_sem, i):
    dp, expert, _ = place_of()
    k = lax.bitwise_xor(dp, i)
    return pltpu.make_async_remote_copy(
        src_ref=sent.at[i],
        dst_ref=home.at[dp],
        send_sem=send_sem.at[k],
        recv_sem=recv_sem.at[k],
        device_id=(i, expert),
        device_id_type=MESH,
    )


def gather_weights(
    at, meet_all, query_ref, key_ref, value_ref, router_ref, gains_row, slot_a, slot_b, master_ref, buf, third, got_a, got_b,
    shard_ref, shards_ref, mine_ref, others_ref, ours_ref, send,
):
    x, y, z, c = at["x"], at["y"], at["z"], at["core"]
    rows, columns = shard_ref.shape
    cut = columns // 256 * 128
    sides = (pl.ds(0, cut), pl.ds(cut, columns - cut))
    for g in range(KV_HEADS):
        here = g * PACK
        shard_ref[:, here : here + PAIR] = query_ref[:, g * PAIR : (g + 1) * PAIR]
        head = slice(g * HEAD_DIM, (g + 1) * HEAD_DIM)
        shard_ref[:, here + PAIR : here + PACK] = jnp.concatenate(
            [key_ref[:, head], value_ref[:, head]], axis=1
        )
    experts = router_ref.shape[1]
    lane = lax.broadcasted_iota(jnp.int32, (rows, EXTRA), 1)
    row = lax.broadcasted_iota(jnp.int32, (rows, EXTRA), 0)
    gains = jnp.broadcast_to(gains_row, (rows, EXTRA))
    extra = jnp.concatenate(
        [router_ref[...], jnp.zeros((rows, EXTRA - experts), full)], axis=1
    )
    for n in range(4):
        column = jnp.sum(jnp.where(lane == row + n * rows, gains, 0.0), axis=1, keepdims=True)
        extra += jnp.where(lane == experts + n, column, 0.0)
    shard_ref[:, KV_HEADS * PACK :] = extra
    meet_all()
    first = [send(shard_ref, shards_ref.at[z], peer_on("z", k)) for k in (1, 2, 3)]
    first += [send(master_ref, others_ref.at[x], peer_on("x", k)) for k in (1, 2, 3)]
    shards_ref[z] = shard_ref[...]
    others_ref[x] = master_ref[...]
    slots = []
    for k in (1, 2, 3):
        slots.append(send(slot_a.at[lax.bitwise_xor(y, k)], got_a.at[y], peer_on("y", k)))
        slots.append(send(slot_b.at[lax.bitwise_xor(z, k)], got_b.at[z], peer_on("z", k)))
    got_a[y] = slot_a[y]
    got_b[z] = slot_b[z]
    for copy in first:
        copy.wait()
    mine = shards_ref[...].reshape(mine_ref.shape).astype(low_type)
    mine_ref[...] = mine
    buf[x, c, y] = mine
    ours = others_ref[...].reshape(ours_ref.shape).astype(low_type)
    ours_ref[...] = ours
    third[z, c, y] = ours
    second = []
    for k in (1, 2, 3):
        for side, axis in ((0, "y"), (1, "x")):
            second.append(
                send(
                    mine_ref.at[:, sides[side]],
                    buf.at[x, c, y, :, sides[side]],
                    peer_on(axis, k),
                )
            )
        second.append(send(ours_ref, third.at[z, c, y], peer_on("y", k)))
    for copy in second:
        copy.wait()
    final = []
    for k in (1, 2, 3):
        piece = buf.at[x, c, :, :, sides[0]]
        final.append(send(piece, piece, peer_on("x", k)))
        piece = buf.at[:, c, y, :, sides[1]]
        final.append(send(piece, piece, peer_on("y", k)))
        piece = third.at[z, c]
        final.append(send(piece, piece, peer_on("z", k)))
    other = peer_on("core", 1)
    last = []
    for piece in (buf.at[x, c, :, :, sides[0]], buf.at[:, c, y, :, sides[1]], third.at[z, c]):
        last.append(send(piece, piece, other))
    for n, k in enumerate((1, 2, 3)):
        final[3 * n].wait_recv()
        piece = buf.at[lax.bitwise_xor(x, k), c, :, :, sides[0]]
        last.append(send(piece, piece, other))
        final[3 * n + 1].wait_recv()
        piece = buf.at[:, c, lax.bitwise_xor(y, k), :, sides[1]]
        last.append(send(piece, piece, other))
        final[3 * n + 2].wait_recv()
        piece = third.at[lax.bitwise_xor(z, k), c]
        last.append(send(piece, piece, other))
    return slots, final, last


def forward_kernel(
    length_ref, query_ref, key_ref, value_ref, router_ref, gains_row, slot_a, slot_b, master_ref, tokens_ref, cos_ref, sin_ref, grad_ref,
    weights_out, rows_ref, output_ref, normed_rows, raw_ref, pack_ref, gains_ref, held_ref, att_ref, log_ref, home_ref, left_ref, right_ref,
    shard_ref, shards_ref, mine_ref, others_ref, ours_ref, weights_ref, third_buf,
    grad_bufs, rows_a, rows_b, sent, flip_ref, score_ref,
    gather_send, gather_recv, send_one, recv_one, send_two, recv_two, send_sem, recv_sem, move_sem,
):
    dp, _, at = place_of()
    y, z = at["y"], at["z"]
    peers = dp_peers() + [peer_on(axis, k) for axis, k in PLANE]
    greet(peers)
    blocks, rows = held_ref.shape[0], held_ref.shape[1]
    wide = tokens_ref.shape[1]
    width = KV_HEADS * HEAD_DIM
    half = wide // 2
    slots_sent, final, last = gather_weights(
        at, lambda: meet(peers), query_ref, key_ref, value_ref, router_ref, gains_row[...], slot_a, slot_b, master_ref,
        weights_ref, third_buf, left_ref, right_ref, shard_ref, shards_ref, mine_ref, others_ref, ours_ref,
        Sender(gather_send, gather_recv),
    )
    send, move = Sender(send_sem, recv_sem), Mover(move_sem)
    along = {}
    for k in (1, 2, 3):
        for side, axis in ((0, "y"), (1, "z")):
            piece = grad_ref.at[:, pl.ds(side * half, half)]
            along[side, k] = send(piece, grad_bufs.at[side, k - 1], peer_on(axis, k))
    for copy in last:
        copy.wait()
    stored = move(weights_ref, weights_out)

    def weights_of(start, count):
        return weights_ref[..., start : start + count].reshape(wide, count)

    extra = flip(weights_of(KV_HEADS * PACK, EXTRA))
    gains_ref[0:1, :] = extra[32:33]
    gains_ref[1:2, :] = extra[34:35]
    key_gain = dot(
        jnp.broadcast_to(extra[35:36], (8, wide)).astype(low_type), key_spread(width, wide)
    )[:1]
    for g in range(KV_HEADS):
        pack_ref[g, :, :PAIR] = extra[33:34, g * PAIR : (g + 1) * PAIR]
        pack_ref[g, :, PAIR:] = jnp.concatenate(
            [key_gain[:, g * HEAD_DIM : (g + 1) * HEAD_DIM], jnp.ones((1, HEAD_DIM), full)],
            axis=1,
        )
    values = tokens_ref[...].astype(full)
    inverse = lax.rsqrt(jnp.mean(values * values, axis=-1, keepdims=True) + norm_eps)
    normed = (values * inverse * gains_ref[0:1, :]).astype(low_type)
    query_sum = jnp.zeros((rows, PAIR), full)
    key_sum = jnp.zeros((rows, PAIR), full)
    for g in range(KV_HEADS):
        raw = dot(normed, weights_of(g * PACK, PACK))
        raw_ref[g] = raw
        query_sum += raw[:, :PAIR] * raw[:, :PAIR]
        key_sum += raw[:, PAIR:] * raw[:, PAIR:]
    is_key = lax.broadcasted_iota(jnp.int32, key_sum.shape, 1) < HEAD_DIM
    query_inv = lax.rsqrt(
        jnp.sum(query_sum, axis=-1, keepdims=True) / (GROUP * width) + norm_eps
    )
    key_inv = lax.rsqrt(
        jnp.sum(jnp.where(is_key, key_sum, 0.0), axis=-1, keepdims=True) / width + norm_eps
    )
    pair_inv = jnp.where(is_key, key_inv, 1.0)
    handed = []
    for k in (1, 2, 3, 4, 5, 6, 7, 0):
        g = lax.bitwise_xor(dp, k)
        target = sent if k else held_ref
        for part, scale in ((0, query_inv), (1, pair_inv)):
            here = slice(part * PAIR, (part + 1) * PAIR)
            scaled = raw_ref[g, :, here] * scale * pack_ref[g, :, here]
            turned = scaled * cos_ref[:, here] + partner(scaled) * sin_ref[:, here]
            target[g, :, here] = turned.astype(low_type)
        if k:
            handed.append(hand_over(sent, held_ref, send_one, recv_one, g))
            handed[-1].start()
    def tokens_of(side, k):
        if k == 0:
            return grad_ref[:, side * half : (side + 1) * half]
        along[side, k].wait_recv()
        return grad_bufs[side, k - 1]

    for copy in slots_sent:
        copy.wait()
    spread = spread_slots(
        send, move, (left_ref, right_ref), tokens_of, (rows_a, rows_b), rows_ref
    )
    wide_query = GROUP * rows
    flat = flip(normed)
    normed_rows[0] = flat.astype(low_type)
    normed_rows[1] = by_place(flat, ("y", "core", "z", "x")).astype(low_type)
    normed_rows[2] = by_place(flat, ("z", "core", "x", "y")).astype(low_type)
    for n in range(4):
        pieces = [
            third_buf[p, m // 4, m % 4, n * 8 : n * 8 + 8, :].astype(full)
            for m in range(8)
            for p in range(4)
        ]
        output_ref[n * 256 : (n + 1) * 256, :] = jnp.concatenate(pieces, axis=0).astype(low_type)

    for i in range(blocks):

        @pl.when(i != dp)
        def _():
            hand_over(sent, held_ref, send_one, recv_one, i).wait_recv()

        span = slice(i * rows, (i + 1) * rows)
        flip_ref[:, span] = flip(held_ref[i, :, PAIR + HEAD_DIM :]).astype(low_type)
        query = flip(held_ref[i, :, :PAIR]).astype(low_type)
        query = jnp.concatenate([query[:HEAD_DIM], query[HEAD_DIM:]], axis=1)
        top = jnp.full((1, wide_query), masked_score, full)
        for j in range(i + 1):
            scores = dot(held_ref[j, :, PAIR : PAIR + HEAD_DIM], query) * score_scale
            if j == i:
                allowed = allowed_of(scores.shape, rows, length_ref[0], i)
                scores = jnp.where(allowed, scores, masked_score)
            score_ref[j * rows : (j + 1) * rows] = scores
            top = jnp.maximum(top, jnp.max(scores, axis=0, keepdims=True))
        soft = jnp.exp(score_ref[: (i + 1) * rows] - top)
        total = jnp.sum(soft, axis=0, keepdims=True)
        acc = dot(flip_ref[:, : (i + 1) * rows], soft.astype(low_type)) / total
        both = jnp.concatenate([acc[:, :rows], acc[:, rows:]], axis=0)
        att_ref[i] = both.T.astype(low_type)
        log_ref[i] = jnp.broadcast_to(top + jnp.log(total), log_ref.shape[1:])

        @pl.when(i != dp)
        def _():
            hand_over(att_ref, home_ref, send_two, recv_two, i).start()

        @pl.when(i == dp)
        def _():
            home_ref[i] = att_ref[i]

    for copy in handed:
        copy.wait_send()
    for copy in spread:
        copy.wait()
    for copies in (along.values(), final):
        for copy in copies:
            copy.wait_send()
    stored.wait()
    for k in range(1, 8):
        hand_over(att_ref, home_ref, send_two, recv_two, lax.bitwise_xor(dp, k)).wait()


def forward(lengths, masters, gains_row, slot_a, slot_b, tokens, cosine, sine, grad, slots, number):
    rows, wide = tokens.shape
    query, key, value, output, router = masters
    share, columns = query.shape[0], KV_HEADS * PACK + EXTRA
    _, _, parts, _ = slot_a.shape
    shapes = [
        ((4, 2, 4, 4 * share, columns), low_type),
        ((4, 4, parts, slots, wide), low_type),
        ((wide, wide), low_type),
        ((3, wide, rows), low_type),
        ((KV_HEADS, rows, PACK), full),
        ((KV_HEADS, 1, PACK), full),
        ((8, wide), full),
        ((8, rows, PACK), low_type),
        ((8, rows, PAIR), low_type),
        ((8, 8, GROUP * rows), full),
        ((KV_HEADS, rows, PAIR), low_type),
        (slot_a.shape, full),
        (slot_b.shape, full),
    ]
    return pl.pallas_call(
        forward_kernel,
        out_shape=[jax.ShapeDtypeStruct(*s) for s in shapes],
        in_specs=[SMEM] + [VMEM] * 12,
        out_specs=[ANY] * 2 + [VMEM] * (len(shapes) - 2),
        scratch_shapes=[
            pltpu.VMEM((share, columns), full),
            pltpu.VMEM((4, share, columns), full),
            pltpu.VMEM((4 * share, columns), low_type),
            pltpu.VMEM((4, share, wide), full),
            pltpu.VMEM((4 * share, wide), low_type),
            pltpu.VMEM((4, 2, 4, 4 * share, columns), low_type),
            pltpu.VMEM((4, 2, 4, 4 * share, wide), low_type),
            pltpu.VMEM((2, 3, rows, wide // 2), low_type),
            pltpu.VMEM((4, 4, parts, slots, wide // 2), low_type),
            pltpu.VMEM((4, 4, parts, slots, wide // 2), low_type),
            pltpu.VMEM((KV_HEADS, rows, PACK), low_type),
            pltpu.VMEM((HEAD_DIM, 8 * rows), low_type),
            pltpu.VMEM((8 * rows, GROUP * rows), full),
            *[pltpu.SemaphoreType.DMA((42,))] * 2,
            *[pltpu.SemaphoreType.DMA((8,))] * 4,
            *[pltpu.SemaphoreType.DMA((30,))] * 2,
            pltpu.SemaphoreType.DMA((9,)),
        ],
        compiler_params=comm_params(number),
        cost_estimate=cost(75),
        name="forward",
    )(lengths, query, key, value, router, gains_row, slot_a, slot_b, output, tokens, cosine, sine, grad)


def backward_kernel(
    length_ref, held_ref, arrive, grad_ref, att_ref, log_ref, home_ref, sent, flip_ref, sum_ref, back_ref, send_sem, recv_sem
):
    dp, _, _ = place_of()
    blocks, rows = held_ref.shape[0], held_ref.shape[1]
    for j in range(blocks):
        flip_ref[:, j * rows : (j + 1) * rows] = flip(held_ref[j, :, PAIR:])[:HEAD_DIM].astype(
            low_type
        )
    none = jnp.zeros((rows, HEAD_DIM), low_type)
    key_scale = jnp.where(
        lax.broadcasted_iota(jnp.int32, (rows, PAIR), 1) < HEAD_DIM, score_scale, 1.0
    )

    def heads_beside(values):
        return jnp.concatenate([values[:HEAD_DIM], values[HEAD_DIM:]], axis=1)

    for i in range(blocks - 1, -1, -1):
        arrive(i)
        query_rows = held_ref[i, :, :PAIR]
        grad_rows = grad_ref[i]
        query = heads_beside(flip(query_rows)).astype(low_type)
        grad_full = heads_beside(flip(grad_rows))
        grad = grad_full.astype(low_type)
        inner = jnp.sum(grad_full * heads_beside(flip(att_ref[i])), axis=0, keepdims=True)
        log_total = log_ref[i, :1, :]
        query_side = jnp.concatenate(
            [
                jnp.concatenate([query_rows[:, :HEAD_DIM], none], axis=1),
                jnp.concatenate([query_rows[:, HEAD_DIM:], none], axis=1),
            ],
            axis=0,
        )
        grad_side = jnp.concatenate(
            [
                jnp.concatenate([none, grad_rows[:, :HEAD_DIM]], axis=1),
                jnp.concatenate([none, grad_rows[:, HEAD_DIM:]], axis=1),
            ],
            axis=0,
        )
        for j in range(i + 1):
            key = held_ref[j, :, PAIR : PAIR + HEAD_DIM]
            value = held_ref[j, :, PAIR + HEAD_DIM :]
            soft = jnp.exp(dot(key, query) * score_scale - log_total)
            if j == i:
                allowed = allowed_of(soft.shape, rows, length_ref[0], i)
                soft = jnp.where(allowed, soft, 0.0)
            score_grad = (soft * (dot(value, grad) - inner)).astype(low_type)
            back_ref[j * rows : (j + 1) * rows] = score_grad
            part = dot(score_grad, query_side) + dot(soft.astype(low_type), grad_side)
            sum_ref[j] = part if i == blocks - 1 else sum_ref[j] + part
        acc = dot(flip_ref[:, : (i + 1) * rows], back_ref[: (i + 1) * rows])
        both = jnp.concatenate([acc[:, :rows], acc[:, rows:]], axis=0) * score_scale
        sent[i, :, :PAIR] = both.T.astype(low_type)
        sent[i, :, PAIR:] = (sum_ref[i] * key_scale).astype(low_type)

        @pl.when(i != dp)
        def _():
            hand_over(sent, home_ref, send_sem, recv_sem, i).start()

        @pl.when(i == dp)
        def _():
            home_ref[i] = sent[i]


def tail_kernel(
    length_ref, held_ref, own_ref, att_ref, log_ref, pack_ref, gains_ref, left_ref, right_ref, made_ref, *refs
):
    given, refs = refs[:12], refs[12:]
    (output_ref, tokens_ref, *sums), refs = refs[:7], refs[7:]
    here, refs = refs[:12], refs[12:]
    held, going, came, refs = refs[0:2], refs[2:4], refs[4:6], refs[6:]
    (grad_ref, home, sent, flip_ref, sum_ref, back_ref, low_ref), refs = refs[:7], refs[7:]
    pieces, reduce_scratch, refs = refs[:5], refs[5:35], refs[35:]
    send_zero, recv_zero, send_one, recv_one, send_two, recv_two, send_three, recv_three, local_sem = refs
    dp, _, _ = place_of()
    peers = dp_peers() + [peer_on(axis, k) for axis, k in PLANE]
    greet(peers)
    move = Mover(local_sem)
    loads = [move(source, target) for source, target in zip(given, here)]
    att_rows, mid_low, raw, cos, sin, weights, normed, tokens, mid_grad, router, ffn, mid = here
    wide = tokens.shape[1]
    width = KV_HEADS * HEAD_DIM
    meet(peers)
    others = [lax.bitwise_xor(dp, k) for k in range(1, 8)]
    for g in others:
        hand_over(own_ref, grad_ref, send_zero, recv_zero, g).start()
    grad_ref[dp] = own_ref[dp]
    homeward = Homeward(
        Sender(send_two, recv_two), move, made_ref, (left_ref, right_ref), held, going, came
    )
    reduce = Reduce(pieces, reduce_scratch, send_three, recv_three)
    loads[0].wait()
    loads[1].wait()
    put_product(pieces[3], 0, att_rows[...], mid_low, 0, wide)
    reduce.cores(3)

    def arrive(i):
        @pl.when(i != dp)
        def _():
            hand_over(own_ref, grad_ref, send_zero, recv_zero, i).wait_recv()

    backward_kernel(
        length_ref, held_ref, arrive, grad_ref, att_ref, log_ref, home, sent, flip_ref, sum_ref, back_ref, send_one, recv_one
    )
    reduce.first(3)
    for load in loads[2:]:
        load.wait()
    for g in others:
        hand_over(sent, home, send_one, recv_one, g).wait()
    query_grad, key_grad = raw_gradients(home, raw, pack_ref, cos, sin, low_ref)
    for n in range(3):
        put_product(pieces[n], 0, normed[n], low_ref, CUTS[n], CUTS[n + 1] - CUTS[n])
        reduce.cores(n)
    for n in range(3):
        reduce.first(n)
    attn_grad = token_gradients(low_ref, weights, tokens, gains_ref, mid_grad, tokens_ref)
    key_wide = dot_nt(
        jnp.broadcast_to(key_grad, (8, width)).astype(low_type), key_spread(width, wide)
    )[:1]
    extra = jnp.concatenate(
        [
            jnp.zeros((32, wide), full),
            attn_grad,
            query_grad,
            ffn[...],
            key_wide,
            jnp.zeros((EXTRA - 36, wide), full),
        ],
        axis=0,
    )
    extra = (extra.T + router[...]).astype(low_type)
    pieces[4][...] = extra.reshape(pieces[4].shape)
    reduce.cores(4)
    homeward.add(1)
    reduce.first(4)
    reduce.second(3)
    homeward.add(2)
    homeward.add(3)
    order = (0, 1, 2, 3, 4)
    for n in (0, 1, 2, 4):
        reduce.second(n)
    homeward.add(0)
    for n in order:
        reduce.third(n)
    output_ref[...] = (mid[...] + homeward.sums()).astype(low_type)
    for n in order:
        sums[n][...] = reduce.finish(n)
    homeward.end()
    for g in others:
        hand_over(own_ref, grad_ref, send_zero, recv_zero, g).wait_send()


def tail(lengths, held, grad, att, logs, pack, gains, left, right, made, given, number):
    blocks, rows, _ = held.shape
    _, _, parts, slots, wide = made.shape
    widths = tuple(CUTS[n + 1] - CUTS[n] for n in range(3)) + (wide, EXTRA)

    def each(*shape, kind=low_type):
        return [pltpu.VMEM(shape + (w,), kind) for w in widths]

    return pl.pallas_call(
        tail_kernel,
        out_shape=[
            jax.ShapeDtypeStruct((rows, wide), low_type),
            jax.ShapeDtypeStruct((rows, wide), low_type),
            *[jax.ShapeDtypeStruct((8, w), full) for w in widths],
        ],
        in_specs=[SMEM] + [VMEM] * 8 + [ANY] * 13,
        out_specs=[VMEM] * 7,
        scratch_shapes=[
            *[pltpu.VMEM(v.shape, v.dtype) for v in given],
            *home_scratch(parts, slots, rows, wide // 2),
            pltpu.VMEM((blocks, rows, PAIR), low_type),
            pltpu.VMEM((KV_HEADS, rows, PACK), low_type),
            pltpu.VMEM((blocks, rows, PACK), low_type),
            pltpu.VMEM((HEAD_DIM, blocks * rows), low_type),
            pltpu.VMEM((blocks, rows, PAIR), full),
            pltpu.VMEM((blocks * rows, GROUP * rows), low_type),
            pltpu.VMEM((rows, KV_HEADS * PACK), low_type),
            *each(4, 2, 4, 32),
            *each(4, 4, 32),
            *each(3, 4, 32),
            *each(3, 32),
            *each(3, 4, 32),
            *each(4, 8, kind=full),
            *each(3, 8, kind=full),
            *[pltpu.SemaphoreType.DMA((8,))] * 4,
            *[pltpu.SemaphoreType.DMA((30,))] * 2,
            *[pltpu.SemaphoreType.DMA((13 * len(widths),))] * 2,
            pltpu.SemaphoreType.DMA((20,)),
        ],
        compiler_params=comm_params(number),
        cost_estimate=cost(90),
        name="tail",
    )(
        lengths, held, grad, att, logs, pack, gains, left, right,
        made, *given,
    )


def finish_kernel(
    first_ref, second_ref, third_ref, last_ref, extra_ref, in_ref, down_ref,
    query_ref, key_ref, value_ref, out_proj_ref, router_ref, attn_ref, ffn_ref, query_gain_ref, key_gain_ref, in_out, down_out,
):
    in_out[...] = in_ref[...]
    down_out[...] = down_ref[...]
    out_proj_ref[...] = last_ref[...]
    for n, ref in enumerate((first_ref, second_ref, third_ref)):
        for start in range(CUTS[n], CUTS[n + 1], PACK):
            g = start // PACK
            piece = ref[:, start - CUTS[n] : start - CUTS[n] + PACK]
            head = slice(g * HEAD_DIM, (g + 1) * HEAD_DIM)
            query_ref[:, g * PAIR : (g + 1) * PAIR] = piece[:, :PAIR]
            key_ref[:, head] = piece[:, PAIR : PAIR + HEAD_DIM]
            value_ref[:, head] = piece[:, PAIR + HEAD_DIM :]
    extra = extra_ref[...]
    experts = router_ref.shape[1]
    router_ref[...] = extra[:, :experts]
    rows = extra.shape[0]
    lane = lax.broadcasted_iota(jnp.int32, (rows, rows), 1)
    row = lax.broadcasted_iota(jnp.int32, (rows, rows), 0)
    for n, ref in enumerate((attn_ref, query_gain_ref, ffn_ref, key_gain_ref)):
        column = jnp.broadcast_to(extra[:, experts + n : experts + n + 1], (rows, rows))
        flat = jnp.sum(jnp.where(lane == row, column, 0.0), axis=0, keepdims=True)
        ref[...] = flat[:, : ref.shape[1]]


def raw_gradients(back_ref, raw_ref, pack_ref, cos_ref, sin_ref, low_ref):
    rows = back_ref.shape[1]
    width = KV_HEADS * HEAD_DIM
    is_key = lax.broadcasted_iota(jnp.int32, (rows, PAIR), 1) < HEAD_DIM
    sums = [[jnp.zeros((rows, PAIR), full) for _ in range(2)] for _ in range(2)]

    def here_of(part):
        return slice(part * PAIR, (part + 1) * PAIR)

    def unturned(g, part):
        here = here_of(part)
        grad = back_ref[g, :, here].astype(full)
        return grad * cos_ref[:, here] - partner(grad) * sin_ref[:, here]

    for g in range(KV_HEADS):
        for part in range(2):
            raw = raw_ref[g, :, here_of(part)]
            sums[part][0] += raw * raw
            sums[part][1] += raw * unturned(g, part) * pack_ref[g, :, here_of(part)]
    mean_of = [GROUP * width, width]
    inverses, shares = [], []
    for part in range(2):
        square, cross = sums[part]
        if part == 1:
            square, cross = jnp.where(is_key, square, 0.0), jnp.where(is_key, cross, 0.0)
        inverse = lax.rsqrt(jnp.sum(square, axis=-1, keepdims=True) / mean_of[part] + norm_eps)
        share = jnp.sum(cross, axis=-1, keepdims=True) * (
            inverse * inverse * inverse / mean_of[part]
        )
        if part == 1:
            inverse = jnp.where(is_key, inverse, 1.0)
            share = jnp.where(is_key, share, 0.0)
        inverses.append(inverse)
        shares.append(share)
    gains = [[], []]
    for g in range(KV_HEADS):
        for part in range(2):
            raw = raw_ref[g, :, here_of(part)]
            grad = unturned(g, part)
            gains[part].append(jnp.sum(raw * inverses[part] * grad, axis=0, keepdims=True))
            result = grad * pack_ref[g, :, here_of(part)] * inverses[part] - raw * shares[part]
            start = g * PACK + part * PAIR
            low_ref[:, start : start + PAIR] = result.astype(low_type)
    query_grad = jnp.concatenate(gains[0], axis=1)
    key_grad = jnp.concatenate(
        [
            jnp.concatenate(
                [gains[1][2 * g][:, :HEAD_DIM], gains[1][2 * g + 1][:, :HEAD_DIM]], axis=1
            )
            for g in range(KV_HEADS // 2)
        ],
        axis=1,
    )
    return query_grad, key_grad


def token_gradients(low_ref, weights_ref, tokens_ref, gains_ref, mid_grad_ref, out_ref):
    normed_grad = dot_nt(low_ref[...], weights_ref[:, : KV_HEADS * PACK])
    values = tokens_ref[...].astype(full)
    wide = values.shape[1]
    inverse = lax.rsqrt(jnp.mean(values * values, axis=-1, keepdims=True) + norm_eps)
    scaled = normed_grad * gains_ref[0:1, :]
    share = jnp.sum(scaled * values, axis=-1, keepdims=True) * (
        inverse * inverse * inverse / wide
    )
    out_ref[...] = (mid_grad_ref[...] + (scaled * inverse - values * share)).astype(low_type)
    return jnp.sum(values * inverse * normed_grad, axis=0, keepdims=True)


def put_product(ref, start, left, right_ref, at, count):
    places = ref.shape[:-1]
    for n in range(0, count, 256):
        value = dot(left, right_ref[:, at + n : at + n + 256]).astype(low_type)
        ref[..., start + n : start + n + 256] = value.reshape(places + (256,))


def on_device(
    tokens_in,
    lengths,
    routes,
    w_query,
    w_key,
    w_value,
    w_output,
    w_router,
    attn_gain,
    ffn_gain,
    query_gain,
    key_gain,
    expert_in,
    expert_down,
    out_grad,
):
    rows, wide = tokens_in.shape[1], tokens_in.shape[2]
    experts = w_router.shape[1]
    parts = expert_in.shape[0]
    owners = experts // parts
    slots = 5 * rows * routes.shape[2] // (4 * experts)
    tokens = tokens_in[0]
    grad_out = out_grad[0]

    place = lax.axis_index("dp") * rows + jnp.arange(rows)
    valid = (place < lengths[0]).astype(jnp.int32)
    ids = jnp.arange(experts)
    chosen = (
        jnp.sum((routes[0][:, :, None] == ids[None, None, :]).astype(jnp.int32), axis=1)
        * valid[:, None]
    )
    earlier = jnp.cumsum(chosen, axis=0) - chosen
    slot_of = jnp.where(chosen == 1, earlier, -1).T.astype(full)

    lane = jnp.arange(PACK)
    frequency = rope_base ** (
        -2.0 * (lane % (HEAD_DIM // 2)).astype(full) / HEAD_DIM
    )
    angles = place.astype(full)[:, None] * frequency[None, :]
    turning = (lane < PAIR + HEAD_DIM)[None, :]
    cosine = jnp.where(turning, jnp.cos(angles), 1.0)
    sign = jnp.where(lane % HEAD_DIM < HEAD_DIM // 2, -1.0, 1.0)
    sine = jnp.where(turning, jnp.sin(angles) * sign, 0.0)

    gains = jnp.concatenate([attn_gain, query_gain, ffn_gain, key_gain])
    gains = jnp.pad(gains, (0, EXTRA - gains.shape[0]))[None]
    slot_a = slot_of.reshape(4, 4, parts, rows)
    slot_b = slot_a.transpose(1, 0, 2, 3)
    (weights, grad_held, output_proj, normed_rows, raw, pack_row, gain_rows, held, att, logs, att_home, left, right) = forward(
        lengths, (w_query, w_key, w_value, w_output, w_router), gains, slot_a, slot_b, tokens, cosine, sine, grad_out, slots, 1
    )
    weights = weights.reshape(wide, KV_HEADS * PACK + EXTRA)
    mid, made, in_grad, down_grad, router_grad, att_rows, mid_grad, mid_low, ffn_grad, att_grad = moe_layer(
        att_home, output_proj, tokens, gain_rows, left, right, grad_out, grad_held, expert_in, expert_down, weights, experts, 2
    )
    output, grad_tokens, *sums = tail(
        lengths, held, att_grad, att, logs, pack_row, gain_rows, left, right, made,
        (att_rows, mid_low, raw, cosine, sine, weights, normed_rows, tokens, mid_grad, router_grad, ffn_grad, mid), 3,
    )
    shapes = [
        (w_query.shape, full),
        (w_key.shape, full),
        (w_value.shape, full),
        (w_output.shape, full),
        (w_router.shape, full),
        ((1, attn_gain.shape[0]), full),
        ((1, ffn_gain.shape[0]), full),
        ((1, query_gain.shape[0]), full),
        ((1, key_gain.shape[0]), full),
        (in_grad.shape, full),
        (down_grad.shape, full),
    ]
    results = pl.pallas_call(
        finish_kernel,
        out_shape=[jax.ShapeDtypeStruct(*s) for s in shapes],
        in_specs=[VMEM] * 7,
        out_specs=[VMEM] * len(shapes),
        name="finish",
        **params(2),
    )(*sums, in_grad, down_grad)
    return (
        output[None],
        grad_tokens[None],
        *results[:5],
        *[row[0] for row in results[5:9]],
        *results[9:],
    )


def solution(mesh):
    in_specs = (
        P("expert", "dp", None),
        P("expert"),
        P("expert", "dp", None),
        P(("dp", "expert"), None),
        P(("dp", "expert"), None),
        P(("dp", "expert"), None),
        P(("dp", "expert"), None),
        P(("dp", "expert"), None),
        P(("dp", "expert")),
        P(("dp", "expert")),
        P(("dp", "expert")),
        P(("dp", "expert")),
        P("expert", None, None),
        P("expert", None, None),
        P("expert", "dp", None),
    )
    out_specs = (
        P("expert", "dp", None),
        P("expert", "dp", None),
        P(("dp", "expert"), None),
        P(("dp", "expert"), None),
        P(("dp", "expert"), None),
        P(("dp", "expert"), None),
        P(("dp", "expert"), None),
        P(("dp", "expert")),
        P(("dp", "expert")),
        P(("dp", "expert")),
        P(("dp", "expert")),
        P("expert", "dp", None),
        P("expert", "dp", None),
    )
    return jax.shard_map(
        on_device, mesh=mesh, in_specs=in_specs, out_specs=out_specs, check_vma=False
    )
```

```python
import functools

import jax
import jax.numpy as jnp
from jax import lax
from jax.experimental import pallas as pl
from jax.experimental.pallas import tpu as pltpu
from jax.sharding import PartitionSpec as P

HEADS = 16
HEAD_DIM = 64
KV_HEADS = 8
GROUP = HEADS // KV_HEADS
PAIR = GROUP * HEAD_DIM
PACK = PAIR + 2 * HEAD_DIM
EXTRA = 128
CUTS = (0, 4 * PACK, 6 * PACK, 8 * PACK)

norm_eps = 1e-06
rope_base = 10000.0
masked_score = -1e30
score_scale = HEAD_DIM ** (-0.5)
low_type = jnp.bfloat16
full = jnp.float32

VMEM = pl.BlockSpec(memory_space=pltpu.VMEM)
SMEM = pl.BlockSpec(memory_space=pltpu.SMEM)
LIMIT = 62 * 1024 * 1024


def dot(left, right):
    return jnp.dot(left, right, preferred_element_type=full)


def dot_nt(left, right):
    return lax.dot_general(left, right, (((1,), (1,)), ((), ())), preferred_element_type=full)


def dot_tn(left, right):
    return lax.dot_general(left, right, (((0,), (0,)), ((), ())), preferred_element_type=full)


def partner(values):
    lane = lax.broadcasted_iota(jnp.int32, values.shape, 1)
    half = HEAD_DIM // 2
    return jnp.where(
        lane % HEAD_DIM < half, pltpu.roll(values, 128 - half, 1), pltpu.roll(values, half, 1)
    )


def turning(cos_ref, sin_ref):
    cos, sin = cos_ref[...], sin_ref[...]
    is_key = lax.broadcasted_iota(jnp.int32, cos.shape, 1) < HEAD_DIM
    return (cos, sin), (jnp.where(is_key, cos, 1.0), jnp.where(is_key, sin, 0.0))


def flip(values):
    return values.astype(full).T


def cost(microseconds):
    return pl.CostEstimate(
        flops=int(microseconds * 1.15e9), bytes_accessed=1 << 20, transcendentals=0
    )


def params(microseconds):
    return dict(
        compiler_params=pltpu.CompilerParams(vmem_limit_bytes=LIMIT),
        cost_estimate=cost(microseconds),
    )


MESH = pl.DeviceIdType.MESH
ANY = pl.BlockSpec(memory_space=pl.ANY)


def comm_params(number):
    return pltpu.CompilerParams(
        collective_id=number, has_side_effects=True, vmem_limit_bytes=LIMIT
    )


def place_of():
    dp, expert = lax.axis_index("dp"), lax.axis_index("expert")
    return dp, expert, dict(x=dp // 2, core=dp % 2, y=expert // 4, z=expert % 4)


def peer_on(axis, step):
    dp, expert, _ = place_of()
    if axis == "core":
        return lax.bitwise_xor(dp, 1), expert
    if axis == "x":
        return lax.bitwise_xor(dp, 2 * step), expert
    if axis == "y":
        return dp, lax.bitwise_xor(expert, 4 * step)
    return dp, lax.bitwise_xor(expert, step)


def greet(peers):
    barrier = pltpu.get_barrier_semaphore()
    for device in peers:
        pl.semaphore_signal(barrier, inc=1, device_id=device, device_id_type=MESH)


def meet(peers):
    pl.semaphore_wait(pltpu.get_barrier_semaphore(), len(peers))


def dp_peers():
    dp, expert, _ = place_of()
    return [(lax.bitwise_xor(dp, k), expert) for k in range(1, 8)]


class Mover:
    def __init__(self, sems):
        self.sems, self.count = sems, 0

    def __call__(self, source, target):
        copy = pltpu.make_async_copy(source, target, self.sems.at[self.count])
        self.count += 1
        copy.start()
        return copy


class Sender:
    def __init__(self, send_sem, recv_sem):
        self.send_sem, self.recv_sem, self.count = send_sem, recv_sem, 0

    def __call__(self, source, target, device):
        copy = pltpu.make_async_remote_copy(
            src_ref=source,
            dst_ref=target,
            send_sem=self.send_sem.at[self.count],
            recv_sem=self.recv_sem.at[self.count],
            device_id=device,
            device_id_type=MESH,
        )
        self.count += 1
        copy.start()
        return copy


AXES = ("x", "y", "z")
CUBE = [("core", 1)] + [(axis, k) for axis in AXES for k in (1, 2, 3)]


def placed_rows(slot_row, slots):
    rows = slot_row.shape[1]
    slot = lax.broadcasted_iota(jnp.int32, (slots, rows), 0).astype(full)
    return jnp.where(slot == slot_row, 1.0, 0.0).astype(low_type)


def placed_of(table, slots):
    table = table.reshape(-1, table.shape[-1])
    return jnp.concatenate(
        [placed_rows(table[e : e + 1], slots) for e in range(table.shape[0])], axis=0
    )


class Reduce:
    ORDERS = (("x", "y", "z"), ("y", "z", "x"), ("z", "x", "y"), ("x", "y", "z"), ("x", "y", "z"))

    def __init__(self, given, scratch, send_sem, recv_sem):
        _, _, self.at = place_of()
        self.given = given
        self.core, self.half, self.row, self.going, self.total, self.last = (
            scratch[n : n + len(given)] for n in range(0, len(scratch), len(given))
        )
        self.send = Sender(send_sem, recv_sem)
        self.copies = {}

    def seat(self, n, axis, k):
        return lax.bitwise_xor(self.at[self.ORDERS[n][axis]], k)

    def peer(self, n, axis, k):
        return peer_on(self.ORDERS[n][axis], k)

    def cores(self, n):
        for k in (1, 2, 3, 0):
            a = self.seat(n, 0, k)
            piece = self.given[n].at[a, 1 - self.at["core"]]
            self.copies[n, 0, k] = self.send(piece, self.core[n].at[a], peer_on("core", 1))

    def pair(self, n, *place):
        a, *rest = place
        own, other = self.given[n][(a, self.at["core"], *rest)], self.core[n][place]
        return own.astype(full) + other.astype(full)

    def first(self, n):
        for k in (1, 2, 3):
            self.copies[n, 0, k].wait_recv()
            self.going[n][k - 1] = self.pair(n, self.seat(n, 0, k)).astype(low_type)
            self.copies[n, 1, k] = self.send(
                self.going[n].at[k - 1], self.half[n].at[k - 1], self.peer(n, 0, k)
            )

    def second(self, n):
        self.copies[n, 0, 0].wait_recv()
        for k in (1, 2, 3):
            self.copies[n, 1, k].wait()
        for k in (1, 2, 3, 0):
            b = self.seat(n, 1, k)
            value = self.pair(n, self.seat(n, 0, 0), b)
            for m in range(3):
                value += self.half[n][m, b].astype(full)
            if k:
                self.going[n][k - 1, 0] = value.astype(low_type)
                self.copies[n, 2, k] = self.send(
                    self.going[n].at[k - 1, 0], self.row[n].at[k - 1], self.peer(n, 1, k)
                )
            else:
                self.total[n][...] = value.reshape(self.total[n].shape)

    def third(self, n):
        for k in (1, 2, 3):
            self.copies[n, 2, k].wait()
        value = self.total[n][...].reshape(self.row[n].shape[1:])
        for m in range(3):
            value += self.row[n][m].astype(full)
        self.total[n][...] = value.reshape(self.total[n].shape)
        for k in (1, 2, 3):
            d = self.seat(n, 2, k)
            self.copies[n, 3, k] = self.send(
                self.total[n].at[d], self.last[n].at[k - 1], self.peer(n, 2, k)
            )

    def finish(self, n):
        for k in (1, 2, 3):
            self.copies[n, 3, k].wait()
        for k in range(4):
            self.copies[n, 0, k].wait_send()
        last = self.last[n]
        return self.total[n][self.seat(n, 2, 0)] + last[0] + last[1] + last[2]


PLANE = [(axis, k) for axis in ("y", "z") for k in (1, 2, 3)]


def spread_slots(send, move, tables, tokens_of, rows_bufs, out_ref):
    _, _, at = place_of()
    y, z = at["y"], at["z"]
    _, _, _, slots, half = rows_bufs[0].shape
    copies = []
    for side in (1, 0):
        rows, table, seat = rows_bufs[side], tables[side], (y, z)[side]
        for k in range(4):
            source = lax.bitwise_xor(seat, k)
            placed = placed_of(table[source], slots)
            rows[k] = dot(placed, tokens_of(side, k)).astype(low_type).reshape(rows.shape[1:])
            if side == 0:
                target = out_ref.at[source, z, :, :, pl.ds(0, half)]
            else:
                target = out_ref.at[y, source, :, :, pl.ds(half, half)]
            across, mine = ("z", z) if side == 0 else ("y", y)
            for n in (1, 2, 3):
                piece = rows.at[k, lax.bitwise_xor(mine, n)]
                copies.append(send(piece, target, peer_on(across, n)))
            copies.append(move(rows.at[k, mine], target))
    return copies


class Homeward:
    def __init__(self, send, move, back_ref, tables, held, going, came):
        _, _, at = place_of()
        self.seats = at["y"], at["z"]
        self.send, self.tables, self.held, self.going, self.came = send, tables, held, going, came
        self.first, self.local, self.second, self.kept = {}, {}, {}, {}
        y, z = self.seats
        half = held[0].shape[-1]
        sides = (pl.ds(0, half), pl.ds(half, half))
        for k in (1, 2, 3, 0):
            to_y, to_z = lax.bitwise_xor(y, k), lax.bitwise_xor(z, k)
            for n in (1, 2, 3):
                piece = back_ref.at[to_y, lax.bitwise_xor(z, n), :, :, sides[0]]
                self.first[0, k, n] = send(piece, held[0].at[k, n], peer_on("z", n))
                piece = back_ref.at[lax.bitwise_xor(y, n), to_z, :, :, sides[1]]
                self.first[1, k, n] = send(piece, held[1].at[k, n], peer_on("y", n))
            self.local[0, k] = move(back_ref.at[to_y, z, :, :, sides[0]], held[0].at[k, 0])
            self.local[1, k] = move(back_ref.at[y, to_z, :, :, sides[1]], held[1].at[k, 0])

    def add(self, k):
        for side, axis in ((0, "y"), (1, "z")):
            held, table = self.held[side], self.tables[side]
            seat, mine = self.seats[side], self.seats[1 - side]
            _, _, parts, slots, half = held.shape
            for n in (1, 2, 3):
                self.first[side, k, n].wait_recv()
            self.local[side, k].wait()
            source = lax.bitwise_xor(seat, k)
            total = jnp.zeros((table.shape[-1], half), full)
            for n in range(4):
                placed = placed_of(table[source, lax.bitwise_xor(mine, n)], slots)
                total += dot_tn(placed, held[k, n].reshape(parts * slots, half))
            if k:
                self.going[side][k - 1] = total.astype(low_type)
                self.second[side, k] = self.send(
                    self.going[side].at[k - 1], self.came[side].at[k - 1], peer_on(axis, k)
                )
            else:
                self.kept[side] = total

    def sums(self):
        for side in (0, 1):
            for k in (1, 2, 3):
                self.second[side, k].wait_recv()
        return jnp.concatenate(
            [
                self.kept[side] + sum(self.came[side][n].astype(full) for n in range(3))
                for side in (0, 1)
            ],
            axis=1,
        )

    def end(self):
        for copies in (self.first, self.second):
            for copy in copies.values():
                copy.wait_send()


def home_scratch(parts, slots, rows, half):
    return [pltpu.VMEM((4, 4, parts, slots, half), low_type)] * 2 + [
        pltpu.VMEM((3, rows, half), low_type)
    ] * 4


def by_place(values, axes):
    strides = dict(x=32, core=16, y=4, z=1)
    counts = dict(x=4, core=2, y=4, z=4)
    places = [0]
    for axis in axes:
        places = [p + n * strides[axis] for p in places for n in range(counts[axis])]
    return jnp.concatenate([values[p * 8 : p * 8 + 8] for p in places], axis=0)


def expert_rows(x, grad, in_w, down_w, router_w, mine_at, experts):
    half = down_w.shape[1]
    projected, logits, hidden_grad = dot(x, in_w), dot(x, router_w), dot(grad, down_w)
    gate_part, up = projected[:, :half], projected[:, half:]
    sigmoid = 1.0 / (1.0 + jnp.exp(-gate_part))
    silu = gate_part * sigmoid
    hidden = (silu * up).astype(low_type).astype(full)
    lane = lax.broadcasted_iota(jnp.int32, logits.shape, 1)
    logits = jnp.where(lane < experts, logits, masked_score)
    shifted = jnp.exp(logits - jnp.max(logits, axis=-1, keepdims=True))
    routing = shifted / jnp.sum(shifted, axis=-1, keepdims=True)
    mine = lane == mine_at
    chosen = jnp.sum(jnp.where(mine, routing, 0.0), axis=-1, keepdims=True)
    gate = chosen.astype(low_type).astype(full)
    gate_grad = jnp.sum(hidden * hidden_grad, axis=-1, keepdims=True)
    logit_grad = (gate_grad * chosen) * (jnp.where(mine, 1.0, 0.0) - routing)
    logit_grad = logit_grad.astype(low_type)
    hidden_grad = hidden_grad * gate
    gate_back = hidden_grad * up * (sigmoid * (1.0 + gate_part * (1.0 - sigmoid)))
    projected_grad = jnp.concatenate(
        [gate_back.astype(low_type), (hidden_grad * silu).astype(low_type)], axis=1
    )
    hidden = (hidden * gate).astype(low_type)
    made = dot_nt(hidden, down_w)
    back = dot_nt(projected_grad, in_w) + dot_nt(logit_grad, router_w)
    return made, back, projected_grad, hidden, logit_grad


def moe_kernel(experts, *refs):
    (att_ref, output_ref, tokens_ref, gains_ref, left_ref, right_ref, grad_ref, held_any, in_any, down_any, weights_any) = refs[:11]
    (mid_ref, made_ref, in_out, down_out, router_out, att_out, mid_grad_ref, low_ref, ffn_ref, att_grad_ref) = refs[11:21]
    (moe_buf, token_bufs, rows_bufs, x_buf, g_buf, p_buf, h_buf, l_buf, y_buf, in_w, down_w, router_w) = refs[21:33]
    (back_bufs, going, came, in_buf, down_buf, in_core, down_core, in_came, down_came) = refs[33:42]
    send_sem, recv_sem, back_send, back_recv, y_sem, local_sem = refs[42:]
    _, expert, at = place_of()
    x, y, z, c = at["x"], at["y"], at["z"], at["core"]
    tables = left_ref, right_ref
    seats = y, z
    rows, wide = mid_ref.shape
    half = wide // 2
    _, parts, _, _, slots, _ = rows_bufs.shape
    peers = [peer_on(axis, k) for axis, k in CUBE]
    greet(peers)
    move, send = Mover(local_sem), Sender(send_sem, recv_sem)
    loads = {
        ("g", 0): move(held_any.at[:, :, 0], g_buf),
        ("in", 0): move(in_any.at[0], in_w),
        ("down", 0): move(down_any.at[0], down_w),
        "router": move(weights_any.at[:, pl.ds(KV_HEADS * PACK, EXTRA)], router_w),
    }
    attended = jnp.concatenate([att_ref[g] for g in range(KV_HEADS)], axis=1)
    mid = tokens_ref[...].astype(full) + dot(attended, output_ref[...])
    mid_ref[...] = mid
    inverse = lax.rsqrt(jnp.mean(mid * mid, axis=-1, keepdims=True) + norm_eps)
    moe_buf[...] = (mid * inverse * gains_ref[1:2, :]).astype(low_type)
    meet(peers)
    along = {}
    for k in (1, 2, 3):
        for side, axis in ((0, "y"), (1, "z")):
            piece = moe_buf.at[:, pl.ds(side * half, half)]
            along[side, k] = send(piece, token_bufs.at[side, k - 1], peer_on(axis, k))
    spread = [[] for _ in range(parts)]

    def spread_part(k, j):
        for side, across in ((0, "z"), (1, "y")):
            source, mine = lax.bitwise_xor(seats[side], k), seats[1 - side]
            cols = pl.ds(side * half, half)
            place = (source, z) if side == 0 else (y, source)
            target = x_buf.at[(j, *place, slice(None), cols)]
            for n in (1, 2, 3):
                piece = rows_bufs.at[side, j, k, lax.bitwise_xor(mine, n)]
                spread[j].append(send(piece, target, peer_on(across, n)))
            x_buf[(j, *place, slice(None), cols)] = rows_bufs[side, j, k, mine]

    for k in range(4):
        for side in (0, 1):
            source = lax.bitwise_xor(seats[side], k)
            placed = placed_of(tables[side][source], slots)
            if k:
                along[side, k].wait_recv()
                tokens = token_bufs[side, k - 1]
            else:
                tokens = moe_buf[:, side * half : (side + 1) * half]
            value = dot(placed, tokens).astype(low_type).reshape(4, parts, slots, half)
            for j in range(parts):
                rows_bufs[side, j, k] = value[:, j]
        spread_part(k, 0)
    for k in range(4):
        for j in range(1, parts):
            spread_part(k, j)
    att_out[...] = flip(attended).astype(low_type)
    loads["router"].wait()

    def back_copy(side, j, k, n):
        if side == 0:
            place = (lax.bitwise_xor(y, k), lax.bitwise_xor(z, n))
        else:
            place = (lax.bitwise_xor(y, n), lax.bitwise_xor(z, k))
        number = ((side * parts + j) * 4 + k) * 3 + n - 1
        return pltpu.make_async_remote_copy(
            src_ref=rows_bufs.at[(side, j, *place)],
            dst_ref=back_bufs.at[side, k, n - 1, j],
            send_sem=back_send.at[number],
            recv_sem=back_recv.at[number],
            device_id=peer_on(("z", "y")[side], n),
            device_id_type=MESH,
        )

    def y_copy(slot, there, j):
        return pltpu.make_async_copy(y_buf.at[slot], made_ref.at[there, :, j], y_sem.at[slot])

    def experts_job(j):
        for copy in spread[j]:
            copy.wait()
        for name in ("g", "in", "down"):
            loads[name, j].wait()

        for turn in range(4):
            k = (turn + 1) % 4
            there = lax.bitwise_xor(y, k)
            count = 4 * slots
            made, back, p, h, l = expert_rows(
                x_buf[j, there].reshape(count, wide),
                g_buf[there].reshape(count, wide),
                in_w[...],
                down_w[...],
                router_w[...],
                parts * expert + j,
                experts,
            )
            slot = turn % 2
            if turn >= 2:
                y_copy(slot, lax.bitwise_xor(y, (turn - 1) % 4), j).wait()
            y_buf[slot] = made.astype(low_type).reshape(y_buf.shape[1:])
            y_copy(slot, there, j).start()
            back = back.astype(low_type)
            for side in (0, 1):
                piece = back[:, side * half : (side + 1) * half]
                rows_bufs[side, j, there] = piece.reshape(4, slots, half)
            for n in (1, 2, 3):
                back_copy(0, j, k, n).start()
            if k:
                for other in range(4):
                    back_copy(1, j, other, k).start()
            p_buf[there] = p
            h_buf[there] = h
            l_buf[there] = l
        for turn in (2, 3):
            y_copy(turn % 2, lax.bitwise_xor(y, (turn + 1) % 4), j).wait()

    def stacked(values):
        return values.reshape(-1, values.shape[-1])

    def in_job(j):
        for n in range(wide // 256):
            cols = slice(n * 256, (n + 1) * 256)
            value = dot_tn(stacked(x_buf[j, :, :, :, cols]), stacked(p_buf[...])).astype(low_type)
            in_buf[j, n, 0] = value[:128]
            in_buf[j, n, 1] = value[128:]
        core_copies["in", j] = send(in_buf.at[j, :, 1 - c], in_core.at[j], peer_on("core", 1))

    def down_job(j):
        for n in range(wide // 256):
            cols = slice(n * 256, (n + 1) * 256)
            value = dot_tn(stacked(g_buf[:, :, :, cols]), stacked(h_buf[...])).astype(low_type)
            down_buf[j, n, 0] = value[:128]
            down_buf[j, n, 1] = value[128:]
            part = dot_tn(stacked(x_buf[j, :, :, :, cols]), stacked(l_buf[...]))
            router_out[cols, :] = part if j == 0 else router_out[cols, :] + part
        core_copies["down", j] = send(
            down_buf.at[j, :, 1 - c], down_core.at[j], peer_on("core", 1)
        )

    core_copies, x_copies = {}, {}
    buffers = {
        "in": (in_buf, in_core, in_came, in_out),
        "down": (down_buf, down_core, down_came, down_out),
    }

    def across_job(name, j):
        own, core, came_x, _ = buffers[name]
        core_copies[name, j].wait_recv()
        for k in (1, 2, 3):
            there = lax.bitwise_xor(x, k)
            value = own[j, there, c].astype(full) + core[j, there].astype(full)
            own[j, there, c] = value.astype(low_type)
            x_copies[name, j, k] = send(
                own.at[j, there, c], came_x.at[j, k - 1], peer_on("x", k)
            )

    def total_job(name, j):
        own, core, came_x, out = buffers[name]
        value = own[j, x, c].astype(full) + core[j, x].astype(full)
        for k in (1, 2, 3):
            x_copies[name, j, k].wait_recv()
            value += came_x[j, k - 1].astype(full)
        out[j] = value

    second, kept = {}, {}

    def add_job(k):
        for side, axis in ((0, "y"), (1, "z")):
            seat, mine = seats[side], seats[1 - side]
            source = lax.bitwise_xor(seat, k)
            total = jnp.zeros((rows, half), full)
            for n in range(4):
                if n:
                    for j in range(parts):
                        back_copy(side, j, k, n).wait_recv()
                    piece = back_bufs[side, k, n - 1].reshape(parts * slots, half)
                else:
                    place = (source, z) if side == 0 else (y, source)
                    piece = jnp.concatenate(
                        [rows_bufs[(side, j, *place)] for j in range(parts)], axis=0
                    )
                placed = placed_of(tables[side][source, lax.bitwise_xor(mine, n)], slots)
                total += dot_tn(placed, piece)
            if k:
                going[side, k - 1] = total.astype(low_type)
                second[side, k] = send(
                    going.at[side, k - 1], came.at[side, k - 1], peer_on(axis, k)
                )
            else:
                kept[side] = total

    experts_job(0)
    for j in range(1, parts):
        loads["in", j] = move(in_any.at[j], in_w)
        loads["down", j] = move(down_any.at[j], down_w)
        in_job(j - 1)
        down_job(j - 1)
        loads["g", j] = move(held_any.at[:, :, j], g_buf)
        across_job("in", j - 1)
        across_job("down", j - 1)
        experts_job(j)
        in_job(j)
        down_job(j)
    add_job(1)
    across_job("in", parts - 1)
    add_job(2)
    across_job("down", parts - 1)
    add_job(3)
    add_job(0)
    sums = []
    for side in (0, 1):
        for k in (1, 2, 3):
            second[side, k].wait_recv()
        sums.append(kept[side] + sum(came[side, n].astype(full) for n in range(3)))
    moe_grad = jnp.concatenate(sums, axis=1)
    mid = mid_ref[...]
    inverse = lax.rsqrt(jnp.mean(mid * mid, axis=-1, keepdims=True) + norm_eps)
    scaled = moe_grad * gains_ref[1:2, :]
    shared = jnp.sum(scaled * mid, axis=-1, keepdims=True) * (inverse * inverse * inverse / wide)
    mid_grad = grad_ref[...].astype(full) + (scaled * inverse - mid * shared)
    mid_grad_ref[...] = mid_grad
    low = mid_grad.astype(low_type)
    low_ref[...] = low
    ffn_ref[...] = jnp.sum(mid * inverse * moe_grad, axis=0, keepdims=True)
    for g in range(KV_HEADS):
        att_grad_ref[g] = dot_nt(low, output_ref[g * PAIR : (g + 1) * PAIR, :]).astype(low_type)
    for j in range(parts):
        total_job("in", j)
        total_job("down", j)
    for copies in (along, second, core_copies, x_copies):
        for copy in copies.values():
            copy.wait_send()
    for side in (0, 1):
        for j in range(parts):
            for k in range(4):
                for n in (1, 2, 3):
                    back_copy(side, j, k, n).wait_send()


def moe_layer(att, output_proj, tokens, gains, left, right, grad, held, in_w, down_w, weights, experts, number):
    rows, wide = tokens.shape
    _, _, parts, slots, _ = held.shape
    half = wide // 2
    hidden = down_w.shape[2]
    shapes = [
        ((rows, wide), full),
        (held.shape, low_type),
        ((parts, wide // 8, 2 * hidden), full),
        ((parts, wide // 8, hidden), full),
        ((wide, EXTRA), full),
        ((wide, rows), low_type),
        ((rows, wide), full),
        ((rows, wide), low_type),
        ((1, wide), full),
        ((KV_HEADS, rows, PAIR), low_type),
    ]
    scratch = [
        (rows, wide),
        (2, 3, rows, half),
        (2, parts, 4, 4, slots, half),
        (parts, 4, 4, slots, wide),
        (4, 4, slots, wide),
        (4, 4 * slots, 2 * hidden),
        (4, 4 * slots, hidden),
        (4, 4 * slots, EXTRA),
        (2, 4, slots, wide),
        in_w.shape[1:],
        down_w.shape[1:],
        (wide, EXTRA),
        (2, 4, 3, parts, slots, half),
        (2, 3, rows, half),
        (2, 3, rows, half),
        (parts, 4, 2, wide // 8, 2 * hidden),
        (parts, 4, 2, wide // 8, hidden),
        (parts, 4, wide // 8, 2 * hidden),
        (parts, 4, wide // 8, hidden),
        (parts, 3, wide // 8, 2 * hidden),
        (parts, 3, wide // 8, hidden),
    ]
    copies = 6 + 24 * parts + 8 * parts + 6
    return pl.pallas_call(
        functools.partial(moe_kernel, experts),
        out_shape=[jax.ShapeDtypeStruct(*s) for s in shapes],
        in_specs=[VMEM] * 7 + [ANY] * 4,
        out_specs=[VMEM, ANY] + [VMEM] * 8,
        scratch_shapes=[
            *[pltpu.VMEM(s, low_type) for s in scratch],
            *[pltpu.SemaphoreType.DMA((copies,))] * 2,
            *[pltpu.SemaphoreType.DMA((24 * parts,))] * 2,
            pltpu.SemaphoreType.DMA((2,)),
            pltpu.SemaphoreType.DMA((3 * parts + 1,)),
        ],
        compiler_params=comm_params(number),
        cost_estimate=cost(120),
        name="moe_layer",
    )(att, output_proj, tokens, gains, left, right, grad, held, in_w, down_w, weights)


def allowed_of(shape, rows, length, i):
    key_at = lax.broadcasted_iota(jnp.int32, shape, 0)
    query_at = lax.broadcasted_iota(jnp.int32, shape, 1) % rows
    return (key_at <= query_at) & (key_at < length - i * rows)


def key_spread(width, wide):
    out = lax.broadcasted_iota(jnp.int32, (wide, width), 0)
    here = lax.broadcasted_iota(jnp.int32, (wide, width), 1)
    return jnp.where(out == (here // 4) * 8 + here % 4, 1.0, 0.0).astype(low_type)


def hand_over(sent, home, send_sem, recv_sem, i):
    dp, expert, _ = place_of()
    k = lax.bitwise_xor(dp, i)
    return pltpu.make_async_remote_copy(
        src_ref=sent.at[i],
        dst_ref=home.at[dp],
        send_sem=send_sem.at[k],
        recv_sem=recv_sem.at[k],
        device_id=(i, expert),
        device_id_type=MESH,
    )


def gather_weights(
    at, meet_all, query_ref, key_ref, value_ref, router_ref, gains_row, slot_a, slot_b, master_ref, buf, third, got_a, got_b,
    shard_ref, shards_ref, mine_ref, others_ref, ours_ref, send, between,
):
    x, y, z, c = at["x"], at["y"], at["z"], at["core"]
    rows, columns = shard_ref.shape
    cut = columns // 256 * 128
    sides = (pl.ds(0, cut), pl.ds(cut, columns - cut))
    for g in range(KV_HEADS):
        here = g * PACK
        shard_ref[:, here : here + PAIR] = query_ref[:, g * PAIR : (g + 1) * PAIR]
        head = slice(g * HEAD_DIM, (g + 1) * HEAD_DIM)
        shard_ref[:, here + PAIR : here + PACK] = jnp.concatenate(
            [key_ref[:, head], value_ref[:, head]], axis=1
        )
    experts = router_ref.shape[1]
    lane = lax.broadcasted_iota(jnp.int32, (rows, EXTRA), 1)
    row = lax.broadcasted_iota(jnp.int32, (rows, EXTRA), 0)
    gains = jnp.broadcast_to(gains_row, (rows, EXTRA))
    extra = jnp.concatenate(
        [router_ref[...], jnp.zeros((rows, EXTRA - experts), full)], axis=1
    )
    for n in range(4):
        column = jnp.sum(jnp.where(lane == row + n * rows, gains, 0.0), axis=1, keepdims=True)
        extra += jnp.where(lane == experts + n, column, 0.0)
    shard_ref[:, KV_HEADS * PACK :] = extra
    meet_all()
    first = [send(shard_ref, shards_ref.at[z], peer_on("z", k)) for k in (1, 2, 3)]
    first += [send(master_ref, others_ref.at[x], peer_on("x", k)) for k in (1, 2, 3)]
    shards_ref[z] = shard_ref[...]
    others_ref[x] = master_ref[...]
    between()
    slots = []
    for k in (1, 2, 3):
        slots.append(send(slot_a.at[lax.bitwise_xor(y, k)], got_a.at[y], peer_on("y", k)))
        slots.append(send(slot_b.at[lax.bitwise_xor(z, k)], got_b.at[z], peer_on("z", k)))
    got_a[y] = slot_a[y]
    got_b[z] = slot_b[z]
    for copy in first:
        copy.wait()
    mine = shards_ref[...].reshape(mine_ref.shape).astype(low_type)
    mine_ref[...] = mine
    buf[x, c, y] = mine
    ours = others_ref[...].reshape(ours_ref.shape).astype(low_type)
    ours_ref[...] = ours
    third[z, c, y] = ours
    second = []
    for k in (1, 2, 3):
        for side, axis in ((0, "y"), (1, "x")):
            second.append(
                send(
                    mine_ref.at[:, sides[side]],
                    buf.at[x, c, y, :, sides[side]],
                    peer_on(axis, k),
                )
            )
        second.append(send(ours_ref, third.at[z, c, y], peer_on("y", k)))
    for copy in second:
        copy.wait()
    final = []
    for k in (1, 2, 3):
        piece = buf.at[x, c, :, :, sides[0]]
        final.append(send(piece, piece, peer_on("x", k)))
        piece = buf.at[:, c, y, :, sides[1]]
        final.append(send(piece, piece, peer_on("y", k)))
        piece = third.at[z, c]
        final.append(send(piece, piece, peer_on("z", k)))
    other = peer_on("core", 1)
    last = []
    for piece in (buf.at[x, c, :, :, sides[0]], buf.at[:, c, y, :, sides[1]], third.at[z, c]):
        last.append(send(piece, piece, other))
    for n, k in enumerate((1, 2, 3)):
        final[3 * n].wait_recv()
        piece = buf.at[lax.bitwise_xor(x, k), c, :, :, sides[0]]
        last.append(send(piece, piece, other))
        final[3 * n + 1].wait_recv()
        piece = buf.at[:, c, lax.bitwise_xor(y, k), :, sides[1]]
        last.append(send(piece, piece, other))
        final[3 * n + 2].wait_recv()
        piece = third.at[lax.bitwise_xor(z, k), c]
        last.append(send(piece, piece, other))
    return slots, final, last


def forward_kernel(
    length_ref, query_ref, key_ref, value_ref, router_ref, gains_row, slot_a, slot_b, master_ref, tokens_ref, cos_ref, sin_ref, grad_ref,
    weights_out, rows_ref, output_out, normed_out, raw_out, held_out, pack_ref, gains_ref, att_ref, log_ref, home_ref, left_ref, right_ref,
    shard_ref, shards_ref, mine_ref, others_ref, ours_ref, weights_ref, third_buf,
    output_ref, normed_rows, raw_ref, held_ref, grad_bufs, rows_a, rows_b, sent, flip_ref, score_ref,
    gather_send, gather_recv, send_one, recv_one, send_two, recv_two, send_sem, recv_sem, move_sem,
):
    dp, _, at = place_of()
    y, z = at["y"], at["z"]
    peers = dp_peers() + [peer_on(axis, k) for axis, k in PLANE]
    greet(peers)
    blocks, rows = held_ref.shape[0], held_ref.shape[1]
    wide = tokens_ref.shape[1]
    width = KV_HEADS * HEAD_DIM
    half = wide // 2
    send, move = Sender(send_sem, recv_sem), Mover(move_sem)
    along = {}

    def start_along(side, axis):
        for k in (1, 2, 3):
            piece = grad_ref.at[:, pl.ds(side * half, half)]
            along[side, k] = send(piece, grad_bufs.at[side, k - 1], peer_on(axis, k))

    slots_sent, final, last = gather_weights(
        at, lambda: meet(peers), query_ref, key_ref, value_ref, router_ref, gains_row[...], slot_a, slot_b, master_ref,
        weights_ref, third_buf, left_ref, right_ref, shard_ref, shards_ref, mine_ref, others_ref, ours_ref,
        Sender(gather_send, gather_recv),
        lambda: start_along(1, "z"),
    )
    start_along(0, "y")
    for copy in last:
        copy.wait()
    stored = [move(weights_ref, weights_out)]

    def weights_of(start, count):
        return weights_ref[..., start : start + count].reshape(wide, count)

    extra = flip(weights_of(KV_HEADS * PACK, EXTRA))
    gains_ref[0:1, :] = extra[32:33]
    gains_ref[1:2, :] = extra[34:35]
    key_gain = dot(
        jnp.broadcast_to(extra[35:36], (8, wide)).astype(low_type), key_spread(width, wide)
    )[:1]
    for g in range(KV_HEADS):
        pack_ref[g, :, :PAIR] = extra[33:34, g * PAIR : (g + 1) * PAIR]
        pack_ref[g, :, PAIR:] = jnp.concatenate(
            [key_gain[:, g * HEAD_DIM : (g + 1) * HEAD_DIM], jnp.ones((1, HEAD_DIM), full)],
            axis=1,
        )
    values = tokens_ref[...].astype(full)
    inverse = lax.rsqrt(jnp.mean(values * values, axis=-1, keepdims=True) + norm_eps)
    normed = (values * inverse * gains_ref[0:1, :]).astype(low_type)
    query_sum = jnp.zeros((rows, PAIR), full)
    key_sum = jnp.zeros((rows, PAIR), full)
    for g in range(KV_HEADS):
        raw = dot(normed, weights_of(g * PACK, PACK))
        raw_ref[g] = raw
        query_sum += raw[:, :PAIR] * raw[:, :PAIR]
        key_sum += raw[:, PAIR:] * raw[:, PAIR:]
    is_key = lax.broadcasted_iota(jnp.int32, key_sum.shape, 1) < HEAD_DIM
    query_inv = lax.rsqrt(
        jnp.sum(query_sum, axis=-1, keepdims=True) / (GROUP * width) + norm_eps
    )
    key_inv = lax.rsqrt(
        jnp.sum(jnp.where(is_key, key_sum, 0.0), axis=-1, keepdims=True) / width + norm_eps
    )
    pair_inv = jnp.where(is_key, key_inv, 1.0)
    handed = []
    tables = turning(cos_ref, sin_ref)
    for k in (1, 2, 3, 4, 5, 6, 7, 0):
        g = lax.bitwise_xor(dp, k)
        target = sent if k else held_ref
        for part, scale in ((0, query_inv), (1, pair_inv)):
            here = slice(part * PAIR, (part + 1) * PAIR)
            scaled = raw_ref[g, :, here] * scale * pack_ref[g, :, here]
            cos, sin = tables[part]
            turned = scaled * cos + partner(scaled) * sin
            target[g, :, here] = turned.astype(low_type)
        if k:
            handed.append(hand_over(sent, held_ref, send_one, recv_one, g))
            handed[-1].start()
    def tokens_of(side, k):
        if k == 0:
            return grad_ref[:, side * half : (side + 1) * half]
        along[side, k].wait_recv()
        return grad_bufs[side, k - 1]

    for copy in slots_sent:
        copy.wait()
    spread = spread_slots(
        send, move, (left_ref, right_ref), tokens_of, (rows_a, rows_b), rows_ref
    )
    stored.append(move(raw_ref, raw_out))
    wide_query = GROUP * rows
    flat = flip(normed)
    normed_rows[0] = flat.astype(low_type)
    normed_rows[1] = by_place(flat, ("y", "core", "z", "x")).astype(low_type)
    normed_rows[2] = by_place(flat, ("z", "core", "x", "y")).astype(low_type)
    for n in range(4):
        pieces = [
            third_buf[p, m // 4, m % 4, n * 8 : n * 8 + 8, :].astype(full)
            for m in range(8)
            for p in range(4)
        ]
        output_ref[n * 256 : (n + 1) * 256, :] = jnp.concatenate(pieces, axis=0).astype(low_type)

    stored.append(move(normed_rows, normed_out))
    stored.append(move(output_ref, output_out))
    for i in range(blocks):

        @pl.when(i != dp)
        def _():
            hand_over(sent, held_ref, send_one, recv_one, i).wait_recv()

        span = slice(i * rows, (i + 1) * rows)
        flip_ref[:, span] = flip(held_ref[i, :, PAIR + HEAD_DIM :]).astype(low_type)
        query = flip(held_ref[i, :, :PAIR]).astype(low_type)
        query = jnp.concatenate([query[:HEAD_DIM], query[HEAD_DIM:]], axis=1)
        top = jnp.full((1, wide_query), masked_score, full)
        for j in range(i + 1):
            scores = dot(held_ref[j, :, PAIR : PAIR + HEAD_DIM], query) * score_scale
            if j == i:
                allowed = allowed_of(scores.shape, rows, length_ref[0], i)
                scores = jnp.where(allowed, scores, masked_score)
            score_ref[j * rows : (j + 1) * rows] = scores
            top = jnp.maximum(top, jnp.max(scores, axis=0, keepdims=True))
        soft = jnp.exp(score_ref[: (i + 1) * rows] - top)
        total = jnp.sum(soft, axis=0, keepdims=True)
        acc = dot(flip_ref[:, : (i + 1) * rows], soft.astype(low_type)) / total
        both = jnp.concatenate([acc[:, :rows], acc[:, rows:]], axis=0)
        att_ref[i] = both.T.astype(low_type)
        log_ref[i] = jnp.broadcast_to(top + jnp.log(total), log_ref.shape[1:])

        if i == blocks - 1:
            stored.append(move(held_ref, held_out))

        @pl.when(i != dp)
        def _():
            hand_over(att_ref, home_ref, send_two, recv_two, i).start()

        @pl.when(i == dp)
        def _():
            home_ref[i] = att_ref[i]

    for copy in handed:
        copy.wait_send()
    for copy in spread:
        copy.wait()
    for copies in (along.values(), final):
        for copy in copies:
            copy.wait_send()
    for copy in stored:
        copy.wait()
    for k in range(1, 8):
        hand_over(att_ref, home_ref, send_two, recv_two, lax.bitwise_xor(dp, k)).wait()


def forward(lengths, masters, gains_row, slot_a, slot_b, tokens, cosine, sine, grad, slots, number):
    rows, wide = tokens.shape
    query, key, value, output, router = masters
    share, columns = query.shape[0], KV_HEADS * PACK + EXTRA
    _, _, parts, _ = slot_a.shape
    shapes = [
        ((4, 2, 4, 4 * share, columns), low_type),
        ((4, 4, parts, slots, wide), low_type),
        ((wide, wide), low_type),
        ((3, wide, rows), low_type),
        ((KV_HEADS, rows, PACK), full),
        ((8, rows, PACK), low_type),
        ((KV_HEADS, 1, PACK), full),
        ((8, wide), full),
        ((8, rows, PAIR), low_type),
        ((8, 8, GROUP * rows), full),
        ((KV_HEADS, rows, PAIR), low_type),
        (slot_a.shape, full),
        (slot_b.shape, full),
    ]
    return pl.pallas_call(
        forward_kernel,
        out_shape=[jax.ShapeDtypeStruct(*s) for s in shapes],
        in_specs=[SMEM] + [VMEM] * 12,
        out_specs=[ANY] * 6 + [VMEM] * (len(shapes) - 6),
        scratch_shapes=[
            pltpu.VMEM((share, columns), full),
            pltpu.VMEM((4, share, columns), full),
            pltpu.VMEM((4 * share, columns), low_type),
            pltpu.VMEM((4, share, wide), full),
            pltpu.VMEM((4 * share, wide), low_type),
            pltpu.VMEM((4, 2, 4, 4 * share, columns), low_type),
            pltpu.VMEM((4, 2, 4, 4 * share, wide), low_type),
            *[pltpu.VMEM(*s) for s in shapes[2:6]],
            pltpu.VMEM((2, 3, rows, wide // 2), low_type),
            pltpu.VMEM((4, 4, parts, slots, wide // 2), low_type),
            pltpu.VMEM((4, 4, parts, slots, wide // 2), low_type),
            pltpu.VMEM((KV_HEADS, rows, PACK), low_type),
            pltpu.VMEM((HEAD_DIM, 8 * rows), low_type),
            pltpu.VMEM((8 * rows, GROUP * rows), full),
            *[pltpu.SemaphoreType.DMA((42,))] * 2,
            *[pltpu.SemaphoreType.DMA((8,))] * 4,
            *[pltpu.SemaphoreType.DMA((30,))] * 2,
            pltpu.SemaphoreType.DMA((13,)),
        ],
        compiler_params=comm_params(number),
        cost_estimate=cost(75),
        name="forward",
    )(lengths, query, key, value, router, gains_row, slot_a, slot_b, output, tokens, cosine, sine, grad)


def backward_kernel(
    length_ref, held_ref, arrive, grad_ref, att_ref, log_ref, home_ref, sent, flip_ref, sum_ref, back_ref, send_sem, recv_sem
):
    dp, _, _ = place_of()
    blocks, rows = held_ref.shape[0], held_ref.shape[1]
    for j in range(blocks):
        flip_ref[:, j * rows : (j + 1) * rows] = flip(held_ref[j, :, PAIR:])[:HEAD_DIM].astype(
            low_type
        )
    none = jnp.zeros((rows, HEAD_DIM), low_type)
    key_scale = jnp.where(
        lax.broadcasted_iota(jnp.int32, (rows, PAIR), 1) < HEAD_DIM, score_scale, 1.0
    )

    def heads_beside(values):
        return jnp.concatenate([values[:HEAD_DIM], values[HEAD_DIM:]], axis=1)

    for i in range(blocks - 1, -1, -1):
        arrive(i)
        query_rows = held_ref[i, :, :PAIR]
        grad_rows = grad_ref[i]
        query = heads_beside(flip(query_rows)).astype(low_type)
        grad_full = heads_beside(flip(grad_rows))
        grad = grad_full.astype(low_type)
        inner = jnp.sum(grad_full * heads_beside(flip(att_ref[i])), axis=0, keepdims=True)
        log_total = log_ref[i, :1, :]
        query_side = jnp.concatenate(
            [
                jnp.concatenate([query_rows[:, :HEAD_DIM], none], axis=1),
                jnp.concatenate([query_rows[:, HEAD_DIM:], none], axis=1),
            ],
            axis=0,
        )
        grad_side = jnp.concatenate(
            [
                jnp.concatenate([none, grad_rows[:, :HEAD_DIM]], axis=1),
                jnp.concatenate([none, grad_rows[:, HEAD_DIM:]], axis=1),
            ],
            axis=0,
        )
        for j in range(i + 1):
            key = held_ref[j, :, PAIR : PAIR + HEAD_DIM]
            value = held_ref[j, :, PAIR + HEAD_DIM :]
            soft = jnp.exp(dot(key, query) * score_scale - log_total)
            if j == i:
                allowed = allowed_of(soft.shape, rows, length_ref[0], i)
                soft = jnp.where(allowed, soft, 0.0)
            score_grad = (soft * (dot(value, grad) - inner)).astype(low_type)
            back_ref[j * rows : (j + 1) * rows] = score_grad
            part = dot(score_grad, query_side) + dot(soft.astype(low_type), grad_side)
            sum_ref[j] = part if i == blocks - 1 else sum_ref[j] + part
        acc = dot(flip_ref[:, : (i + 1) * rows], back_ref[: (i + 1) * rows])
        both = jnp.concatenate([acc[:, :rows], acc[:, rows:]], axis=0) * score_scale
        sent[i, :, :PAIR] = both.T.astype(low_type)
        sent[i, :, PAIR:] = (sum_ref[i] * key_scale).astype(low_type)

        @pl.when(i != dp)
        def _():
            hand_over(sent, home_ref, send_sem, recv_sem, i).start()

        @pl.when(i == dp)
        def _():
            home_ref[i] = sent[i]


def tail_kernel(
    length_ref, held_ref, own_ref, att_ref, log_ref, pack_ref, gains_ref, left_ref, right_ref, made_ref, *refs
):
    given, refs = refs[:12], refs[12:]
    (output_ref, tokens_ref, *sums), refs = refs[:7], refs[7:]
    here, refs = refs[:12], refs[12:]
    held, going, came, refs = refs[0:2], refs[2:4], refs[4:6], refs[6:]
    (grad_ref, home, sent, flip_ref, sum_ref, back_ref, low_ref), refs = refs[:7], refs[7:]
    pieces, reduce_scratch, refs = refs[:5], refs[5:35], refs[35:]
    send_zero, recv_zero, send_one, recv_one, send_two, recv_two, send_three, recv_three, local_sem = refs
    dp, _, _ = place_of()
    peers = dp_peers() + [peer_on(axis, k) for axis, k in PLANE]
    greet(peers)
    move = Mover(local_sem)
    loads = [move(source, target) for source, target in zip(given, here)]
    att_rows, mid_low, raw, cos, sin, weights, normed, tokens, mid_grad, router, ffn, mid = here
    wide = tokens.shape[1]
    width = KV_HEADS * HEAD_DIM
    meet(peers)
    others = [lax.bitwise_xor(dp, k) for k in range(1, 8)]
    for g in others:
        hand_over(own_ref, grad_ref, send_zero, recv_zero, g).start()
    grad_ref[dp] = own_ref[dp]
    homeward = Homeward(
        Sender(send_two, recv_two), move, made_ref, (left_ref, right_ref), held, going, came
    )
    reduce = Reduce(pieces, reduce_scratch, send_three, recv_three)
    loads[0].wait()
    loads[1].wait()
    put_product(pieces[3], 0, att_rows[...], mid_low, 0, wide)
    reduce.cores(3)

    def arrive(i):
        @pl.when(i != dp)
        def _():
            hand_over(own_ref, grad_ref, send_zero, recv_zero, i).wait_recv()

    backward_kernel(
        length_ref, held_ref, arrive, grad_ref, att_ref, log_ref, home, sent, flip_ref, sum_ref, back_ref, send_one, recv_one
    )
    reduce.first(3)
    for load in loads[2:]:
        load.wait()
    homeward.add(1)
    homeward.add(2)
    for g in others:
        hand_over(sent, home, send_one, recv_one, g).wait()
    query_grad, key_grad = raw_gradients(home, raw, pack_ref, cos, sin, low_ref)
    for n in range(3):
        put_product(pieces[n], 0, normed[n], low_ref, CUTS[n], CUTS[n + 1] - CUTS[n])
        reduce.cores(n)
    for n in range(3):
        reduce.first(n)
    attn_grad = token_gradients(low_ref, weights, tokens, gains_ref, mid_grad, tokens_ref)
    key_wide = dot_nt(
        jnp.broadcast_to(key_grad, (8, width)).astype(low_type), key_spread(width, wide)
    )[:1]
    extra = jnp.concatenate(
        [
            jnp.zeros((32, wide), full),
            attn_grad,
            query_grad,
            ffn[...],
            key_wide,
            jnp.zeros((EXTRA - 36, wide), full),
        ],
        axis=0,
    )
    extra = (extra.T + router[...]).astype(low_type)
    pieces[4][...] = extra.reshape(pieces[4].shape)
    reduce.cores(4)
    homeward.add(3)
    reduce.first(4)
    reduce.second(3)
    order = (0, 1, 2, 3, 4)
    for n in (0, 1, 2, 4):
        reduce.second(n)
    homeward.add(0)
    for n in order:
        reduce.third(n)
    output_ref[...] = (mid[...] + homeward.sums()).astype(low_type)
    for n in order:
        sums[n][...] = reduce.finish(n)
    homeward.end()
    for g in others:
        hand_over(own_ref, grad_ref, send_zero, recv_zero, g).wait_send()


def tail(lengths, held, grad, att, logs, pack, gains, left, right, made, given, number):
    blocks, rows, _ = held.shape
    _, _, parts, slots, wide = made.shape
    widths = tuple(CUTS[n + 1] - CUTS[n] for n in range(3)) + (wide, EXTRA)

    def each(*shape, kind=low_type):
        return [pltpu.VMEM(shape + (w,), kind) for w in widths]

    return pl.pallas_call(
        tail_kernel,
        out_shape=[
            jax.ShapeDtypeStruct((rows, wide), low_type),
            jax.ShapeDtypeStruct((rows, wide), low_type),
            *[jax.ShapeDtypeStruct((8, w), full) for w in widths],
        ],
        in_specs=[SMEM] + [VMEM] * 8 + [ANY] * 13,
        out_specs=[VMEM] * 7,
        scratch_shapes=[
            *[pltpu.VMEM(v.shape, v.dtype) for v in given],
            *home_scratch(parts, slots, rows, wide // 2),
            pltpu.VMEM((blocks, rows, PAIR), low_type),
            pltpu.VMEM((KV_HEADS, rows, PACK), low_type),
            pltpu.VMEM((blocks, rows, PACK), low_type),
            pltpu.VMEM((HEAD_DIM, blocks * rows), low_type),
            pltpu.VMEM((blocks, rows, PAIR), full),
            pltpu.VMEM((blocks * rows, GROUP * rows), low_type),
            pltpu.VMEM((rows, KV_HEADS * PACK), low_type),
            *each(4, 2, 4, 32),
            *each(4, 4, 32),
            *each(3, 4, 32),
            *each(3, 32),
            *each(3, 4, 32),
            *each(4, 8, kind=full),
            *each(3, 8, kind=full),
            *[pltpu.SemaphoreType.DMA((8,))] * 4,
            *[pltpu.SemaphoreType.DMA((30,))] * 2,
            *[pltpu.SemaphoreType.DMA((13 * len(widths),))] * 2,
            pltpu.SemaphoreType.DMA((20,)),
        ],
        compiler_params=comm_params(number),
        cost_estimate=cost(90),
        name="tail",
    )(
        lengths, held, grad, att, logs, pack, gains, left, right,
        made, *given,
    )


def finish_kernel(
    first_ref, second_ref, third_ref, last_ref, extra_ref, in_ref, down_ref, output_ref, tokens_ref,
    query_ref, key_ref, value_ref, out_proj_ref, router_ref, attn_ref, ffn_ref, query_gain_ref, key_gain_ref, in_out, down_out, output_out, tokens_out,
):
    output_out[...] = output_ref[...]
    tokens_out[...] = tokens_ref[...]
    in_out[...] = in_ref[...]
    down_out[...] = down_ref[...]
    out_proj_ref[...] = last_ref[...]
    for n, ref in enumerate((first_ref, second_ref, third_ref)):
        for start in range(CUTS[n], CUTS[n + 1], PACK):
            g = start // PACK
            piece = ref[:, start - CUTS[n] : start - CUTS[n] + PACK]
            head = slice(g * HEAD_DIM, (g + 1) * HEAD_DIM)
            query_ref[:, g * PAIR : (g + 1) * PAIR] = piece[:, :PAIR]
            key_ref[:, head] = piece[:, PAIR : PAIR + HEAD_DIM]
            value_ref[:, head] = piece[:, PAIR + HEAD_DIM :]
    extra = extra_ref[...]
    experts = router_ref.shape[1]
    router_ref[...] = extra[:, :experts]
    rows = extra.shape[0]
    lane = lax.broadcasted_iota(jnp.int32, (rows, rows), 1)
    row = lax.broadcasted_iota(jnp.int32, (rows, rows), 0)
    for n, ref in enumerate((attn_ref, query_gain_ref, ffn_ref, key_gain_ref)):
        column = jnp.broadcast_to(extra[:, experts + n : experts + n + 1], (rows, rows))
        flat = jnp.sum(jnp.where(lane == row, column, 0.0), axis=0, keepdims=True)
        ref[...] = flat[:, : ref.shape[1]]


def raw_gradients(back_ref, raw_ref, pack_ref, cos_ref, sin_ref, low_ref):
    rows = back_ref.shape[1]
    width = KV_HEADS * HEAD_DIM
    is_key = lax.broadcasted_iota(jnp.int32, (rows, PAIR), 1) < HEAD_DIM
    sums = [[jnp.zeros((rows, PAIR), full) for _ in range(2)] for _ in range(2)]

    def here_of(part):
        return slice(part * PAIR, (part + 1) * PAIR)

    tables = turning(cos_ref, sin_ref)

    def unturned(g, part):
        grad = back_ref[g, :, here_of(part)].astype(full)
        cos, sin = tables[part]
        return grad * cos - partner(grad) * sin

    for g in range(KV_HEADS):
        for part in range(2):
            raw = raw_ref[g, :, here_of(part)]
            sums[part][0] += raw * raw
            sums[part][1] += raw * unturned(g, part) * pack_ref[g, :, here_of(part)]
    mean_of = [GROUP * width, width]
    inverses, shares = [], []
    for part in range(2):
        square, cross = sums[part]
        if part == 1:
            square, cross = jnp.where(is_key, square, 0.0), jnp.where(is_key, cross, 0.0)
        inverse = lax.rsqrt(jnp.sum(square, axis=-1, keepdims=True) / mean_of[part] + norm_eps)
        share = jnp.sum(cross, axis=-1, keepdims=True) * (
            inverse * inverse * inverse / mean_of[part]
        )
        if part == 1:
            inverse = jnp.where(is_key, inverse, 1.0)
            share = jnp.where(is_key, share, 0.0)
        inverses.append(inverse)
        shares.append(share)
    gains = [[], []]
    for g in range(KV_HEADS):
        for part in range(2):
            raw = raw_ref[g, :, here_of(part)]
            grad = unturned(g, part)
            gains[part].append(jnp.sum(raw * inverses[part] * grad, axis=0, keepdims=True))
            result = grad * pack_ref[g, :, here_of(part)] * inverses[part] - raw * shares[part]
            start = g * PACK + part * PAIR
            low_ref[:, start : start + PAIR] = result.astype(low_type)
    query_grad = jnp.concatenate(gains[0], axis=1)
    key_grad = jnp.concatenate(
        [
            jnp.concatenate(
                [gains[1][2 * g][:, :HEAD_DIM], gains[1][2 * g + 1][:, :HEAD_DIM]], axis=1
            )
            for g in range(KV_HEADS // 2)
        ],
        axis=1,
    )
    return query_grad, key_grad


def token_gradients(low_ref, weights_ref, tokens_ref, gains_ref, mid_grad_ref, out_ref):
    normed_grad = dot_nt(low_ref[...], weights_ref[:, : KV_HEADS * PACK])
    values = tokens_ref[...].astype(full)
    wide = values.shape[1]
    inverse = lax.rsqrt(jnp.mean(values * values, axis=-1, keepdims=True) + norm_eps)
    scaled = normed_grad * gains_ref[0:1, :]
    share = jnp.sum(scaled * values, axis=-1, keepdims=True) * (
        inverse * inverse * inverse / wide
    )
    out_ref[...] = (mid_grad_ref[...] + (scaled * inverse - values * share)).astype(low_type)
    return jnp.sum(values * inverse * normed_grad, axis=0, keepdims=True)


def put_product(ref, start, left, right_ref, at, count):
    places = ref.shape[:-1]
    for n in range(0, count, 256):
        value = dot(left, right_ref[:, at + n : at + n + 256]).astype(low_type)
        ref[..., start + n : start + n + 256] = value.reshape(places + (256,))


def on_device(
    tokens_in,
    lengths,
    routes,
    w_query,
    w_key,
    w_value,
    w_output,
    w_router,
    attn_gain,
    ffn_gain,
    query_gain,
    key_gain,
    expert_in,
    expert_down,
    out_grad,
):
    rows, wide = tokens_in.shape[1], tokens_in.shape[2]
    experts = w_router.shape[1]
    parts = expert_in.shape[0]
    owners = experts // parts
    slots = 5 * rows * routes.shape[2] // (4 * experts)
    tokens = tokens_in[0]
    grad_out = out_grad[0]

    place = lax.axis_index("dp") * rows + jnp.arange(rows)
    valid = (place < lengths[0]).astype(jnp.int32)
    ids = jnp.arange(experts)
    chosen = (
        jnp.sum((routes[0][:, :, None] == ids[None, None, :]).astype(jnp.int32), axis=1)
        * valid[:, None]
    )
    earlier = jnp.cumsum(chosen, axis=0) - chosen
    slot_of = jnp.where(chosen == 1, earlier, -1).T.astype(full)

    lane = jnp.arange(PAIR)
    frequency = rope_base ** (-2.0 * (lane % (HEAD_DIM // 2)).astype(full) / HEAD_DIM)
    angles = place.astype(full)[:, None] * frequency[None, :]
    cosine = jnp.cos(angles)
    sine = jnp.sin(angles) * jnp.where(lane % HEAD_DIM < HEAD_DIM // 2, -1.0, 1.0)

    gains = jnp.concatenate([attn_gain, query_gain, ffn_gain, key_gain])
    gains = jnp.pad(gains, (0, EXTRA - gains.shape[0]))[None]
    slot_a = slot_of.reshape(4, 4, parts, rows)
    slot_b = slot_a.transpose(1, 0, 2, 3)
    (weights, grad_held, output_proj, normed_rows, raw, held, pack_row, gain_rows, att, logs, att_home, left, right) = forward(
        lengths, (w_query, w_key, w_value, w_output, w_router), gains, slot_a, slot_b, tokens, cosine, sine, grad_out, slots, 1
    )
    weights = weights.reshape(wide, KV_HEADS * PACK + EXTRA)
    mid, made, in_grad, down_grad, router_grad, att_rows, mid_grad, mid_low, ffn_grad, att_grad = moe_layer(
        att_home, output_proj, tokens, gain_rows, left, right, grad_out, grad_held, expert_in, expert_down, weights, experts, 2
    )
    output, grad_tokens, *sums = tail(
        lengths, held, att_grad, att, logs, pack_row, gain_rows, left, right, made,
        (att_rows, mid_low, raw, cosine, sine, weights, normed_rows, tokens, mid_grad, router_grad, ffn_grad, mid), 3,
    )
    shapes = [
        (w_query.shape, full),
        (w_key.shape, full),
        (w_value.shape, full),
        (w_output.shape, full),
        (w_router.shape, full),
        ((1, attn_gain.shape[0]), full),
        ((1, ffn_gain.shape[0]), full),
        ((1, query_gain.shape[0]), full),
        ((1, key_gain.shape[0]), full),
        (in_grad.shape, full),
        (down_grad.shape, full),
        (output.shape, low_type),
        (grad_tokens.shape, low_type),
    ]
    results = pl.pallas_call(
        finish_kernel,
        out_shape=[jax.ShapeDtypeStruct(*s) for s in shapes],
        in_specs=[VMEM] * 9,
        out_specs=[VMEM] * len(shapes),
        name="finish",
        **params(2),
    )(*sums, in_grad, down_grad, output, grad_tokens)
    return (
        results[11][None],
        results[12][None],
        *results[:5],
        *[row[0] for row in results[5:9]],
        *results[9:11],
    )


def solution(mesh):
    in_specs = (
        P("expert", "dp", None),
        P("expert"),
        P("expert", "dp", None),
        P(("dp", "expert"), None),
        P(("dp", "expert"), None),
        P(("dp", "expert"), None),
        P(("dp", "expert"), None),
        P(("dp", "expert"), None),
        P(("dp", "expert")),
        P(("dp", "expert")),
        P(("dp", "expert")),
        P(("dp", "expert")),
        P("expert", None, None),
        P("expert", None, None),
        P("expert", "dp", None),
    )
    out_specs = (
        P("expert", "dp", None),
        P("expert", "dp", None),
        P(("dp", "expert"), None),
        P(("dp", "expert"), None),
        P(("dp", "expert"), None),
        P(("dp", "expert"), None),
        P(("dp", "expert"), None),
        P(("dp", "expert")),
        P(("dp", "expert")),
        P(("dp", "expert")),
        P(("dp", "expert")),
        P("expert", "dp", None),
        P("expert", "dp", None),
    )
    return jax.shard_map(
        on_device, mesh=mesh, in_specs=in_specs, out_specs=out_specs, check_vma=False
    )
```
